32 devices in a mesh: region: 8 (over z, y), sub: 4 (over x, core).
Axes of the slice: x: 2, y: 2, z: 4, core: 2. Of those that a mesh axis runs over, the one named last changes fastest.
Arguments:
- mode_rows: bfloat16 [16384, 4096], P(('region', 'sub')), may hold values from -0.09375 to 0.09375
- input_rows: bfloat16 [512, 4096], P(('region', 'sub')), may hold values from -0.25 to 0.25
- input_factor: bfloat16 [512, 128], P(('region', 'sub')), may hold values from -6 to 6
- mode_freq: float32 [4096], replicated, may hold values from 0.5 to 2
- mode_damping: float32 [4096], replicated, may hold values from 0.02 to 0.2
- line_freq: float32 [2], replicated, may hold values from 0.6 to 1.6
- boundary_rows: int32 [4096], P(('region', 'sub')), may hold values from 0 to 511
- connectivity: int32 [4, 16384], P(None, ('region', 'sub')), may hold values from 0 to 639
- stress_coef: float32 [4, 16384], P(None, ('region', 'sub')), may hold values from -3 to 3
Outputs:
- stress_psd: float32 [2, 16384], P(None, ('region', 'sub'))
The draws below stay inside these ranges and needn't reach their ends.
Inputs may be any that keep to these rules, and one draw needn't show every extreme that they name: `boundary_rows`: local row numbers of the sending device. `connectivity`: rows of the node table of the element's device.
All inputs are finite; a program needn't handle non-finite values.
Results may differ from the reference program's by a relative error of at most 0.0013.
Values may be sent and summed in bfloat16 or wider, within the bound.
No kernel may reach another device: no remote copies, remote signals or barrier semaphores. Data moves between devices by JAX's collectives and lax.ppermute only.
A program may use at most 64 MiB of HBM per device.

```python
import math
import jax
import jax.numpy as jnp
from jax import lax

M = 4096
NIN = 512
R = 32
LINES = 2
ROWS_DEV = 512
BOUND = 64
ELEM_NODES = 4
ELEM_DEV = 512
DOFS = 16384
ELEMS = 16384
EXPORTS = 4096
DEVICES = 32


def place_ends(array, key, low, top_value):
    place = [jax.random.randint(jax.random.fold_in(key, axis), (), 0, length) for axis, length in enumerate(array.shape)]
    widest = array.shape.index(max(array.shape))
    next_to = place[:widest] + [(place[widest] + 1) % array.shape[widest]] + place[widest + 1:]
    return array.at[tuple(place)].set(low).at[tuple(next_to)].set(top_value)


def block_scale(own_key, dims, pieces, smallest, largest):
    def one(position, blocks):
        draws = jax.random.uniform(jax.random.fold_in(jax.random.fold_in(own_key, 6), position), (blocks,), jnp.float32, smallest / len(pieces), largest / len(pieces))
        return jnp.repeat(jnp.exp(draws), dims[position] // blocks).reshape((-1,) + (1,) * (len(dims) - position - 1))

    level = one(*pieces[0])
    for cut in pieces[1:]:
        level = level * one(*cut)
    return level


def gaussian(own_key, extent, deviation, reach, split=(), dtype=jnp.bfloat16):
    result = deviation * jax.random.normal(own_key, extent, jnp.float32)
    if split:
        result = result * block_scale(own_key, extent, split, -0.22, 0.18)
    return jnp.clip(result, -reach, reach).astype(dtype)


def setup_inputs(seed: int = 0) -> dict:
    streams_of = jax.random.split(jax.random.key(seed), 10)
    return {
        "mode_rows": gaussian(streams_of[0], (DOFS, M), M ** -0.5, 0.09375, ((0, 32),)),
        "input_rows": gaussian(streams_of[1], (NIN, M), NIN ** -0.5, 0.25, ((0, 32),)),
        "input_factor": gaussian(streams_of[2], (NIN, LINES * 2 * R), 1.0, 6.0, ((0, 32),)),
        "mode_freq": jnp.clip(jnp.exp(jax.random.uniform(streams_of[3], (M,), jnp.float32, math.log(0.5), math.log(2.0))), 0.5, 2.0),
        "mode_damping": jnp.clip(jnp.exp(jax.random.uniform(streams_of[4], (M,), jnp.float32, math.log(0.02), math.log(0.2))), 0.02, 0.2),
        "line_freq": jnp.clip(jax.random.uniform(streams_of[5], (LINES,), jnp.float32, 0.6, 1.6), 0.6, 1.6),
        "boundary_rows": place_ends(jax.random.randint(streams_of[6], (EXPORTS,), 0, ROWS_DEV), jax.random.fold_in(streams_of[6], 1), 0, ROWS_DEV - 1).astype(jnp.int32),
        "connectivity": place_ends(jax.random.randint(streams_of[7], (ELEM_NODES, ELEMS), 0, ROWS_DEV + 2 * BOUND), jax.random.fold_in(streams_of[7], 1), 0, (ROWS_DEV + 2 * BOUND) - 1).astype(jnp.int32),
        "stress_coef": gaussian(streams_of[8], (ELEM_NODES, ELEMS), 0.5, 3.0, ((1, 32),), jnp.float32),
    }


def modal_gain(mode_freq, mode_damping, line_omega):
    detune = mode_freq * mode_freq - line_omega * line_omega
    damped = 2.0 * mode_damping * mode_freq * line_omega
    magnitude = detune * detune + damped * damped
    return detune / magnitude, -damped / magnitude


def apply_gain(summed, gain_real, gain_imag):
    half_cols = summed.shape[1] // 2
    forced_real = summed[:, :half_cols]
    forced_imag = summed[:, half_cols:]
    out_real = gain_real[:, None] * forced_real - gain_imag[:, None] * forced_imag
    out_imag = gain_real[:, None] * forced_imag + gain_imag[:, None] * forced_real
    return jnp.concatenate([out_real, out_imag], axis=1).astype(jnp.bfloat16)


def reference(mode_rows, input_rows, input_factor, mode_freq, mode_damping, line_freq, boundary_rows, connectivity, stress_coef):
    line_count = line_freq.shape[0]
    columns = input_factor.shape[1] // line_count
    pseudos = []
    for line_no in range(line_count):
        factor = input_factor[:, line_no * columns:(line_no + 1) * columns]
        summed = lax.dot_general(input_rows, factor, (((0,), (0,)), ((), ())), preferred_element_type=jnp.float32)
        gain_real, gain_imag = modal_gain(mode_freq, mode_damping, line_freq[line_no])
        pseudos.append(apply_gain(summed, gain_real, gain_imag))

    def recover(shapes_block):
        parts_list = [jnp.dot(shapes_block, pseudo, preferred_element_type=jnp.float32).astype(jnp.bfloat16) for pseudo in pseudos]
        return jnp.concatenate(parts_list, axis=1)

    responses = lax.map(recover, mode_rows.reshape(DEVICES, ROWS_DEV, M))
    width_all = responses.shape[2]
    picks = boundary_rows.reshape(DEVICES, 2 * BOUND)
    exports = jax.vmap(lambda node_rows, chosen: node_rows[chosen])(responses, picks)
    blank = jnp.zeros((1, BOUND, width_all), jnp.bfloat16)
    lower = jnp.concatenate([blank, exports[:-1, BOUND:]], axis=0)
    upper = jnp.concatenate([exports[1:, :BOUND], blank], axis=0)
    node_table = jnp.concatenate([lower, responses, upper], axis=1)
    links = connectivity.reshape(ELEM_NODES, DEVICES, ELEM_DEV).transpose(1, 0, 2)
    weights = stress_coef.reshape(ELEM_NODES, DEVICES, ELEM_DEV).transpose(1, 0, 2)
    gathered = jax.vmap(lambda node_rows, chosen: node_rows[chosen])(node_table, links)
    stress = jnp.sum(weights[:, :, :, None] * gathered.astype(jnp.float32), axis=1)
    squares = (stress * stress).reshape(DEVICES, ELEM_DEV, line_count, columns)
    power = jnp.mean(squares, axis=3)
    return power.transpose(2, 0, 1).reshape(line_count, DEVICES * ELEM_DEV)
```

```python
import functools

import jax
import jax.numpy as jnp
from jax import lax
from jax.experimental import pallas as pl
from jax.experimental.pallas import tpu as pltpu
from jax.sharding import PartitionSpec as P

AXES = ("region", "sub")
LANES = 128
F32 = jnp.float32
BF16 = jnp.bfloat16
VMEM_BYTES = 24 * 1024 * 1024


def whole(*_):
    return pl.BlockSpec(memory_space=pltpu.VMEM)


def modal_gain(freq, damping, omega):
    detune = freq * freq - omega * omega
    damped = 2.0 * damping * freq * omega
    magnitude = detune * detune + damped * damped
    return detune / magnitude, -damped / magnitude


def setup_kernel(boundary_ref, connect_ref, coef_ref, modes_ref, export_ref, high_ref, low_ref):
    rows = modes_ref.shape[0]
    exports = boundary_ref.shape[0]
    pick = lax.broadcasted_iota(jnp.int32, (exports, rows), 1) == boundary_ref[...]
    pick = pick.astype(F32).astype(BF16)
    step = 1024
    for start in range(0, modes_ref.shape[1], step):
        block = modes_ref[:, start : start + step]
        export_ref[:, start : start + step] = jnp.dot(
            pick, block, preferred_element_type=F32
        ).astype(BF16)
    nodes, elems = high_ref.shape
    tall = 64
    for start in range(0, nodes, tall):
        node = lax.broadcasted_iota(jnp.int32, (tall, elems), 0) + start
        total = jnp.zeros((tall, elems), F32)
        for corner in range(connect_ref.shape[0]):
            hit = node == connect_ref[corner : corner + 1, :]
            total = total + jnp.where(hit, coef_ref[corner : corner + 1, :], 0.0)
        high = total.astype(BF16)
        high_ref[start : start + tall, :] = high
        low_ref[start : start + tall, :] = (total - high.astype(F32)).astype(BF16)


def scale_transposed(forced, freq, damping, line_ref, columns):
    half = columns // 2
    pieces = []
    for line in range(line_ref.shape[0]):
        gain_real, gain_imag = modal_gain(freq, damping, line_ref[line])
        real = forced[line * columns : line * columns + half]
        imag = forced[line * columns + half : (line + 1) * columns]
        pieces.append(gain_real * real - gain_imag * imag)
        pieces.append(gain_real * imag + gain_imag * real)
    return jnp.concatenate(pieces, axis=0)


def pseudo_kernel(line_ref, freq_ref, damping_ref, got_ref, pseudo_ref, *, rows):
    devices, _, width = got_ref.shape
    me = lax.axis_index(AXES)
    shapes = got_ref[:, :rows, :].reshape(devices * rows, width)
    factor = got_ref[:, rows:, :].reshape(devices * rows, width)
    forced = lax.dot_general(
        factor, shapes, (((0,), (0,)), ((), ())), preferred_element_type=F32
    )
    columns = width // line_ref.shape[0]
    scaled = scale_transposed(
        forced, freq_ref[pl.ds(me, 1), :], damping_ref[pl.ds(me, 1), :], line_ref, columns
    )
    pseudo_ref[...] = scaled.T.astype(BF16)


def stress_kernel(own_ref, lower_ref, upper_ref, pseudo_ref, high_ref, low_ref, power_ref, total, *, lines):
    step = pl.program_id(0)

    @pl.when(step == 0)
    def _():
        total[...] = jnp.zeros_like(total)

    rim = lower_ref.shape[0]
    rows = own_ref.shape[0]
    block = pseudo_ref[...]
    total[:rim] += jnp.dot(lower_ref[...], block, preferred_element_type=F32)
    total[rim : rim + rows] += jnp.dot(own_ref[...], block, preferred_element_type=F32)
    total[rim + rows :] += jnp.dot(upper_ref[...], block, preferred_element_type=F32)

    @pl.when(step == pl.num_programs(0) - 1)
    def _():
        table = total[...].T.astype(BF16)
        stress = jnp.dot(table, high_ref[...], preferred_element_type=F32)
        stress = stress + jnp.dot(table, low_ref[...], preferred_element_type=F32)
        squares = stress * stress
        columns = squares.shape[0] // lines
        for line in range(lines):
            power_ref[line : line + 1, :] = (
                jnp.sum(squares[line * columns : (line + 1) * columns], axis=0, keepdims=True)
                / columns
            )


def setup(boundary_rows, connectivity, stress_coef, mode_rows):
    exports = boundary_rows.shape[0]
    rows, modes = mode_rows.shape
    elems = connectivity.shape[1]
    nodes = rows + exports
    return pl.pallas_call(
        setup_kernel,
        out_shape=[
            jax.ShapeDtypeStruct((exports, modes), BF16),
            jax.ShapeDtypeStruct((nodes, elems), BF16),
            jax.ShapeDtypeStruct((nodes, elems), BF16),
        ],
        in_specs=[whole()] * 4,
        out_specs=[whole()] * 3,
        compiler_params=pltpu.CompilerParams(vmem_limit_bytes=VMEM_BYTES),
        cost_estimate=pl.CostEstimate(
            flops=2 * exports * rows * modes + 8 * nodes * elems,
            bytes_accessed=2 * (rows + exports) * modes + 4 * nodes * elems,
            transcendentals=0,
        ),
        name="setup",
    )(boundary_rows.reshape(exports, 1), connectivity, stress_coef, mode_rows)


def pseudo_part(got, line_freq, mode_freq, mode_damping, rows):
    devices, _, width = got.shape
    modes = mode_freq.shape[0] // devices
    return pl.pallas_call(
        functools.partial(pseudo_kernel, rows=rows),
        out_shape=jax.ShapeDtypeStruct((modes, width), BF16),
        in_specs=[pl.BlockSpec(memory_space=pltpu.SMEM), whole(), whole(), whole()],
        out_specs=whole(),
        compiler_params=pltpu.CompilerParams(vmem_limit_bytes=VMEM_BYTES),
        cost_estimate=pl.CostEstimate(
            flops=2 * devices * rows * modes * width,
            bytes_accessed=2 * got.size,
            transcendentals=0,
        ),
        name="pseudo",
    )(line_freq, mode_freq.reshape(devices, modes), mode_damping.reshape(devices, modes), got)


def stress_part(mode_rows, lower, upper, pseudo, high, low, lines):
    rows, modes = mode_rows.shape
    rim = lower.shape[0]
    nodes, elems = high.shape
    width = pseudo.shape[1]
    step = 1024
    return pl.pallas_call(
        functools.partial(stress_kernel, lines=lines),
        out_shape=jax.ShapeDtypeStruct((lines, elems), F32),
        grid=(modes // step,),
        in_specs=[
            pl.BlockSpec((rows, step), lambda i: (0, i)),
            pl.BlockSpec((rim, step), lambda i: (0, i)),
            pl.BlockSpec((rim, step), lambda i: (0, i)),
            pl.BlockSpec((step, width), lambda i: (i, 0)),
            whole(),
            whole(),
        ],
        out_specs=whole(),
        scratch_shapes=[pltpu.VMEM((nodes, width), F32)],
        compiler_params=pltpu.CompilerParams(vmem_limit_bytes=VMEM_BYTES),
        cost_estimate=pl.CostEstimate(
            flops=2 * nodes * modes * width + 4 * nodes * elems * width,
            bytes_accessed=2 * (nodes + width) * modes + 4 * nodes * elems,
            transcendentals=0,
        ),
        name="stress",
    )(mode_rows, lower, upper, pseudo, high, low)


def pseudo_by_sum(input_rows, input_factor, mode_freq, mode_damping, line_freq):
    lines = line_freq.shape[0]
    columns = input_factor.shape[1] // lines
    half = columns // 2
    forced = lax.psum(
        lax.dot_general(
            input_rows, input_factor, (((0,), (0,)), ((), ())), preferred_element_type=F32
        ),
        AXES,
    )
    pieces = []
    for line in range(lines):
        gain_real, gain_imag = modal_gain(mode_freq, mode_damping, line_freq[line])
        gain_real, gain_imag = gain_real[:, None], gain_imag[:, None]
        real = forced[:, line * columns : line * columns + half]
        imag = forced[:, line * columns + half : (line + 1) * columns]
        pieces.append(gain_real * real - gain_imag * imag)
        pieces.append(gain_real * imag + gain_imag * real)
    return jnp.concatenate(pieces, axis=1).astype(BF16)


def pseudo_by_exchange(devices, input_rows, input_factor, mode_freq, mode_damping, line_freq):
    rows, modes = input_rows.shape
    width = input_factor.shape[1]
    blocks = input_rows.reshape(rows, devices, modes // devices).transpose(1, 0, 2)
    factors = jnp.broadcast_to(input_factor[None], (devices, rows, width))
    got = lax.all_to_all(jnp.concatenate([blocks, factors], axis=1), AXES, 0, 0)
    part = pseudo_part(got, line_freq, mode_freq, mode_damping, rows)
    return lax.all_gather(part, AXES, axis=0, tiled=True)


def local(
    devices,
    mode_rows,
    input_rows,
    input_factor,
    mode_freq,
    mode_damping,
    line_freq,
    boundary_rows,
    connectivity,
    stress_coef,
):
    rows, modes = input_rows.shape
    rim = boundary_rows.shape[0] // 2
    exports, high, low = setup(boundary_rows, connectivity, stress_coef, mode_rows)
    up = [(i, i + 1) for i in range(devices - 1)]
    down = [(i + 1, i) for i in range(devices - 1)]
    lower = lax.ppermute(exports[rim:], AXES, up)
    upper = lax.ppermute(exports[:rim], AXES, down)
    if modes == devices * LANES and input_factor.shape[1] == LANES and rows % 16 == 0:
        pseudo = pseudo_by_exchange(
            devices, input_rows, input_factor, mode_freq, mode_damping, line_freq
        )
    else:
        pseudo = pseudo_by_sum(input_rows, input_factor, mode_freq, mode_damping, line_freq)
    return stress_part(mode_rows, lower, upper, pseudo, high, low, line_freq.shape[0])


def solution(mesh):
    devices = 1
    for axis in AXES:
        devices *= mesh.shape[axis]
    placed = (
        P(AXES, None),
        P(AXES, None),
        P(AXES, None),
        P(),
        P(),
        P(),
        P(AXES),
        P(None, AXES),
        P(None, AXES),
    )
    return jax.shard_map(
        functools.partial(local, devices),
        mesh=mesh,
        in_specs=placed,
        out_specs=P(None, AXES),
        check_vma=False,
    )
```

```python
import functools
import math

import jax
import jax.numpy as jnp
from jax import lax
from jax.experimental import pallas as pl
from jax.experimental.pallas import tpu as pltpu
from jax.sharding import PartitionSpec as P

AXES = ("region", "sub")
LANES = 128
F32 = jnp.float32
BF16 = jnp.bfloat16
VMEM_BYTES = 24 * 1024 * 1024
FAST_SHAPE = (8, 4)


def whole(*_):
    return pl.BlockSpec(memory_space=pltpu.VMEM)


def modal_gain(freq, damping, omega):
    detune = freq * freq - omega * omega
    damped = 2.0 * damping * freq * omega
    magnitude = detune * detune + damped * damped
    return detune / magnitude, -damped / magnitude


def setup_kernel(connect_ref, coef_ref, high_ref, low_ref):
    nodes, elems = high_ref.shape
    tall = 64
    for start in range(0, nodes, tall):
        node = lax.broadcasted_iota(jnp.int32, (tall, elems), 0) + start
        total = jnp.zeros((tall, elems), F32)
        for corner in range(connect_ref.shape[0]):
            hit = node == connect_ref[corner : corner + 1, :]
            total = total + jnp.where(hit, coef_ref[corner : corner + 1, :], 0.0)
        high = total.astype(BF16)
        high_ref[start : start + tall, :] = high
        low_ref[start : start + tall, :] = (total - high.astype(F32)).astype(BF16)


def scale_transposed(forced, freq, damping, line_ref, columns):
    half = columns // 2
    pieces = []
    for line in range(line_ref.shape[0]):
        gain_real, gain_imag = modal_gain(freq, damping, line_ref[line])
        real = forced[line * columns : line * columns + half]
        imag = forced[line * columns + half : (line + 1) * columns]
        pieces.append(gain_real * real - gain_imag * imag)
        pieces.append(gain_real * imag + gain_imag * real)
    return jnp.concatenate(pieces, axis=0)


def slab_of(device):
    core = device % 2
    plane = (device // 2) % 4
    return core * 16 + plane * 4 + device // 8


def pseudo_kernel(line_ref, freq_ref, damping_ref, got_ref, pseudo_ref, *, rows):
    devices, _, width = got_ref.shape
    slab = slab_of(lax.axis_index(AXES))
    shapes = got_ref[:, :rows, :].reshape(devices * rows, width)
    factor = got_ref[:, rows:, :].reshape(devices * rows, width)
    forced = lax.dot_general(
        factor, shapes, (((0,), (0,)), ((), ())), preferred_element_type=F32
    )
    columns = width // line_ref.shape[0]
    scaled = scale_transposed(
        forced, freq_ref[pl.ds(slab, 1), :], damping_ref[pl.ds(slab, 1), :], line_ref, columns
    )
    pseudo_ref[...] = scaled.T.astype(BF16)


def first_kernel(modes_ref, pseudo_ref, total_ref):
    depth = pseudo_ref.shape[0]
    core = lax.axis_index(AXES) % 2
    here = pl.ds(pl.multiple_of(core * depth, depth), depth)
    total_ref[...] = jnp.dot(modes_ref[:, here], pseudo_ref[...], preferred_element_type=F32)


def second_kernel(boundary_ref, modes_ref, pseudo_ref, total_ref, table_ref, export_ref):
    rows = modes_ref.shape[0]
    depth = pseudo_ref.shape[0]
    exports = export_ref.shape[0]
    other = 1 - lax.axis_index(AXES) % 2
    here = pl.ds(pl.multiple_of(other * depth, depth), depth)
    total = total_ref[...] + jnp.dot(
        modes_ref[:, here], pseudo_ref[...], preferred_element_type=F32
    )
    responses = total.astype(BF16)
    pick = lax.broadcasted_iota(jnp.int32, (exports, rows), 1) == boundary_ref[...]
    pick = pick.astype(F32).astype(BF16)
    export_ref[...] = jnp.dot(pick, responses, preferred_element_type=F32).astype(BF16)
    table_ref[...] = total.T.astype(BF16)


def own_kernel(table_ref, high_ref, low_ref, stress_ref, *, rim):
    rows = table_ref.shape[1]
    table = table_ref[...]
    stress = jnp.dot(table, high_ref[rim : rim + rows, :], preferred_element_type=F32)
    stress_ref[...] = stress + jnp.dot(
        table, low_ref[rim : rim + rows, :], preferred_element_type=F32
    )


def power_kernel(stress_ref, lower_ref, upper_ref, high_ref, low_ref, power_ref):
    rim = lower_ref.shape[0]
    nodes = high_ref.shape[0]
    lines = power_ref.shape[0]
    stress = stress_ref[...]
    for rows_ref, start in ((lower_ref, 0), (upper_ref, nodes - rim)):
        for part in (high_ref, low_ref):
            stress = stress + lax.dot_general(
                rows_ref[...],
                part[start : start + rim, :],
                (((0,), (0,)), ((), ())),
                preferred_element_type=F32,
            )
    squares = stress * stress
    columns = squares.shape[0] // lines
    for line in range(lines):
        power_ref[line : line + 1, :] = (
            jnp.sum(squares[line * columns : (line + 1) * columns], axis=0, keepdims=True)
            / columns
        )


def call(kernel, name, out, *operands, flops, smem=0):
    shapes = [jax.ShapeDtypeStruct(shape, dtype) for shape, dtype in out]
    moved = sum(x.size * x.dtype.itemsize for x in operands)
    moved += sum(math.prod(shape) * jnp.dtype(dtype).itemsize for shape, dtype in out)
    specs = [pl.BlockSpec(memory_space=pltpu.SMEM)] * smem + [whole()] * (len(operands) - smem)
    result = pl.pallas_call(
        kernel,
        out_shape=shapes,
        in_specs=specs,
        out_specs=[whole()] * len(out),
        compiler_params=pltpu.CompilerParams(vmem_limit_bytes=VMEM_BYTES),
        cost_estimate=pl.CostEstimate(flops=flops, bytes_accessed=moved, transcendentals=0),
        name=name,
    )(*operands)
    return result if len(out) > 1 else result[0]


def pseudo_by_sum(input_rows, input_factor, mode_freq, mode_damping, line_freq):
    lines = line_freq.shape[0]
    columns = input_factor.shape[1] // lines
    half = columns // 2
    forced = lax.psum(
        lax.dot_general(
            input_rows, input_factor, (((0,), (0,)), ((), ())), preferred_element_type=F32
        ),
        AXES,
    )
    pieces = []
    for line in range(lines):
        gain_real, gain_imag = modal_gain(mode_freq, mode_damping, line_freq[line])
        gain_real, gain_imag = gain_real[:, None], gain_imag[:, None]
        real = forced[:, line * columns : line * columns + half]
        imag = forced[:, line * columns + half : (line + 1) * columns]
        pieces.append(gain_real * real - gain_imag * imag)
        pieces.append(gain_real * imag + gain_imag * real)
    return jnp.concatenate(pieces, axis=1).astype(BF16)


def gather_by(block, groups):
    count = len(groups[0])
    sent = jnp.broadcast_to(block[None], (count,) + block.shape)
    got = lax.all_to_all(sent, AXES, 0, 0, axis_index_groups=groups)
    return got.reshape((count * block.shape[0],) + block.shape[1:])


def own_pseudo(input_rows, input_factor, mode_freq, mode_damping, line_freq):
    devices = math.prod(FAST_SHAPE)
    rows, modes = input_rows.shape
    width = input_factor.shape[1]
    slab = modes // devices
    blocks = input_rows.reshape(rows, 2, 4, 4, slab).transpose(3, 2, 1, 0, 4)
    blocks = blocks.reshape(devices, rows, slab)
    factors = jnp.broadcast_to(input_factor[None], (devices, rows, width))
    got = lax.all_to_all(jnp.concatenate([blocks, factors], axis=1), AXES, 0, 0)
    return call(
        functools.partial(pseudo_kernel, rows=rows),
        "pseudo",
        [((slab, width), BF16)],
        line_freq,
        mode_freq.reshape(devices, slab),
        mode_damping.reshape(devices, slab),
        got,
        flops=2 * devices * rows * slab * width,
        smem=1,
    )


def local(
    shape,
    mode_rows,
    input_rows,
    input_factor,
    mode_freq,
    mode_damping,
    line_freq,
    boundary_rows,
    connectivity,
    stress_coef,
):
    devices = math.prod(shape)
    rows, modes = mode_rows.shape
    width = input_factor.shape[1]
    lines = line_freq.shape[0]
    exports = boundary_rows.shape[0]
    rim = exports // 2
    elems = connectivity.shape[1]
    nodes = rows + exports
    high, low = call(
        setup_kernel,
        "setup",
        [((nodes, elems), BF16)] * 2,
        connectivity,
        stress_coef,
        flops=16 * nodes * elems,
    )
    inputs = (input_rows, input_factor, mode_freq, mode_damping, line_freq)
    if shape == FAST_SHAPE and modes == devices * LANES and input_rows.shape[0] % 16 == 0:
        block = own_pseudo(*inputs)
        columns = [[z * 8 + plane for z in range(4)] for plane in range(8)]
        planes = [[z * 8 + p * 2 + c for p in range(4)] for z in range(4) for c in range(2)]
        mine = gather_by(gather_by(block, columns), planes)
        theirs = lax.ppermute(mine, AXES, [(i, i ^ 1) for i in range(devices)])
    else:
        pseudo = pseudo_by_sum(*inputs).reshape(2, modes // 2, width)
        core = lax.axis_index(AXES) % 2
        mine = lax.dynamic_index_in_dim(pseudo, core, 0, keepdims=False)
        theirs = lax.dynamic_index_in_dim(pseudo, 1 - core, 0, keepdims=False)
    total = call(
        first_kernel,
        "first",
        [((rows, width), F32)],
        mode_rows,
        mine,
        flops=rows * modes * width,
    )
    table, export = call(
        second_kernel,
        "second",
        [((width, rows), BF16), ((exports, width), BF16)],
        boundary_rows.reshape(exports, 1),
        mode_rows,
        theirs,
        total,
        flops=rows * modes * width + 2 * exports * rows * width,
    )
    lower = lax.ppermute(export[rim:], AXES, [(i, i + 1) for i in range(devices - 1)])
    upper = lax.ppermute(export[:rim], AXES, [(i + 1, i) for i in range(devices - 1)])
    stress = call(
        functools.partial(own_kernel, rim=rim),
        "own",
        [((width, elems), F32)],
        table,
        high,
        low,
        flops=4 * rows * elems * width,
    )
    return call(
        power_kernel,
        "power",
        [((lines, elems), F32)],
        stress,
        lower,
        upper,
        high,
        low,
        flops=4 * exports * elems * width,
    )


def solution(mesh):
    shape = tuple(mesh.shape[axis] for axis in AXES)
    placed = (
        P(AXES, None),
        P(AXES, None),
        P(AXES, None),
        P(),
        P(),
        P(),
        P(AXES),
        P(None, AXES),
        P(None, AXES),
    )
    return jax.shard_map(
        functools.partial(local, shape),
        mesh=mesh,
        in_specs=placed,
        out_specs=P(None, AXES),
        check_vma=False,
    )
```

```python
import functools
import math

import jax
import jax.numpy as jnp
from jax import lax
from jax.experimental import pallas as pl
from jax.experimental.pallas import tpu as pltpu
from jax.sharding import PartitionSpec as P

AXES = ("region", "sub")
LANES = 128
F32 = jnp.float32
BF16 = jnp.bfloat16
VMEM_BYTES = 24 * 1024 * 1024
VMEM_MOST = 50 * 1024 * 1024
VMEM_ALL = 60 * 1024 * 1024
FAST_SHAPE = (8, 4)


def whole(*_):
    return pl.BlockSpec(memory_space=pltpu.VMEM)


def remains():
    return pl.BlockSpec(memory_space=pltpu.HBM)


def modal_gain(freq, damping, omega):
    detune = freq * freq - omega * omega
    damped = 2.0 * damping * freq * omega
    magnitude = detune * detune + damped * damped
    return detune / magnitude, -damped / magnitude


def setup_kernel(connect_ref, coef_ref, high_ref, low_ref):
    nodes, elems = high_ref.shape
    tall = 64
    for start in range(0, nodes, tall):
        node = lax.broadcasted_iota(jnp.int32, (tall, elems), 0) + start
        total = jnp.zeros((tall, elems), F32)
        for corner in range(connect_ref.shape[0]):
            hit = node == connect_ref[corner : corner + 1, :]
            total = total + jnp.where(hit, coef_ref[corner : corner + 1, :], 0.0)
        high = total.astype(BF16)
        high_ref[start : start + tall, :] = high
        low_ref[start : start + tall, :] = (total - high.astype(F32)).astype(BF16)


def slab_of(device):
    core = device % 2
    plane = (device // 2) % 4
    return core * 16 + plane * 4 + device // 8


def pack_kernel(
    line_hbm, freq_hbm, damping_hbm, rows_hbm, factor_hbm, sent_ref, gain_ref,
    line_ref, freq_ref, damping_ref, rows_ref, factor_ref, sems,
):
    devices, _, width = sent_ref.shape
    rows = rows_ref.shape[0]
    pairs = (
        (rows_hbm, rows_ref),
        (factor_hbm, factor_ref),
        (line_hbm, line_ref),
        (freq_hbm, freq_ref),
        (damping_hbm, damping_ref),
    )
    copies = [pltpu.make_async_copy(a, b, sems.at[k]) for k, (a, b) in enumerate(pairs)]
    for copy in copies:
        copy.start()
    copies[0].wait()
    copies[1].wait()
    factor = factor_ref[...]
    for device in range(devices):
        slab = slab_of(device)
        sent_ref[device, :rows, :] = rows_ref[:, slab * width : (slab + 1) * width]
        sent_ref[device, rows:, :] = factor
    for copy in copies[2:]:
        copy.wait()
    slab = pl.ds(slab_of(lax.axis_index(AXES)), 1)
    for line in range(line_ref.shape[0]):
        real, imag = modal_gain(freq_ref[slab, :], damping_ref[slab, :], line_ref[line])
        gain_ref[2 * line : 2 * line + 1, :] = real
        gain_ref[2 * line + 1 : 2 * line + 2, :] = imag


def pseudo_kernel(gain_ref, got_ref, pseudo_ref, *, rows, lines):
    devices, _, width = got_ref.shape
    shapes = got_ref[:, :rows, :].reshape(devices * rows, width)
    factor = got_ref[:, rows:, :].reshape(devices * rows, width)
    forced = lax.dot_general(
        factor, shapes, (((0,), (0,)), ((), ())), preferred_element_type=F32
    )
    columns = width // lines
    half = columns // 2
    pieces = []
    for line in range(lines):
        gain_real = gain_ref[2 * line : 2 * line + 1, :]
        gain_imag = gain_ref[2 * line + 1 : 2 * line + 2, :]
        real = forced[line * columns : line * columns + half]
        imag = forced[line * columns + half : (line + 1) * columns]
        pieces.append(gain_real * real - gain_imag * imag)
        pieces.append(gain_real * imag + gain_imag * real)
    pseudo = jnp.concatenate(pieces, axis=0).T.astype(BF16)
    for copy in range(pseudo_ref.shape[0]):
        pseudo_ref[copy] = pseudo


def first_kernel(
    boundary_hbm, modes_hbm, pseudo_ref, total_ref, other_ref, pick_ref, boundary_ref, near_ref, sems
):
    depth = pseudo_ref.shape[0]
    parts = sems.shape[0] - 2
    step = depth // parts
    core = lax.axis_index(AXES) % 2
    copies = [
        pltpu.make_async_copy(
            modes_hbm.at[:, pl.ds(pl.multiple_of(core * depth + k * step, step), step)],
            near_ref.at[:, k * step : (k + 1) * step],
            sems.at[k],
        )
        for k in range(parts)
    ]
    copies.append(pltpu.make_async_copy(boundary_hbm, boundary_ref, sems.at[parts]))
    copies.append(
        pltpu.make_async_copy(
            modes_hbm.at[:, pl.ds(pl.multiple_of((1 - core) * depth, depth), depth)],
            other_ref,
            sems.at[parts + 1],
        )
    )
    for copy in copies:
        copy.start()
    total = None
    for k in range(parts):
        copies[k].wait()
        here = slice(k * step, (k + 1) * step)
        term = jnp.dot(near_ref[:, here], pseudo_ref[here, :], preferred_element_type=F32)
        total = term if total is None else total + term
    total_ref[...] = total
    copies[parts].wait()
    pick = lax.broadcasted_iota(jnp.int32, pick_ref.shape, 0) == boundary_ref[...]
    pick_ref[...] = pick.astype(F32).astype(BF16)
    copies[parts + 1].wait()


def second_kernel(pick_ref, modes_ref, pseudo_ref, total_ref, table_ref, far_ref, near_ref):
    total = total_ref[...] + jnp.dot(
        modes_ref[...], pseudo_ref[...], preferred_element_type=F32
    )
    export = lax.dot_general(
        pick_ref[...], total.astype(BF16), (((0,), (0,)), ((), ())), preferred_element_type=F32
    ).astype(BF16)
    odd = lax.axis_index(AXES) % 2 == 1
    rim = far_ref.shape[0]
    far_ref[...] = jnp.where(odd, export[rim:], export[:rim])
    near_ref[...] = jnp.where(odd, export[:rim], export[rim:])
    table_ref[...] = total.T.astype(BF16)


def own_kernel(table_ref, high_ref, low_ref, stress_ref, *, rim):
    rows = table_ref.shape[1]
    table = table_ref[...]
    stress = jnp.dot(table, high_ref[rim : rim + rows, :], preferred_element_type=F32)
    stress_ref[...] = stress + jnp.dot(
        table, low_ref[rim : rim + rows, :], preferred_element_type=F32
    )


def power_kernel(stress_ref, far_ref, near_ref, high_ref, low_ref, power_ref):
    rim = far_ref.shape[0]
    nodes = high_ref.shape[0]
    lines = power_ref.shape[0]
    odd = lax.axis_index(AXES) % 2
    after = nodes - rim
    stress = stress_ref[...]
    for rows_ref, start in ((near_ref, after * (1 - odd)), (far_ref, after * odd)):
        here = pl.ds(pl.multiple_of(start, rim), rim)
        for part in (high_ref, low_ref):
            stress = stress + lax.dot_general(
                rows_ref[...],
                part[here, :],
                (((0,), (0,)), ((), ())),
                preferred_element_type=F32,
            )
    squares = stress * stress
    columns = squares.shape[0] // lines
    for line in range(lines):
        power_ref[line : line + 1, :] = (
            jnp.sum(squares[line * columns : (line + 1) * columns], axis=0, keepdims=True)
            / columns
        )


def call(kernel, name, out, *operands, flops, hbm=0, scratch=(), vmem=VMEM_BYTES):
    shapes = [jax.ShapeDtypeStruct(shape, dtype) for shape, dtype in out]
    moved = sum(x.size * x.dtype.itemsize for x in operands)
    moved += sum(math.prod(shape) * jnp.dtype(dtype).itemsize for shape, dtype in out)
    result = pl.pallas_call(
        kernel,
        out_shape=shapes,
        in_specs=[remains()] * hbm + [whole()] * (len(operands) - hbm),
        out_specs=[whole()] * len(out),
        scratch_shapes=scratch,
        compiler_params=pltpu.CompilerParams(vmem_limit_bytes=vmem),
        cost_estimate=pl.CostEstimate(flops=flops, bytes_accessed=moved, transcendentals=0),
        name=name,
    )(*operands)
    return result if len(out) > 1 else result[0]


def pseudo_by_sum(input_rows, input_factor, mode_freq, mode_damping, line_freq):
    lines = line_freq.shape[0]
    columns = input_factor.shape[1] // lines
    half = columns // 2
    forced = lax.psum(
        lax.dot_general(
            input_rows, input_factor, (((0,), (0,)), ((), ())), preferred_element_type=F32
        ),
        AXES,
    )
    pieces = []
    for line in range(lines):
        gain_real, gain_imag = modal_gain(mode_freq, mode_damping, line_freq[line])
        gain_real, gain_imag = gain_real[:, None], gain_imag[:, None]
        real = forced[:, line * columns : line * columns + half]
        imag = forced[:, line * columns + half : (line + 1) * columns]
        pieces.append(gain_real * real - gain_imag * imag)
        pieces.append(gain_real * imag + gain_imag * real)
    return jnp.concatenate(pieces, axis=1).astype(BF16)


def exchange(sent, groups):
    got = lax.all_to_all(sent, AXES, 0, 0, axis_index_groups=groups)
    return got.reshape((-1,) + got.shape[2:])


def own_pseudo(input_rows, input_factor, mode_freq, mode_damping, line_freq, copies):
    devices = math.prod(FAST_SHAPE)
    rows, modes = input_rows.shape
    width = input_factor.shape[1]
    slab = modes // devices
    lines = line_freq.shape[0]
    sent, gains = call(
        pack_kernel,
        "pack",
        [((devices, 2 * rows, width), BF16), ((2 * lines, slab), F32)],
        line_freq,
        mode_freq.reshape(devices, slab),
        mode_damping.reshape(devices, slab),
        input_rows,
        input_factor,
        flops=0,
        hbm=5,
        vmem=VMEM_ALL,
        scratch=[
            pltpu.SMEM((lines,), F32),
            pltpu.VMEM((devices, slab), F32),
            pltpu.VMEM((devices, slab), F32),
            pltpu.VMEM((rows, modes), BF16),
            pltpu.VMEM((rows, width), BF16),
            pltpu.SemaphoreType.DMA((5,)),
        ],
    )
    got = lax.all_to_all(sent, AXES, 0, 0)
    return call(
        functools.partial(pseudo_kernel, rows=rows, lines=lines),
        "pseudo",
        [((copies, slab, width), BF16)],
        gains,
        got,
        flops=2 * devices * rows * slab * width,
    )


def local(
    shape,
    mode_rows,
    input_rows,
    input_factor,
    mode_freq,
    mode_damping,
    line_freq,
    boundary_rows,
    connectivity,
    stress_coef,
):
    devices = math.prod(shape)
    rows, modes = mode_rows.shape
    width = input_factor.shape[1]
    lines = line_freq.shape[0]
    exports = boundary_rows.shape[0]
    rim = exports // 2
    elems = connectivity.shape[1]
    nodes = rows + exports
    high, low = call(
        setup_kernel,
        "setup",
        [((nodes, elems), BF16)] * 2,
        connectivity,
        stress_coef,
        flops=16 * nodes * elems,
    )
    inputs = (input_rows, input_factor, mode_freq, mode_damping, line_freq)
    if shape == FAST_SHAPE and modes == devices * LANES and input_rows.shape[0] % 16 == 0:
        columns = [[z * 8 + plane for z in range(4)] for plane in range(8)]
        planes = [[z * 8 + p * 2 + c for p in range(4)] for z in range(4) for c in range(2)]
        block = exchange(own_pseudo(*inputs, copies=4), columns)
        mine = exchange(jnp.broadcast_to(block[None], (4,) + block.shape), planes)
        theirs = lax.ppermute(mine, AXES, [(i, i ^ 1) for i in range(devices)])
    else:
        pseudo = pseudo_by_sum(*inputs).reshape(2, modes // 2, width)
        core = lax.axis_index(AXES) % 2
        mine = lax.dynamic_index_in_dim(pseudo, core, 0, keepdims=False)
        theirs = lax.dynamic_index_in_dim(pseudo, 1 - core, 0, keepdims=False)
    total, others, pick = call(
        first_kernel,
        "first",
        [((rows, width), F32), ((rows, modes // 2), BF16), ((rows, exports), BF16)],
        boundary_rows.reshape(1, exports),
        mode_rows,
        mine,
        flops=rows * modes * width,
        hbm=2,
        vmem=VMEM_MOST,
        scratch=[
            pltpu.VMEM((1, exports), jnp.int32),
            pltpu.VMEM((rows, modes // 2), BF16),
            pltpu.SemaphoreType.DMA((6,)),
        ],
    )
    table, far, near = call(
        second_kernel,
        "second",
        [((width, rows), BF16), ((rim, width), BF16), ((rim, width), BF16)],
        pick,
        others,
        theirs,
        total,
        flops=rows * modes * width + 2 * exports * rows * width,
    )
    inner = [(i, i ^ 1) for i in range(devices)]
    outer = [(i, i + 1) for i in range(1, devices - 1, 2)]
    outer += [(j, i) for i, j in outer]
    near = lax.ppermute(near, AXES, inner)
    far = lax.ppermute(far, AXES, outer)
    stress = call(
        functools.partial(own_kernel, rim=rim),
        "own",
        [((width, elems), F32)],
        table,
        high,
        low,
        flops=4 * rows * elems * width,
    )
    return call(
        power_kernel,
        "power",
        [((lines, elems), F32)],
        stress,
        far,
        near,
        high,
        low,
        flops=4 * exports * elems * width,
    )


def solution(mesh):
    shape = tuple(mesh.shape[axis] for axis in AXES)
    placed = (
        P(AXES, None),
        P(AXES, None),
        P(AXES, None),
        P(),
        P(),
        P(),
        P(AXES),
        P(None, AXES),
        P(None, AXES),
    )
    return jax.shard_map(
        functools.partial(local, shape),
        mesh=mesh,
        in_specs=placed,
        out_specs=P(None, AXES),
        check_vma=False,
    )
```

```python
import functools
import math

import jax
import jax.numpy as jnp
from jax import lax
from jax.experimental import pallas as pl
from jax.experimental.pallas import tpu as pltpu
from jax.sharding import PartitionSpec as P

AXES = ("region", "sub")
LANES = 128
F32 = jnp.float32
BF16 = jnp.bfloat16
VMEM_BYTES = 24 * 1024 * 1024
VMEM_ALL = 60 * 1024 * 1024
FAST_SHAPE = (8, 4)


def whole(*_):
    return pl.BlockSpec(memory_space=pltpu.VMEM)


def remains():
    return pl.BlockSpec(memory_space=pltpu.HBM)


def modal_gain(freq, damping, omega):
    detune = freq * freq - omega * omega
    damped = 2.0 * damping * freq * omega
    magnitude = detune * detune + damped * damped
    return detune / magnitude, -damped / magnitude


def setup_kernel(boundary_ref, connect_ref, coef_ref, pick_ref, high_ref, low_ref):
    pick = lax.broadcasted_iota(jnp.int32, pick_ref.shape, 0) == boundary_ref[...]
    pick_ref[...] = pick.astype(F32).astype(BF16)
    nodes, elems = high_ref.shape
    tall = 64
    for start in range(0, nodes, tall):
        node = lax.broadcasted_iota(jnp.int32, (tall, elems), 0) + start
        total = jnp.zeros((tall, elems), F32)
        for corner in range(connect_ref.shape[0]):
            hit = node == connect_ref[corner : corner + 1, :]
            total = total + jnp.where(hit, coef_ref[corner : corner + 1, :], 0.0)
        high = total.astype(BF16)
        high_ref[start : start + tall, :] = high
        low_ref[start : start + tall, :] = (total - high.astype(F32)).astype(BF16)


def slab_of(device):
    return device % 2 * 8 + device // 2 % 8


def pack_kernel(
    line_hbm, freq_hbm, damping_hbm, rows_hbm, factor_hbm, sent_ref, gain_ref,
    line_ref, freq_ref, damping_ref, rows_ref, factor_ref, sems,
):
    devices, _, width = sent_ref.shape
    rows = rows_ref.shape[0]
    parts = sent_ref.shape[1] // rows - 1
    lines = line_ref.shape[0]
    pairs = (
        (rows_hbm, rows_ref),
        (factor_hbm, factor_ref),
        (line_hbm, line_ref),
        (freq_hbm, freq_ref),
        (damping_hbm, damping_ref),
    )
    copies = [pltpu.make_async_copy(a, b, sems.at[k]) for k, (a, b) in enumerate(pairs)]
    for copy in copies:
        copy.start()
    copies[0].wait()
    copies[1].wait()
    factor = factor_ref[...]
    for device in range(devices):
        for part in range(parts):
            here = (slab_of(device) * parts + part) * width
            sent_ref[device, part * rows : (part + 1) * rows, :] = rows_ref[:, here : here + width]
        sent_ref[device, parts * rows :, :] = factor
    for copy in copies[2:]:
        copy.wait()
    slab = slab_of(lax.axis_index(AXES))
    for part in range(parts):
        here = pl.ds(slab * parts + part, 1)
        for line in range(lines):
            real, imag = modal_gain(freq_ref[here, :], damping_ref[here, :], line_ref[line])
            row = 2 * (part * lines + line)
            gain_ref[row : row + 1, :] = real
            gain_ref[row + 1 : row + 2, :] = imag


def pseudo_kernel(gain_ref, got_ref, pseudo_ref, *, rows, lines):
    devices, tall, width = got_ref.shape
    parts = tall // rows - 1
    factor = got_ref[:, parts * rows :, :].reshape(devices * rows, width)
    columns = width // lines
    half = columns // 2
    for part in range(parts):
        shapes = got_ref[:, part * rows : (part + 1) * rows, :].reshape(devices * rows, width)
        forced = lax.dot_general(
            factor, shapes, (((0,), (0,)), ((), ())), preferred_element_type=F32
        )
        pieces = []
        for line in range(lines):
            row = 2 * (part * lines + line)
            gain_real = gain_ref[row : row + 1, :]
            gain_imag = gain_ref[row + 1 : row + 2, :]
            real = forced[line * columns : line * columns + half]
            imag = forced[line * columns + half : (line + 1) * columns]
            pieces.append(gain_real * real - gain_imag * imag)
            pieces.append(gain_real * imag + gain_imag * real)
        pseudo = jnp.concatenate(pieces, axis=0).T.astype(BF16)
        for copy in range(pseudo_ref.shape[0]):
            pseudo_ref[copy, part * width : (part + 1) * width, :] = pseudo


def first_kernel(modes_ref, pseudo_ref, total_ref):
    depth = pseudo_ref.shape[0]
    core = lax.axis_index(AXES) % 2
    here = pl.ds(pl.multiple_of(core * depth, depth), depth)
    total_ref[...] = jnp.dot(modes_ref[:, here], pseudo_ref[...], preferred_element_type=F32)


def second_kernel(pick_ref, modes_ref, pseudo_ref, total_ref, table_ref, far_ref, near_ref):
    depth = pseudo_ref.shape[0]
    odd = lax.axis_index(AXES) % 2
    here = pl.ds(pl.multiple_of((1 - odd) * depth, depth), depth)
    total = total_ref[...] + jnp.dot(
        modes_ref[:, here], pseudo_ref[...], preferred_element_type=F32
    )
    export = lax.dot_general(
        pick_ref[...], total.astype(BF16), (((0,), (0,)), ((), ())), preferred_element_type=F32
    ).astype(BF16)
    rim = far_ref.shape[0]
    far_ref[...] = jnp.where(odd == 1, export[rim:], export[:rim])
    near_ref[...] = jnp.where(odd == 1, export[:rim], export[rim:])
    table_ref[...] = total.T.astype(BF16)


def own_kernel(table_ref, high_ref, low_ref, stress_ref, *, rim):
    rows = table_ref.shape[1]
    table = table_ref[...]
    stress = jnp.dot(table, high_ref[rim : rim + rows, :], preferred_element_type=F32)
    stress_ref[...] = stress + jnp.dot(
        table, low_ref[rim : rim + rows, :], preferred_element_type=F32
    )


def power_kernel(stress_ref, far_ref, near_ref, high_ref, low_ref, power_ref):
    rim = far_ref.shape[0]
    nodes = high_ref.shape[0]
    lines = power_ref.shape[0]
    odd = lax.axis_index(AXES) % 2
    after = nodes - rim
    stress = stress_ref[...]
    for rows_ref, start in ((near_ref, after * (1 - odd)), (far_ref, after * odd)):
        here = pl.ds(pl.multiple_of(start, rim), rim)
        for part in (high_ref, low_ref):
            stress = stress + lax.dot_general(
                rows_ref[...],
                part[here, :],
                (((0,), (0,)), ((), ())),
                preferred_element_type=F32,
            )
    squares = stress * stress
    columns = squares.shape[0] // lines
    for line in range(lines):
        power_ref[line : line + 1, :] = (
            jnp.sum(squares[line * columns : (line + 1) * columns], axis=0, keepdims=True)
            / columns
        )


def call(kernel, name, out, *operands, flops, hbm=0, scratch=(), vmem=VMEM_BYTES):
    shapes = [jax.ShapeDtypeStruct(shape, dtype) for shape, dtype in out]
    moved = sum(x.size * x.dtype.itemsize for x in operands)
    moved += sum(math.prod(shape) * jnp.dtype(dtype).itemsize for shape, dtype in out)
    result = pl.pallas_call(
        kernel,
        out_shape=shapes,
        in_specs=[remains()] * hbm + [whole()] * (len(operands) - hbm),
        out_specs=[whole()] * len(out),
        scratch_shapes=scratch,
        compiler_params=pltpu.CompilerParams(vmem_limit_bytes=vmem),
        cost_estimate=pl.CostEstimate(flops=flops, bytes_accessed=moved, transcendentals=0),
        name=name,
    )(*operands)
    return result if len(out) > 1 else result[0]


def pseudo_by_sum(input_rows, input_factor, mode_freq, mode_damping, line_freq):
    lines = line_freq.shape[0]
    columns = input_factor.shape[1] // lines
    half = columns // 2
    forced = lax.psum(
        lax.dot_general(
            input_rows, input_factor, (((0,), (0,)), ((), ())), preferred_element_type=F32
        ),
        AXES,
    )
    pieces = []
    for line in range(lines):
        gain_real, gain_imag = modal_gain(mode_freq, mode_damping, line_freq[line])
        gain_real, gain_imag = gain_real[:, None], gain_imag[:, None]
        real = forced[:, line * columns : line * columns + half]
        imag = forced[:, line * columns + half : (line + 1) * columns]
        pieces.append(gain_real * real - gain_imag * imag)
        pieces.append(gain_real * imag + gain_imag * real)
    return jnp.concatenate(pieces, axis=1).astype(BF16)


def own_pseudo(input_rows, input_factor, mode_freq, mode_damping, line_freq, copies):
    devices = math.prod(FAST_SHAPE)
    rows, modes = input_rows.shape
    width = input_factor.shape[1]
    lines = line_freq.shape[0]
    parts = modes // (devices // 2 * width)
    sent, gains = call(
        pack_kernel,
        "pack",
        [((devices, (parts + 1) * rows, width), BF16), ((parts * 2 * lines, width), F32)],
        line_freq,
        mode_freq.reshape(-1, width),
        mode_damping.reshape(-1, width),
        input_rows,
        input_factor,
        flops=0,
        hbm=5,
        vmem=VMEM_ALL,
        scratch=[
            pltpu.SMEM((lines,), F32),
            pltpu.VMEM((modes // width, width), F32),
            pltpu.VMEM((modes // width, width), F32),
            pltpu.VMEM((rows, modes), BF16),
            pltpu.VMEM((rows, width), BF16),
            pltpu.SemaphoreType.DMA((5,)),
        ],
    )
    got = lax.all_to_all(sent, AXES, 0, 0)
    return call(
        functools.partial(pseudo_kernel, rows=rows, lines=lines),
        "pseudo",
        [((copies, parts * width, width), BF16)],
        gains,
        got,
        flops=8 * 1024**3,
    )


def local(
    shape,
    mode_rows,
    input_rows,
    input_factor,
    mode_freq,
    mode_damping,
    line_freq,
    boundary_rows,
    connectivity,
    stress_coef,
):
    devices = math.prod(shape)
    rows, modes = mode_rows.shape
    width = input_factor.shape[1]
    lines = line_freq.shape[0]
    exports = boundary_rows.shape[0]
    rim = exports // 2
    elems = connectivity.shape[1]
    nodes = rows + exports
    pick, high, low = call(
        setup_kernel,
        "setup",
        [((rows, exports), BF16)] + [((nodes, elems), BF16)] * 2,
        boundary_rows.reshape(1, exports),
        connectivity,
        stress_coef,
        flops=16 * nodes * elems,
    )
    inputs = (input_rows, input_factor, mode_freq, mode_damping, line_freq)
    if shape == FAST_SHAPE and modes == devices * LANES and input_rows.shape[0] % 16 == 0:
        groups = [[h * 16 + j * 2 + c for j in range(8)] for h in range(2) for c in range(2)]
        got = lax.all_to_all(own_pseudo(*inputs, copies=8), AXES, 0, 0, axis_index_groups=groups)
        mine = got.reshape(modes // 2, width)
        theirs = lax.ppermute(mine, AXES, [(i, i ^ 1) for i in range(devices)])
    else:
        pseudo = pseudo_by_sum(*inputs).reshape(2, modes // 2, width)
        core = lax.axis_index(AXES) % 2
        mine = lax.dynamic_index_in_dim(pseudo, core, 0, keepdims=False)
        theirs = lax.dynamic_index_in_dim(pseudo, 1 - core, 0, keepdims=False)
    total = call(
        first_kernel,
        "first",
        [((rows, width), F32)],
        mode_rows,
        mine,
        flops=rows * modes * width,
    )
    table, far, near = call(
        second_kernel,
        "second",
        [((width, rows), BF16), ((rim, width), BF16), ((rim, width), BF16)],
        pick,
        mode_rows,
        theirs,
        total,
        flops=rows * modes * width + 2 * exports * rows * width,
    )
    inner = [(i, i ^ 1) for i in range(devices)]
    outer = [(i, i + 1) for i in range(1, devices - 1, 2)]
    outer += [(j, i) for i, j in outer]
    near = lax.ppermute(near, AXES, inner)
    far = lax.ppermute(far, AXES, outer)
    stress = call(
        functools.partial(own_kernel, rim=rim),
        "own",
        [((width, elems), F32)],
        table,
        high,
        low,
        flops=4 * rows * elems * width,
    )
    return call(
        power_kernel,
        "power",
        [((lines, elems), F32)],
        stress,
        far,
        near,
        high,
        low,
        flops=4 * exports * elems * width,
    )


def solution(mesh):
    shape = tuple(mesh.shape[axis] for axis in AXES)
    placed = (
        P(AXES, None),
        P(AXES, None),
        P(AXES, None),
        P(),
        P(),
        P(),
        P(AXES),
        P(None, AXES),
        P(None, AXES),
    )
    return jax.shard_map(
        functools.partial(local, shape),
        mesh=mesh,
        in_specs=placed,
        out_specs=P(None, AXES),
        check_vma=False,
    )
```

```python
import functools
import math

import jax
import jax.numpy as jnp
from jax import lax
from jax.experimental import pallas as pl
from jax.experimental.pallas import tpu as pltpu
from jax.sharding import PartitionSpec as P

AXES = ("region", "sub")
LANES = 128
F32 = jnp.float32
BF16 = jnp.bfloat16
VMEM_BYTES = 24 * 1024 * 1024
LONG = 8 * 1024**3
FAST_SHAPE = (8, 4)


def whole(*_):
    return pl.BlockSpec(memory_space=pltpu.VMEM)


def modal_gain(freq, damping, omega):
    detune = freq * freq - omega * omega
    damped = 2.0 * damping * freq * omega
    magnitude = detune * detune + damped * damped
    return detune / magnitude, -damped / magnitude


def slab_of(device):
    return device % 2 * 8 + device // 2 % 8


def ones_kernel(ones_ref):
    ones_ref[...] = jnp.ones_like(ones_ref)


def pack_kernel(ones_ref, line_ref, freq_ref, damping_ref, rows_ref, factor_ref, sent_ref, gain_ref):
    devices, _, width = sent_ref.shape
    rows = rows_ref.shape[0]
    parts = sent_ref.shape[1] // rows - 1
    lines = line_ref.shape[1]
    factor = factor_ref[...]
    for device in range(devices):
        for part in range(parts):
            here = (slab_of(device) * parts + part) * width
            sent_ref[device, part * rows : (part + 1) * rows, :] = rows_ref[:, here : here + width]
        sent_ref[device, parts * rows :, :] = factor
    slab = slab_of(lax.axis_index(AXES))
    one = ones_ref[0:1, :]
    for part in range(parts):
        here = pl.ds(slab * parts + part, 1)
        for line in range(lines):
            omega = line_ref[:, line : line + 1]
            real, imag = modal_gain(freq_ref[here, :], damping_ref[here, :], omega)
            row = 2 * (part * lines + line)
            gain_ref[row : row + 1, :] = real * one
            gain_ref[row + 1 : row + 2, :] = imag * one


def pseudo_kernel(gain_ref, got_ref, pseudo_ref, *, rows, lines):
    devices, tall, width = got_ref.shape
    parts = tall // rows - 1
    factor = got_ref[:, parts * rows :, :].reshape(devices * rows, width)
    columns = width // lines
    half = columns // 2
    for part in range(parts):
        shapes = got_ref[:, part * rows : (part + 1) * rows, :].reshape(devices * rows, width)
        forced = lax.dot_general(
            factor, shapes, (((0,), (0,)), ((), ())), preferred_element_type=F32
        )
        pieces = []
        for line in range(lines):
            row = 2 * (part * lines + line)
            gain_real = gain_ref[row : row + 1, :]
            gain_imag = gain_ref[row + 1 : row + 2, :]
            real = forced[line * columns : line * columns + half]
            imag = forced[line * columns + half : (line + 1) * columns]
            pieces.append(gain_real * real - gain_imag * imag)
            pieces.append(gain_real * imag + gain_imag * real)
        pseudo = jnp.concatenate(pieces, axis=0).T.astype(BF16)
        for copy in range(pseudo_ref.shape[0]):
            pseudo_ref[copy, part * width : (part + 1) * width, :] = pseudo


def first_kernel(boundary_ref, modes_ref, pseudo_ref, total_ref, part_ref, picked_ref):
    rows = modes_ref.shape[0]
    depth = pseudo_ref.shape[0]
    odd = lax.axis_index(AXES) % 2
    mine = pl.ds(pl.multiple_of(odd * depth, depth), depth)
    other = pl.ds(pl.multiple_of((1 - odd) * depth, depth), depth)
    total = jnp.dot(modes_ref[:, mine], pseudo_ref[...], preferred_element_type=F32)
    total_ref[...] = total
    pick = lax.broadcasted_iota(jnp.int32, (rows, boundary_ref.shape[1]), 0) == boundary_ref[...]
    pick = pick.astype(F32).T
    part_ref[...] = jnp.dot(
        pick, total, precision=lax.Precision.HIGHEST, preferred_element_type=F32
    )
    picked_ref[...] = jnp.dot(
        pick.astype(BF16), modes_ref[:, other], preferred_element_type=F32
    ).astype(BF16)


def export_kernel(part_ref, picked_ref, pseudo_ref, far_ref, near_ref):
    export = part_ref[...] + jnp.dot(
        picked_ref[...], pseudo_ref[...], preferred_element_type=F32
    )
    export = export.astype(BF16)
    odd = lax.axis_index(AXES) % 2 == 1
    rim = far_ref.shape[0]
    far_ref[...] = jnp.where(odd, export[rim:], export[:rim])
    near_ref[...] = jnp.where(odd, export[:rim], export[rim:])


def own_kernel(
    connect_ref, coef_ref, modes_ref, pseudo_ref, total_ref, stress_ref, high_ref, low_ref, own_ref
):
    depth = pseudo_ref.shape[0]
    rows = modes_ref.shape[0]
    elems = connect_ref.shape[1]
    rim = high_ref.shape[0] // 2
    odd = lax.axis_index(AXES) % 2

    def matrix(start, tall):
        node = lax.broadcasted_iota(jnp.int32, (tall, elems), 0) + start
        total = jnp.zeros((tall, elems), F32)
        for corner in range(connect_ref.shape[0]):
            hit = node == connect_ref[corner : corner + 1, :]
            total = total + jnp.where(hit, coef_ref[corner : corner + 1, :], 0.0)
        high = total.astype(BF16)
        return high, (total - high.astype(F32)).astype(BF16)

    after = rim + rows
    for place, start in ((0, after * odd), (1, after * (1 - odd))):
        here = slice(place * rim, (place + 1) * rim)
        high_ref[here, :], low_ref[here, :] = matrix(start, rim)
    for start in range(0, rows, rim):
        here = slice(start, start + rim)
        own_ref[0, here, :], own_ref[1, here, :] = matrix(start + rim, rim)
    other = pl.ds(pl.multiple_of((1 - odd) * depth, depth), depth)
    total = total_ref[...] + jnp.dot(
        modes_ref[:, other], pseudo_ref[...], preferred_element_type=F32
    )
    table = total.T.astype(BF16)
    stress = jnp.dot(table, own_ref[0], preferred_element_type=F32)
    stress_ref[...] = stress + jnp.dot(table, own_ref[1], preferred_element_type=F32)


def power_kernel(stress_ref, far_ref, near_ref, high_ref, low_ref, power_ref):
    rows = jnp.concatenate([far_ref[...], near_ref[...]], axis=0)
    stress = stress_ref[...]
    for part in (high_ref, low_ref):
        stress = stress + lax.dot_general(
            rows, part[...], (((0,), (0,)), ((), ())), preferred_element_type=F32
        )
    squares = stress * stress
    lines = power_ref.shape[0]
    columns = squares.shape[0] // lines
    for line in range(lines):
        power_ref[line : line + 1, :] = (
            jnp.sum(squares[line * columns : (line + 1) * columns], axis=0, keepdims=True)
            / columns
        )


def call(kernel, name, out, *operands, flops, scratch=()):
    shapes = [jax.ShapeDtypeStruct(shape, dtype) for shape, dtype in out]
    moved = sum(x.size * x.dtype.itemsize for x in operands)
    moved += sum(math.prod(shape) * jnp.dtype(dtype).itemsize for shape, dtype in out)
    result = pl.pallas_call(
        kernel,
        out_shape=shapes,
        in_specs=[whole()] * len(operands),
        out_specs=[whole()] * len(out),
        scratch_shapes=scratch,
        compiler_params=pltpu.CompilerParams(vmem_limit_bytes=VMEM_BYTES),
        cost_estimate=pl.CostEstimate(flops=flops, bytes_accessed=moved, transcendentals=0),
        name=name,
    )(*operands)
    return result if len(out) > 1 else result[0]


def pseudo_by_sum(input_rows, input_factor, mode_freq, mode_damping, line_freq):
    lines = line_freq.shape[0]
    columns = input_factor.shape[1] // lines
    half = columns // 2
    forced = lax.psum(
        lax.dot_general(
            input_rows, input_factor, (((0,), (0,)), ((), ())), preferred_element_type=F32
        ),
        AXES,
    )
    pieces = []
    for line in range(lines):
        gain_real, gain_imag = modal_gain(mode_freq, mode_damping, line_freq[line])
        gain_real, gain_imag = gain_real[:, None], gain_imag[:, None]
        real = forced[:, line * columns : line * columns + half]
        imag = forced[:, line * columns + half : (line + 1) * columns]
        pieces.append(gain_real * real - gain_imag * imag)
        pieces.append(gain_real * imag + gain_imag * real)
    return jnp.concatenate(pieces, axis=1).astype(BF16)


def own_pseudo(input_rows, input_factor, mode_freq, mode_damping, line_freq, copies):
    devices = math.prod(FAST_SHAPE)
    rows, modes = input_rows.shape
    width = input_factor.shape[1]
    lines = line_freq.shape[0]
    parts = modes // (devices // 2 * width)
    ones = call(ones_kernel, "ones", [((8, width), F32)], flops=LONG)
    sent, gains = call(
        pack_kernel,
        "pack",
        [((devices, (parts + 1) * rows, width), BF16), ((parts * 2 * lines, width), F32)],
        ones,
        line_freq.reshape(1, lines),
        mode_freq.reshape(-1, width),
        mode_damping.reshape(-1, width),
        input_rows,
        input_factor,
        flops=0,
    )
    got = lax.all_to_all(sent, AXES, 0, 0)
    return call(
        functools.partial(pseudo_kernel, rows=rows, lines=lines),
        "pseudo",
        [((copies, parts * width, width), BF16)],
        gains,
        got,
        flops=LONG,
    )


def local(
    shape,
    mode_rows,
    input_rows,
    input_factor,
    mode_freq,
    mode_damping,
    line_freq,
    boundary_rows,
    connectivity,
    stress_coef,
):
    devices = math.prod(shape)
    rows, modes = mode_rows.shape
    width = input_factor.shape[1]
    lines = line_freq.shape[0]
    exports = boundary_rows.shape[0]
    rim = exports // 2
    elems = connectivity.shape[1]
    inputs = (input_rows, input_factor, mode_freq, mode_damping, line_freq)
    if shape == FAST_SHAPE and modes == devices * LANES and input_rows.shape[0] % 16 == 0:
        groups = [[h * 16 + j * 2 + c for j in range(8)] for h in range(2) for c in range(2)]
        got = lax.all_to_all(own_pseudo(*inputs, copies=8), AXES, 0, 0, axis_index_groups=groups)
        mine = got.reshape(modes // 2, width)
        theirs = lax.ppermute(mine, AXES, [(i, i ^ 1) for i in range(devices)])
    else:
        pseudo = pseudo_by_sum(*inputs).reshape(2, modes // 2, width)
        core = lax.axis_index(AXES) % 2
        mine = lax.dynamic_index_in_dim(pseudo, core, 0, keepdims=False)
        theirs = lax.dynamic_index_in_dim(pseudo, 1 - core, 0, keepdims=False)
    total, part, picked = call(
        first_kernel,
        "first",
        [((rows, width), F32), ((exports, width), F32), ((exports, modes // 2), BF16)],
        boundary_rows.reshape(1, exports),
        mode_rows,
        mine,
        flops=rows * modes * (width + exports),
    )
    far, near = call(
        export_kernel,
        "export",
        [((rim, width), BF16)] * 2,
        part,
        picked,
        theirs,
        flops=exports * modes * width,
    )
    inner = [(i, i ^ 1) for i in range(devices)]
    outer = [(i, i + 1) for i in range(1, devices - 1, 2)]
    outer += [(j, i) for i, j in outer]
    near = lax.ppermute(near, AXES, inner)
    far = lax.ppermute(far, AXES, outer)
    stress, high, low = call(
        own_kernel,
        "own",
        [((width, elems), F32)] + [((exports, elems), BF16)] * 2,
        connectivity,
        stress_coef,
        mode_rows,
        theirs,
        total,
        flops=rows * modes * width + 4 * rows * elems * width,
        scratch=[pltpu.VMEM((2, rows, elems), BF16)],
    )
    return call(
        power_kernel,
        "power",
        [((lines, elems), F32)],
        stress,
        far,
        near,
        high,
        low,
        flops=4 * exports * elems * width,
    )


def solution(mesh):
    shape = tuple(mesh.shape[axis] for axis in AXES)
    placed = (
        P(AXES, None),
        P(AXES, None),
        P(AXES, None),
        P(),
        P(),
        P(),
        P(AXES),
        P(None, AXES),
        P(None, AXES),
    )
    return jax.shard_map(
        functools.partial(local, shape),
        mesh=mesh,
        in_specs=placed,
        out_specs=P(None, AXES),
        check_vma=False,
    )
```

```python
import functools
import math

import jax
import jax.numpy as jnp
from jax import lax
from jax.experimental import pallas as pl
from jax.experimental.pallas import tpu as pltpu
from jax.sharding import PartitionSpec as P

AXES = ("region", "sub")
LANES = 128
F32 = jnp.float32
BF16 = jnp.bfloat16
VMEM_BYTES = 24 * 1024 * 1024
LONG = 8 * 1024**3
FAST_SHAPE = (8, 4)


def whole(*_):
    return pl.BlockSpec(memory_space=pltpu.VMEM)


def modal_gain(freq, damping, omega):
    detune = freq * freq - omega * omega
    damped = 2.0 * damping * freq * omega
    magnitude = detune * detune + damped * damped
    return detune / magnitude, -damped / magnitude


def slab_of(device):
    return device % 2 * 8 + device // 2 % 8


def exchange_order(devices):
    planes = devices // 4
    return [z * planes + plane for plane in range(planes) for z in (0, 2, 1, 3)]


def ones_kernel(ones_ref):
    ones_ref[...] = jnp.ones_like(ones_ref)


def pack_kernel(ones_ref, line_ref, freq_ref, damping_ref, rows_ref, factor_ref, sent_ref, gain_ref):
    devices, _, width = sent_ref.shape
    rows = rows_ref.shape[0]
    parts = sent_ref.shape[1] // rows - 1
    lines = line_ref.shape[1]
    factor = factor_ref[...]
    for place, device in enumerate(exchange_order(devices)):
        for part in range(parts):
            here = (slab_of(device) * parts + part) * width
            sent_ref[place, part * rows : (part + 1) * rows, :] = rows_ref[:, here : here + width]
        sent_ref[place, parts * rows :, :] = factor
    slab = slab_of(lax.axis_index(AXES))
    one = ones_ref[0:1, :]
    for part in range(parts):
        here = pl.ds(slab * parts + part, 1)
        for line in range(lines):
            omega = line_ref[:, line : line + 1]
            real, imag = modal_gain(freq_ref[here, :], damping_ref[here, :], omega)
            row = 2 * (part * lines + line)
            gain_ref[row : row + 1, :] = real * one
            gain_ref[row + 1 : row + 2, :] = imag * one


def pseudo_kernel(gain_ref, got_ref, pseudo_ref, *, rows, lines):
    devices, tall, width = got_ref.shape
    parts = tall // rows - 1
    factor = got_ref[:, parts * rows :, :].reshape(devices * rows, width)
    columns = width // lines
    half = columns // 2
    for part in range(parts):
        shapes = got_ref[:, part * rows : (part + 1) * rows, :].reshape(devices * rows, width)
        forced = lax.dot_general(
            factor, shapes, (((0,), (0,)), ((), ())), preferred_element_type=F32
        )
        pieces = []
        for line in range(lines):
            row = 2 * (part * lines + line)
            gain_real = gain_ref[row : row + 1, :]
            gain_imag = gain_ref[row + 1 : row + 2, :]
            real = forced[line * columns : line * columns + half]
            imag = forced[line * columns + half : (line + 1) * columns]
            pieces.append(gain_real * real - gain_imag * imag)
            pieces.append(gain_real * imag + gain_imag * real)
        pseudo = jnp.concatenate(pieces, axis=0).T.astype(BF16)
        for copy in range(pseudo_ref.shape[0]):
            pseudo_ref[copy, part * width : (part + 1) * width, :] = pseudo


def first_kernel(boundary_ref, modes_ref, pseudo_ref, total_ref, part_ref, picked_ref):
    rows = modes_ref.shape[0]
    depth = pseudo_ref.shape[0]
    odd = lax.axis_index(AXES) % 2
    mine = pl.ds(pl.multiple_of(odd * depth, depth), depth)
    other = pl.ds(pl.multiple_of((1 - odd) * depth, depth), depth)
    total = jnp.dot(modes_ref[:, mine], pseudo_ref[...], preferred_element_type=F32)
    total_ref[...] = total
    exports = boundary_ref.shape[1]
    chosen = jnp.broadcast_to(boundary_ref[...], (exports, exports)).astype(F32).T
    column = lax.broadcasted_iota(jnp.int32, (exports, exports), 1).astype(F32)
    pick = jnp.concatenate(
        [(column + start == chosen).astype(F32) for start in range(0, rows, exports)], axis=1
    ).astype(BF16)
    high = total.astype(BF16)
    rest = total - high.astype(F32)
    middle = rest.astype(BF16)
    low = (rest - middle.astype(F32)).astype(BF16)
    parts = jnp.dot(
        pick, jnp.concatenate([high, middle, low], axis=1), preferred_element_type=F32
    )
    width = total.shape[1]
    part_ref[...] = parts[:, :width] + parts[:, width : 2 * width] + parts[:, 2 * width :]
    picked_ref[...] = jnp.dot(
        pick, modes_ref[:, other], preferred_element_type=F32
    ).astype(BF16)


def export_kernel(part_ref, picked_ref, pseudo_ref, far_ref, near_ref):
    export = part_ref[...] + jnp.dot(
        picked_ref[...], pseudo_ref[...], preferred_element_type=F32
    )
    export = export.astype(BF16)
    odd = lax.axis_index(AXES) % 2 == 1
    rim = far_ref.shape[0]
    far_ref[...] = jnp.where(odd, export[rim:], export[:rim])
    near_ref[...] = jnp.where(odd, export[:rim], export[rim:])


def own_kernel(
    connect_ref, coef_ref, modes_ref, pseudo_ref, total_ref, stress_ref, high_ref, low_ref, own_ref
):
    depth = pseudo_ref.shape[0]
    rows = modes_ref.shape[0]
    elems = connect_ref.shape[1]
    rim = high_ref.shape[0] // 2
    odd = lax.axis_index(AXES) % 2

    def matrix(start, tall):
        node = lax.broadcasted_iota(jnp.int32, (tall, elems), 0) + start
        total = jnp.zeros((tall, elems), F32)
        for corner in range(connect_ref.shape[0]):
            hit = node == connect_ref[corner : corner + 1, :]
            total = total + jnp.where(hit, coef_ref[corner : corner + 1, :], 0.0)
        high = total.astype(BF16)
        return high, (total - high.astype(F32)).astype(BF16)

    after = rim + rows
    for place, start in ((0, after * odd), (1, after * (1 - odd))):
        here = slice(place * rim, (place + 1) * rim)
        high_ref[here, :], low_ref[here, :] = matrix(start, rim)
    for start in range(0, rows, rim):
        here = slice(start, start + rim)
        own_ref[0, here, :], own_ref[1, here, :] = matrix(start + rim, rim)
    other = pl.ds(pl.multiple_of((1 - odd) * depth, depth), depth)
    total = total_ref[...] + jnp.dot(
        modes_ref[:, other], pseudo_ref[...], preferred_element_type=F32
    )
    table = total.T.astype(BF16)
    stress = jnp.dot(table, own_ref[0], preferred_element_type=F32)
    stress_ref[...] = stress + jnp.dot(table, own_ref[1], preferred_element_type=F32)


def power_kernel(stress_ref, far_ref, near_ref, high_ref, low_ref, power_ref):
    rows = jnp.concatenate([far_ref[...], near_ref[...]], axis=0)
    stress = stress_ref[...]
    for part in (high_ref, low_ref):
        stress = stress + lax.dot_general(
            rows, part[...], (((0,), (0,)), ((), ())), preferred_element_type=F32
        )
    squares = stress * stress
    lines = power_ref.shape[0]
    columns = squares.shape[0] // lines
    for line in range(lines):
        power_ref[line : line + 1, :] = (
            jnp.sum(squares[line * columns : (line + 1) * columns], axis=0, keepdims=True)
            / columns
        )


def call(kernel, name, out, *operands, flops, scratch=()):
    shapes = [jax.ShapeDtypeStruct(shape, dtype) for shape, dtype in out]
    moved = sum(x.size * x.dtype.itemsize for x in operands)
    moved += sum(math.prod(shape) * jnp.dtype(dtype).itemsize for shape, dtype in out)
    result = pl.pallas_call(
        kernel,
        out_shape=shapes,
        in_specs=[whole()] * len(operands),
        out_specs=[whole()] * len(out),
        scratch_shapes=scratch,
        compiler_params=pltpu.CompilerParams(vmem_limit_bytes=VMEM_BYTES),
        cost_estimate=pl.CostEstimate(flops=flops, bytes_accessed=moved, transcendentals=0),
        name=name,
    )(*operands)
    return result if len(out) > 1 else result[0]


def pseudo_by_sum(input_rows, input_factor, mode_freq, mode_damping, line_freq):
    lines = line_freq.shape[0]
    columns = input_factor.shape[1] // lines
    half = columns // 2
    forced = lax.psum(
        lax.dot_general(
            input_rows, input_factor, (((0,), (0,)), ((), ())), preferred_element_type=F32
        ),
        AXES,
    )
    pieces = []
    for line in range(lines):
        gain_real, gain_imag = modal_gain(mode_freq, mode_damping, line_freq[line])
        gain_real, gain_imag = gain_real[:, None], gain_imag[:, None]
        real = forced[:, line * columns : line * columns + half]
        imag = forced[:, line * columns + half : (line + 1) * columns]
        pieces.append(gain_real * real - gain_imag * imag)
        pieces.append(gain_real * imag + gain_imag * real)
    return jnp.concatenate(pieces, axis=1).astype(BF16)


def own_pseudo(input_rows, input_factor, mode_freq, mode_damping, line_freq, copies):
    devices = math.prod(FAST_SHAPE)
    rows, modes = input_rows.shape
    width = input_factor.shape[1]
    lines = line_freq.shape[0]
    parts = modes // (devices // 2 * width)
    ones = call(ones_kernel, "ones", [((8, width), F32)], flops=LONG)
    sent, gains = call(
        pack_kernel,
        "pack",
        [((devices, (parts + 1) * rows, width), BF16), ((parts * 2 * lines, width), F32)],
        ones,
        line_freq.reshape(1, lines),
        mode_freq.reshape(-1, width),
        mode_damping.reshape(-1, width),
        input_rows,
        input_factor,
        flops=0,
    )
    got = lax.all_to_all(sent, AXES, 0, 0, axis_index_groups=[exchange_order(devices)])
    return call(
        functools.partial(pseudo_kernel, rows=rows, lines=lines),
        "pseudo",
        [((copies, parts * width, width), BF16)],
        gains,
        got,
        flops=LONG,
    )


def local(
    shape,
    mode_rows,
    input_rows,
    input_factor,
    mode_freq,
    mode_damping,
    line_freq,
    boundary_rows,
    connectivity,
    stress_coef,
):
    devices = math.prod(shape)
    rows, modes = mode_rows.shape
    width = input_factor.shape[1]
    lines = line_freq.shape[0]
    exports = boundary_rows.shape[0]
    rim = exports // 2
    elems = connectivity.shape[1]
    inputs = (input_rows, input_factor, mode_freq, mode_damping, line_freq)
    if shape == FAST_SHAPE and modes == devices * LANES and input_rows.shape[0] % 16 == 0:
        groups = [[h * 16 + j * 2 + c for j in range(8)] for h in range(2) for c in range(2)]
        got = lax.all_to_all(own_pseudo(*inputs, copies=8), AXES, 0, 0, axis_index_groups=groups)
        mine = got.reshape(modes // 2, width)
        theirs = lax.ppermute(mine, AXES, [(i, i ^ 1) for i in range(devices)])
    else:
        pseudo = pseudo_by_sum(*inputs).reshape(2, modes // 2, width)
        core = lax.axis_index(AXES) % 2
        mine = lax.dynamic_index_in_dim(pseudo, core, 0, keepdims=False)
        theirs = lax.dynamic_index_in_dim(pseudo, 1 - core, 0, keepdims=False)
    total, part, picked = call(
        first_kernel,
        "first",
        [((rows, width), F32), ((exports, width), F32), ((exports, modes // 2), BF16)],
        boundary_rows.reshape(1, exports),
        mode_rows,
        mine,
        flops=rows * modes * (width + exports),
    )
    far, near = call(
        export_kernel,
        "export",
        [((rim, width), BF16)] * 2,
        part,
        picked,
        theirs,
        flops=exports * modes * width,
    )
    inner = [(i, i ^ 1) for i in range(devices)]
    outer = [(i, i + 1) for i in range(1, devices - 1, 2)]
    outer += [(j, i) for i, j in outer]
    near = lax.ppermute(near, AXES, inner)
    far = lax.ppermute(far, AXES, outer)
    stress, high, low = call(
        own_kernel,
        "own",
        [((width, elems), F32)] + [((exports, elems), BF16)] * 2,
        connectivity,
        stress_coef,
        mode_rows,
        theirs,
        total,
        flops=rows * modes * width + 4 * rows * elems * width,
        scratch=[pltpu.VMEM((2, rows, elems), BF16)],
    )
    return call(
        power_kernel,
        "power",
        [((lines, elems), F32)],
        stress,
        far,
        near,
        high,
        low,
        flops=4 * exports * elems * width,
    )


def solution(mesh):
    shape = tuple(mesh.shape[axis] for axis in AXES)
    placed = (
        P(AXES, None),
        P(AXES, None),
        P(AXES, None),
        P(),
        P(),
        P(),
        P(AXES),
        P(None, AXES),
        P(None, AXES),
    )
    return jax.shard_map(
        functools.partial(local, shape),
        mesh=mesh,
        in_specs=placed,
        out_specs=P(None, AXES),
        check_vma=False,
    )
```

```python
import functools
import math

import jax
import jax.numpy as jnp
from jax import lax
from jax.experimental import pallas as pl
from jax.experimental.pallas import tpu as pltpu
from jax.sharding import PartitionSpec as P

AXES = ("region", "sub")
LANES = 128
F32 = jnp.float32
BF16 = jnp.bfloat16
VMEM_BYTES = 24 * 1024 * 1024
LONG = 8 * 1024**3
FAST_SHAPE = (8, 4)


def whole(*_):
    return pl.BlockSpec(memory_space=pltpu.VMEM)


def modal_gain(freq, damping, omega):
    detune = freq * freq - omega * omega
    damped = 2.0 * damping * freq * omega
    magnitude = detune * detune + damped * damped
    return detune / magnitude, -damped / magnitude


def ones_kernel(ones_ref):
    ones_ref[...] = jnp.ones_like(ones_ref)


def pack_kernel(ones_ref, line_ref, freq_ref, damping_ref, rows_ref, factor_ref, sent_ref, gain_ref):
    chips, tall, width = sent_ref.shape
    rows = rows_ref.shape[0]
    parts = (tall // rows - 1) // 2
    slabs = rows_ref.shape[1] // (2 * parts * width)
    lines = line_ref.shape[1]
    factor = factor_ref[...]
    for chip in range(chips):
        for half in range(2):
            for part in range(parts):
                here = ((half * slabs + chip % slabs) * parts + part) * width
                place = (half * parts + part) * rows
                sent_ref[chip, place : place + rows, :] = rows_ref[:, here : here + width]
        sent_ref[chip, 2 * parts * rows :, :] = factor
    me = lax.axis_index(AXES)
    slab = me % 2 * slabs + me // 2 % slabs
    one = ones_ref[0:1, :]
    for part in range(parts):
        here = pl.ds(slab * parts + part, 1)
        for line in range(lines):
            omega = line_ref[:, line : line + 1]
            real, imag = modal_gain(freq_ref[here, :], damping_ref[here, :], omega)
            row = 2 * (part * lines + line)
            gain_ref[row : row + 1, :] = real * one
            gain_ref[row + 1 : row + 2, :] = imag * one


def partial_kernel(got_ref, own_ref, other_ref):
    chips, tall, width = got_ref.shape
    parts = own_ref.shape[0]
    rows = tall // (2 * parts + 1)
    factor = got_ref[:, 2 * parts * rows :, :].reshape(chips * rows, width)
    odd = lax.axis_index(AXES) % 2
    for sums_ref, half in ((other_ref, 1 - odd), (own_ref, odd)):
        for part in range(parts):
            here = pl.ds(pl.multiple_of((half * parts + part) * rows, rows), rows)
            shapes = got_ref[:, here, :].reshape(chips * rows, width)
            sums_ref[part] = lax.dot_general(
                factor, shapes, (((0,), (0,)), ((), ())), preferred_element_type=F32
            )


def pseudo_kernel(gain_ref, own_ref, other_ref, pseudo_ref, *, lines):
    parts, width, _ = own_ref.shape
    columns = width // lines
    half = columns // 2
    for part in range(parts):
        forced = own_ref[part] + other_ref[part]
        pieces = []
        for line in range(lines):
            row = 2 * (part * lines + line)
            gain_real = gain_ref[row : row + 1, :]
            gain_imag = gain_ref[row + 1 : row + 2, :]
            real = forced[line * columns : line * columns + half]
            imag = forced[line * columns + half : (line + 1) * columns]
            pieces.append(gain_real * real - gain_imag * imag)
            pieces.append(gain_real * imag + gain_imag * real)
        pseudo = jnp.concatenate(pieces, axis=0).T.astype(BF16)
        for copy in range(pseudo_ref.shape[0]):
            pseudo_ref[copy, part * width : (part + 1) * width, :] = pseudo


def first_kernel(boundary_ref, modes_ref, pseudo_ref, total_ref, part_ref, picked_ref):
    rows = modes_ref.shape[0]
    depth = pseudo_ref.shape[0]
    odd = lax.axis_index(AXES) % 2
    mine = pl.ds(pl.multiple_of(odd * depth, depth), depth)
    other = pl.ds(pl.multiple_of((1 - odd) * depth, depth), depth)
    total = jnp.dot(modes_ref[:, mine], pseudo_ref[...], preferred_element_type=F32)
    total_ref[...] = total
    exports = boundary_ref.shape[1]
    chosen = jnp.broadcast_to(boundary_ref[...], (exports, exports)).astype(F32).T
    column = lax.broadcasted_iota(jnp.int32, (exports, exports), 1).astype(F32)
    pick = jnp.concatenate(
        [(column + start == chosen).astype(F32) for start in range(0, rows, exports)], axis=1
    ).astype(BF16)
    high = total.astype(BF16)
    rest = total - high.astype(F32)
    middle = rest.astype(BF16)
    low = (rest - middle.astype(F32)).astype(BF16)
    parts = jnp.dot(
        pick, jnp.concatenate([high, middle, low], axis=1), preferred_element_type=F32
    )
    width = total.shape[1]
    part_ref[...] = parts[:, :width] + parts[:, width : 2 * width] + parts[:, 2 * width :]
    picked_ref[...] = jnp.dot(
        pick, modes_ref[:, other], preferred_element_type=F32
    ).astype(BF16)


def export_kernel(part_ref, picked_ref, pseudo_ref, far_ref, near_ref):
    export = part_ref[...] + jnp.dot(
        picked_ref[...], pseudo_ref[...], preferred_element_type=F32
    )
    export = export.astype(BF16)
    odd = lax.axis_index(AXES) % 2 == 1
    rim = far_ref.shape[0]
    far_ref[...] = jnp.where(odd, export[rim:], export[:rim])
    near_ref[...] = jnp.where(odd, export[:rim], export[rim:])


def own_kernel(
    connect_ref, coef_ref, modes_ref, pseudo_ref, total_ref, stress_ref, rim_ref, own_ref
):
    depth = pseudo_ref.shape[0]
    rows = modes_ref.shape[0]
    elems = connect_ref.shape[1]
    rim = rim_ref.shape[0] // 4
    odd = lax.axis_index(AXES) % 2

    def matrix(start, tall):
        node = lax.broadcasted_iota(jnp.int32, (tall, elems), 0) + start
        total = jnp.zeros((tall, elems), F32)
        for corner in range(connect_ref.shape[0]):
            hit = node == connect_ref[corner : corner + 1, :]
            total = total + jnp.where(hit, coef_ref[corner : corner + 1, :], 0.0)
        high = total.astype(BF16)
        return high, (total - high.astype(F32)).astype(BF16)

    after = rim + rows
    for place, start in ((0, after * odd), (1, after * (1 - odd))):
        high, low = matrix(start, rim)
        rim_ref[place * rim : (place + 1) * rim, :] = high
        rim_ref[(place + 2) * rim : (place + 3) * rim, :] = low
    for start in range(0, rows, rim):
        here = slice(start, start + rim)
        own_ref[0, here, :], own_ref[1, here, :] = matrix(start + rim, rim)
    other = pl.ds(pl.multiple_of((1 - odd) * depth, depth), depth)
    total = total_ref[...] + jnp.dot(
        modes_ref[:, other], pseudo_ref[...], preferred_element_type=F32
    )
    table = total.T.astype(BF16)
    stress = jnp.dot(table, own_ref[0], preferred_element_type=F32)
    stress_ref[...] = stress + jnp.dot(table, own_ref[1], preferred_element_type=F32)


def power_kernel(stress_ref, far_ref, near_ref, rim_ref, power_ref):
    rows = [far_ref[...], near_ref[...]]
    stress = stress_ref[...] + lax.dot_general(
        jnp.concatenate(rows + rows, axis=0),
        rim_ref[...],
        (((0,), (0,)), ((), ())),
        preferred_element_type=F32,
    )
    squares = stress * stress
    lines = power_ref.shape[0]
    columns = squares.shape[0] // lines
    for line in range(lines):
        power_ref[line : line + 1, :] = (
            jnp.sum(squares[line * columns : (line + 1) * columns], axis=0, keepdims=True)
            / columns
        )


def call(kernel, name, out, *operands, flops, scratch=()):
    shapes = [jax.ShapeDtypeStruct(shape, dtype) for shape, dtype in out]
    moved = sum(x.size * x.dtype.itemsize for x in operands)
    moved += sum(math.prod(shape) * jnp.dtype(dtype).itemsize for shape, dtype in out)
    result = pl.pallas_call(
        kernel,
        out_shape=shapes,
        in_specs=[whole()] * len(operands),
        out_specs=[whole()] * len(out),
        scratch_shapes=scratch,
        compiler_params=pltpu.CompilerParams(vmem_limit_bytes=VMEM_BYTES),
        cost_estimate=pl.CostEstimate(flops=flops, bytes_accessed=moved, transcendentals=0),
        name=name,
    )(*operands)
    return result if len(out) > 1 else result[0]


def pseudo_by_sum(input_rows, input_factor, mode_freq, mode_damping, line_freq):
    lines = line_freq.shape[0]
    columns = input_factor.shape[1] // lines
    half = columns // 2
    forced = lax.psum(
        lax.dot_general(
            input_rows, input_factor, (((0,), (0,)), ((), ())), preferred_element_type=F32
        ),
        AXES,
    )
    pieces = []
    for line in range(lines):
        gain_real, gain_imag = modal_gain(mode_freq, mode_damping, line_freq[line])
        gain_real, gain_imag = gain_real[:, None], gain_imag[:, None]
        real = forced[:, line * columns : line * columns + half]
        imag = forced[:, line * columns + half : (line + 1) * columns]
        pieces.append(gain_real * real - gain_imag * imag)
        pieces.append(gain_real * imag + gain_imag * real)
    return jnp.concatenate(pieces, axis=1).astype(BF16)


def own_pseudo(input_rows, input_factor, mode_freq, mode_damping, line_freq, copies):
    devices = math.prod(FAST_SHAPE)
    chips = devices // 2
    rows, modes = input_rows.shape
    width = input_factor.shape[1]
    lines = line_freq.shape[0]
    parts = modes // (chips * width)
    ones = call(ones_kernel, "ones", [((8, width), F32)], flops=LONG)
    sent, gains = call(
        pack_kernel,
        "pack",
        [((chips, (2 * parts + 1) * rows, width), BF16), ((parts * 2 * lines, width), F32)],
        ones,
        line_freq.reshape(1, lines),
        mode_freq.reshape(-1, width),
        mode_damping.reshape(-1, width),
        input_rows,
        input_factor,
        flops=0,
    )
    cores = [[2 * chip + core for chip in range(chips)] for core in range(2)]
    got = lax.all_to_all(sent, AXES, 0, 0, axis_index_groups=cores)
    own, other = call(
        partial_kernel,
        "partial",
        [((parts, width, width), F32)] * 2,
        got,
        flops=LONG,
    )
    other = lax.ppermute(other, AXES, [(i, i ^ 1) for i in range(devices)])
    return call(
        functools.partial(pseudo_kernel, lines=lines),
        "pseudo",
        [((copies, parts * width, width), BF16)],
        gains,
        own,
        other,
        flops=LONG,
    )


def local(
    shape,
    mode_rows,
    input_rows,
    input_factor,
    mode_freq,
    mode_damping,
    line_freq,
    boundary_rows,
    connectivity,
    stress_coef,
):
    devices = math.prod(shape)
    rows, modes = mode_rows.shape
    width = input_factor.shape[1]
    lines = line_freq.shape[0]
    exports = boundary_rows.shape[0]
    rim = exports // 2
    elems = connectivity.shape[1]
    inputs = (input_rows, input_factor, mode_freq, mode_damping, line_freq)
    if shape == FAST_SHAPE and modes == devices * LANES and input_rows.shape[0] % 16 == 0:
        groups = [[h * 16 + j * 2 + c for j in range(8)] for h in range(2) for c in range(2)]
        got = lax.all_to_all(own_pseudo(*inputs, copies=8), AXES, 0, 0, axis_index_groups=groups)
        mine = got.reshape(modes // 2, width)
        theirs = lax.ppermute(mine, AXES, [(i, i ^ 1) for i in range(devices)])
    else:
        pseudo = pseudo_by_sum(*inputs).reshape(2, modes // 2, width)
        core = lax.axis_index(AXES) % 2
        mine = lax.dynamic_index_in_dim(pseudo, core, 0, keepdims=False)
        theirs = lax.dynamic_index_in_dim(pseudo, 1 - core, 0, keepdims=False)
    total, part, picked = call(
        first_kernel,
        "first",
        [((rows, width), F32), ((exports, width), F32), ((exports, modes // 2), BF16)],
        boundary_rows.reshape(1, exports),
        mode_rows,
        mine,
        flops=rows * modes * (width + exports),
    )
    far, near = call(
        export_kernel,
        "export",
        [((rim, width), BF16)] * 2,
        part,
        picked,
        theirs,
        flops=exports * modes * width,
    )
    inner = [(i, i ^ 1) for i in range(devices)]
    outer = [(i, i + 1) for i in range(1, devices - 1, 2)]
    outer += [(j, i) for i, j in outer]
    near = lax.ppermute(near, AXES, inner)
    far = lax.ppermute(far, AXES, outer)
    stress, matrix = call(
        own_kernel,
        "own",
        [((width, elems), F32), ((2 * exports, elems), BF16)],
        connectivity,
        stress_coef,
        mode_rows,
        theirs,
        total,
        flops=rows * modes * width + 4 * rows * elems * width,
        scratch=[pltpu.VMEM((2, rows, elems), BF16)],
    )
    return call(
        power_kernel,
        "power",
        [((lines, elems), F32)],
        stress,
        far,
        near,
        matrix,
        flops=4 * exports * elems * width,
    )


def solution(mesh):
    shape = tuple(mesh.shape[axis] for axis in AXES)
    placed = (
        P(AXES, None),
        P(AXES, None),
        P(AXES, None),
        P(),
        P(),
        P(),
        P(AXES),
        P(None, AXES),
        P(None, AXES),
    )
    return jax.shard_map(
        functools.partial(local, shape),
        mesh=mesh,
        in_specs=placed,
        out_specs=P(None, AXES),
        check_vma=False,
    )
```

```python
import functools
import math

import jax
import jax.numpy as jnp
from jax import lax
from jax.experimental import pallas as pl
from jax.experimental.pallas import tpu as pltpu
from jax.sharding import PartitionSpec as P

AXES = ("region", "sub")
LANES = 128
F32 = jnp.float32
BF16 = jnp.bfloat16
VMEM_BYTES = 24 * 1024 * 1024
LONG = 8 * 1024**3
FAST_SHAPE = (8, 4)


def whole(*_):
    return pl.BlockSpec(memory_space=pltpu.VMEM)


def modal_gain(freq, damping, omega):
    detune = freq * freq - omega * omega
    damped = 2.0 * damping * freq * omega
    magnitude = detune * detune + damped * damped
    return detune / magnitude, -damped / magnitude


def slab_of(device):
    return device % 2 * 8 + device // 2 % 8


def ones_kernel(ones_ref):
    ones_ref[...] = jnp.ones_like(ones_ref)


def pack_kernel(ones_ref, rows_ref, factor_ref, sent_ref):
    devices, _, width = sent_ref.shape
    rows = rows_ref.shape[0]
    parts = sent_ref.shape[1] // rows - 1
    factor = factor_ref[...] * ones_ref[0:1, :].astype(BF16)
    for device in range(devices):
        for part in range(parts):
            here = (slab_of(device) * parts + part) * width
            sent_ref[device, part * rows : (part + 1) * rows, :] = rows_ref[:, here : here + width]
        sent_ref[device, parts * rows :, :] = factor


def pseudo_kernel(line_ref, freq_ref, damping_ref, got_ref, pseudo_ref, *, rows):
    devices, tall, width = got_ref.shape
    parts = tall // rows - 1
    lines = line_ref.shape[1]
    columns = width // lines
    half = columns // 2
    slab = slab_of(lax.axis_index(AXES))
    factor = got_ref[:, parts * rows :, :].reshape(devices * rows, width)
    shapes = [
        got_ref[:, part * rows : (part + 1) * rows, :].reshape(devices * rows, width)
        for part in range(parts)
    ]
    forced = lax.dot_general(
        factor,
        jnp.concatenate(shapes, axis=1),
        (((0,), (0,)), ((), ())),
        preferred_element_type=F32,
    )
    for part in range(parts):
        here = pl.ds(slab * parts + part, 1)
        summed = forced[:, part * width : (part + 1) * width]
        pieces = []
        for line in range(lines):
            gain_real, gain_imag = modal_gain(
                freq_ref[here, :], damping_ref[here, :], line_ref[:, line : line + 1]
            )
            real = summed[line * columns : line * columns + half]
            imag = summed[line * columns + half : (line + 1) * columns]
            pieces.append(gain_real * real - gain_imag * imag)
            pieces.append(gain_real * imag + gain_imag * real)
        pseudo = jnp.concatenate(pieces, axis=0).T.astype(BF16)
        for copy in range(pseudo_ref.shape[0]):
            pseudo_ref[copy, part * width : (part + 1) * width, :] = pseudo


def first_kernel(boundary_ref, modes_ref, pseudo_ref, total_ref, part_ref, picked_ref):
    rows = modes_ref.shape[0]
    depth = pseudo_ref.shape[0]
    odd = lax.axis_index(AXES) % 2
    mine = pl.ds(pl.multiple_of(odd * depth, depth), depth)
    other = pl.ds(pl.multiple_of((1 - odd) * depth, depth), depth)
    total = jnp.dot(modes_ref[:, mine], pseudo_ref[...], preferred_element_type=F32)
    total_ref[...] = total
    exports = boundary_ref.shape[1]
    chosen = jnp.broadcast_to(boundary_ref[...], (exports, exports)).astype(F32).T
    column = lax.broadcasted_iota(jnp.int32, (exports, exports), 1).astype(F32)
    pick = jnp.concatenate(
        [(column + start == chosen).astype(F32) for start in range(0, rows, exports)], axis=1
    ).astype(BF16)
    high = total.astype(BF16)
    rest = total - high.astype(F32)
    middle = rest.astype(BF16)
    low = (rest - middle.astype(F32)).astype(BF16)
    parts = jnp.dot(
        pick, jnp.concatenate([high, middle, low], axis=1), preferred_element_type=F32
    )
    width = total.shape[1]
    part_ref[...] = parts[:, :width] + parts[:, width : 2 * width] + parts[:, 2 * width :]
    picked_ref[...] = jnp.dot(
        pick, modes_ref[:, other], preferred_element_type=F32
    ).astype(BF16)


def export_kernel(part_ref, picked_ref, pseudo_ref, far_ref, near_ref):
    export = part_ref[...] + jnp.dot(
        picked_ref[...], pseudo_ref[...], preferred_element_type=F32
    )
    export = export.astype(BF16)
    odd = lax.axis_index(AXES) % 2 == 1
    rim = far_ref.shape[0]
    far_ref[...] = jnp.where(odd, export[rim:], export[:rim])
    near_ref[...] = jnp.where(odd, export[:rim], export[rim:])


def own_kernel(
    connect_ref, coef_ref, modes_ref, pseudo_ref, total_ref, stress_ref, rim_ref, own_ref
):
    depth = pseudo_ref.shape[0]
    rows = modes_ref.shape[0]
    elems = connect_ref.shape[1]
    rim = rim_ref.shape[0] // 4
    odd = lax.axis_index(AXES) % 2

    def matrix(start, tall):
        node = lax.broadcasted_iota(jnp.int32, (tall, elems), 0) + start
        total = jnp.zeros((tall, elems), F32)
        for corner in range(connect_ref.shape[0]):
            hit = node == connect_ref[corner : corner + 1, :]
            total = total + jnp.where(hit, coef_ref[corner : corner + 1, :], 0.0)
        high = total.astype(BF16)
        return high, (total - high.astype(F32)).astype(BF16)

    after = rim + rows
    for place, start in ((0, after * odd), (1, after * (1 - odd))):
        high, low = matrix(start, rim)
        rim_ref[place * rim : (place + 1) * rim, :] = high
        rim_ref[(place + 2) * rim : (place + 3) * rim, :] = low
    for start in range(0, rows, rim):
        here = slice(start, start + rim)
        own_ref[0, here, :], own_ref[1, here, :] = matrix(start + rim, rim)
    other = pl.ds(pl.multiple_of((1 - odd) * depth, depth), depth)
    total = total_ref[...] + jnp.dot(
        modes_ref[:, other], pseudo_ref[...], preferred_element_type=F32
    )
    table = total.T.astype(BF16)
    stress = jnp.dot(table, own_ref[0], preferred_element_type=F32)
    stress_ref[...] = stress + jnp.dot(table, own_ref[1], preferred_element_type=F32)


def power_kernel(stress_ref, far_ref, near_ref, rim_ref, power_ref):
    rows = [far_ref[...], near_ref[...]]
    stress = stress_ref[...] + lax.dot_general(
        jnp.concatenate(rows + rows, axis=0),
        rim_ref[...],
        (((0,), (0,)), ((), ())),
        preferred_element_type=F32,
    )
    squares = stress * stress
    lines = power_ref.shape[0]
    columns = squares.shape[0] // lines
    for line in range(lines):
        power_ref[line : line + 1, :] = (
            jnp.sum(squares[line * columns : (line + 1) * columns], axis=0, keepdims=True)
            / columns
        )


def call(kernel, name, out, *operands, flops, scratch=()):
    shapes = [jax.ShapeDtypeStruct(shape, dtype) for shape, dtype in out]
    moved = sum(x.size * x.dtype.itemsize for x in operands)
    moved += sum(math.prod(shape) * jnp.dtype(dtype).itemsize for shape, dtype in out)
    result = pl.pallas_call(
        kernel,
        out_shape=shapes,
        in_specs=[whole()] * len(operands),
        out_specs=[whole()] * len(out),
        scratch_shapes=scratch,
        compiler_params=pltpu.CompilerParams(vmem_limit_bytes=VMEM_BYTES),
        cost_estimate=pl.CostEstimate(flops=flops, bytes_accessed=moved, transcendentals=0),
        name=name,
    )(*operands)
    return result if len(out) > 1 else result[0]


def pseudo_by_sum(input_rows, input_factor, mode_freq, mode_damping, line_freq):
    lines = line_freq.shape[0]
    columns = input_factor.shape[1] // lines
    half = columns // 2
    forced = lax.psum(
        lax.dot_general(
            input_rows, input_factor, (((0,), (0,)), ((), ())), preferred_element_type=F32
        ),
        AXES,
    )
    pieces = []
    for line in range(lines):
        gain_real, gain_imag = modal_gain(mode_freq, mode_damping, line_freq[line])
        gain_real, gain_imag = gain_real[:, None], gain_imag[:, None]
        real = forced[:, line * columns : line * columns + half]
        imag = forced[:, line * columns + half : (line + 1) * columns]
        pieces.append(gain_real * real - gain_imag * imag)
        pieces.append(gain_real * imag + gain_imag * real)
    return jnp.concatenate(pieces, axis=1).astype(BF16)


def own_pseudo(input_rows, input_factor, mode_freq, mode_damping, line_freq, copies):
    devices = math.prod(FAST_SHAPE)
    rows, modes = input_rows.shape
    width = input_factor.shape[1]
    lines = line_freq.shape[0]
    parts = modes // (devices // 2 * width)
    ones = call(ones_kernel, "ones", [((8, width), F32)], flops=LONG)
    sent = call(
        pack_kernel,
        "pack",
        [((devices, (parts + 1) * rows, width), BF16)],
        ones,
        input_rows,
        input_factor,
        flops=LONG,
    )
    got = lax.all_to_all(sent, AXES, 0, 0)
    return call(
        functools.partial(pseudo_kernel, rows=rows),
        "pseudo",
        [((copies, parts * width, width), BF16)],
        line_freq.reshape(1, lines),
        mode_freq.reshape(-1, width),
        mode_damping.reshape(-1, width),
        got,
        flops=LONG,
    )


def local(
    shape,
    mode_rows,
    input_rows,
    input_factor,
    mode_freq,
    mode_damping,
    line_freq,
    boundary_rows,
    connectivity,
    stress_coef,
):
    devices = math.prod(shape)
    rows, modes = mode_rows.shape
    width = input_factor.shape[1]
    lines = line_freq.shape[0]
    exports = boundary_rows.shape[0]
    rim = exports // 2
    elems = connectivity.shape[1]
    inputs = (input_rows, input_factor, mode_freq, mode_damping, line_freq)
    if shape == FAST_SHAPE and modes == devices * LANES and input_rows.shape[0] % 16 == 0:
        groups = [[h * 16 + j * 2 + c for j in range(8)] for h in range(2) for c in range(2)]
        got = lax.all_to_all(own_pseudo(*inputs, copies=8), AXES, 0, 0, axis_index_groups=groups)
        mine = got.reshape(modes // 2, width)
        theirs = lax.ppermute(mine, AXES, [(i, i ^ 1) for i in range(devices)])
    else:
        pseudo = pseudo_by_sum(*inputs).reshape(2, modes // 2, width)
        core = lax.axis_index(AXES) % 2
        mine = lax.dynamic_index_in_dim(pseudo, core, 0, keepdims=False)
        theirs = lax.dynamic_index_in_dim(pseudo, 1 - core, 0, keepdims=False)
    total, part, picked = call(
        first_kernel,
        "first",
        [((rows, width), F32), ((exports, width), F32), ((exports, modes // 2), BF16)],
        boundary_rows.reshape(1, exports),
        mode_rows,
        mine,
        flops=rows * modes * (width + exports),
    )
    far, near = call(
        export_kernel,
        "export",
        [((rim, width), BF16)] * 2,
        part,
        picked,
        theirs,
        flops=exports * modes * width,
    )
    inner = [(i, i ^ 1) for i in range(devices)]
    outer = [(i, i + 1) for i in range(1, devices - 1, 2)]
    outer += [(j, i) for i, j in outer]
    near = lax.ppermute(near, AXES, inner)
    far = lax.ppermute(far, AXES, outer)
    stress, matrix = call(
        own_kernel,
        "own",
        [((width, elems), F32), ((2 * exports, elems), BF16)],
        connectivity,
        stress_coef,
        mode_rows,
        theirs,
        total,
        flops=rows * modes * width + 4 * rows * elems * width,
        scratch=[pltpu.VMEM((2, rows, elems), BF16)],
    )
    return call(
        power_kernel,
        "power",
        [((lines, elems), F32)],
        stress,
        far,
        near,
        matrix,
        flops=4 * exports * elems * width,
    )


def solution(mesh):
    shape = tuple(mesh.shape[axis] for axis in AXES)
    placed = (
        P(AXES, None),
        P(AXES, None),
        P(AXES, None),
        P(),
        P(),
        P(),
        P(AXES),
        P(None, AXES),
        P(None, AXES),
    )
    return jax.shard_map(
        functools.partial(local, shape),
        mesh=mesh,
        in_specs=placed,
        out_specs=P(None, AXES),
        check_vma=False,
    )
```

```python
import functools
import math

import jax
import jax.numpy as jnp
from jax import lax
from jax.experimental import pallas as pl
from jax.experimental.pallas import tpu as pltpu
from jax.sharding import PartitionSpec as P

AXES = ("region", "sub")
LANES = 128
F32 = jnp.float32
BF16 = jnp.bfloat16
VMEM_BYTES = 24 * 1024 * 1024
LONG = 8 * 1024**3
FAST_SHAPE = (8, 4)


def whole(*_):
    return pl.BlockSpec(memory_space=pltpu.VMEM)


def modal_gain(freq, damping, omega):
    detune = freq * freq - omega * omega
    damped = 2.0 * damping * freq * omega
    magnitude = detune * detune + damped * damped
    return detune / magnitude, -damped / magnitude


def slab_of(device):
    return device % 2 * 8 + device // 2 % 8


def ones_kernel(ones_ref):
    ones_ref[...] = jnp.ones_like(ones_ref)


def pack_kernel(ones_ref, rows_ref, factor_ref, sent_ref):
    devices, _, width = sent_ref.shape
    rows = rows_ref.shape[0]
    parts = sent_ref.shape[1] // rows - 1
    factor = factor_ref[...] * ones_ref[0:1, :].astype(BF16)
    for device in range(devices):
        for part in range(parts):
            here = (slab_of(device) * parts + part) * width
            sent_ref[device, part * rows : (part + 1) * rows, :] = rows_ref[:, here : here + width]
        sent_ref[device, parts * rows :, :] = factor


def pseudo_kernel(line_ref, freq_ref, damping_ref, got_ref, pseudo_ref, *, rows):
    devices, tall, width = got_ref.shape
    parts = tall // rows - 1
    lines = line_ref.shape[1]
    columns = width // lines
    half = columns // 2
    slab = slab_of(lax.axis_index(AXES))
    factor = got_ref[:, parts * rows :, :].reshape(devices * rows, width)
    shapes = [
        got_ref[:, part * rows : (part + 1) * rows, :].reshape(devices * rows, width)
        for part in range(parts)
    ]
    forced = lax.dot_general(
        factor,
        jnp.concatenate(shapes, axis=1),
        (((0,), (0,)), ((), ())),
        preferred_element_type=F32,
    )
    for part in range(parts):
        here = pl.ds(slab * parts + part, 1)
        summed = forced[:, part * width : (part + 1) * width]
        pieces = []
        for line in range(lines):
            gain_real, gain_imag = modal_gain(
                freq_ref[here, :], damping_ref[here, :], line_ref[:, line : line + 1]
            )
            real = summed[line * columns : line * columns + half]
            imag = summed[line * columns + half : (line + 1) * columns]
            pieces.append(gain_real * real - gain_imag * imag)
            pieces.append(gain_real * imag + gain_imag * real)
        pseudo = jnp.concatenate(pieces, axis=0).T.astype(BF16)
        for copy in range(pseudo_ref.shape[0]):
            pseudo_ref[copy, part * width : (part + 1) * width, :] = pseudo


def first_kernel(
    boundary_ref, modes_ref, pseudo_ref, total_ref, pick_ref, part_ref, picked_ref
):
    rows = modes_ref.shape[0]
    depth = pseudo_ref.shape[0]
    odd = lax.axis_index(AXES) % 2
    mine = pl.ds(pl.multiple_of(odd * depth, depth), depth)
    total_ref[...] = jnp.dot(modes_ref[:, mine], pseudo_ref[...], preferred_element_type=F32)
    exports = boundary_ref.shape[1]
    chosen = jnp.broadcast_to(boundary_ref[...], (exports, exports)).astype(F32).T
    column = lax.broadcasted_iota(jnp.int32, (exports, exports), 1).astype(F32)
    pick_ref[...] = jnp.concatenate(
        [(column + start == chosen).astype(F32) for start in range(0, rows, exports)], axis=1
    ).astype(BF16)

    @pl.when(odd == 0)
    def _():
        pick = pick_ref[...]
        total = total_ref[...]
        high = total.astype(BF16)
        rest = total - high.astype(F32)
        middle = rest.astype(BF16)
        low = (rest - middle.astype(F32)).astype(BF16)
        parts = jnp.dot(
            pick, jnp.concatenate([high, middle, low], axis=1), preferred_element_type=F32
        )
        width = total.shape[1]
        part_ref[...] = parts[:, :width] + parts[:, width : 2 * width] + parts[:, 2 * width :]
        picked_ref[...] = jnp.dot(
            pick, modes_ref[:, depth:], preferred_element_type=F32
        ).astype(BF16)


def export_kernel(
    pick_ref, part_ref, picked_ref, modes_ref, total_ref, pseudo_ref, far_ref, near_ref, full_ref
):
    depth = pseudo_ref.shape[0]
    odd = lax.axis_index(AXES) % 2
    rim = far_ref.shape[0]

    @pl.when(odd == 0)
    def _():
        export = part_ref[...] + jnp.dot(
            picked_ref[...], pseudo_ref[...], preferred_element_type=F32
        )
        export = export.astype(BF16)
        far_ref[...] = export[:rim]
        near_ref[...] = export[rim:]

    @pl.when(odd == 1)
    def _():
        full = total_ref[...] + jnp.dot(
            modes_ref[:, :depth], pseudo_ref[...], preferred_element_type=F32
        )
        full_ref[...] = full
        export = jnp.dot(
            pick_ref[...], full.astype(BF16), preferred_element_type=F32
        ).astype(BF16)
        far_ref[...] = export[rim:]
        near_ref[...] = export[:rim]


def own_kernel(
    connect_ref, coef_ref, modes_ref, pseudo_ref, total_ref, full_ref, stress_ref, rim_ref, own_ref, table_ref
):
    depth = pseudo_ref.shape[0]
    rows = modes_ref.shape[0]
    elems = connect_ref.shape[1]
    rim = rim_ref.shape[0] // 4
    odd = lax.axis_index(AXES) % 2

    @pl.when(odd == 0)
    def _():
        total = total_ref[...] + jnp.dot(
            modes_ref[:, depth:], pseudo_ref[...], preferred_element_type=F32
        )
        table_ref[...] = total.T.astype(BF16)

    @pl.when(odd == 1)
    def _():
        table_ref[...] = full_ref[...].T.astype(BF16)

    def matrix(start, tall):
        node = lax.broadcasted_iota(jnp.int32, (tall, elems), 0) + start
        total = jnp.zeros((tall, elems), F32)
        for corner in range(connect_ref.shape[0]):
            hit = node == connect_ref[corner : corner + 1, :]
            total = total + jnp.where(hit, coef_ref[corner : corner + 1, :], 0.0)
        high = total.astype(BF16)
        return high, (total - high.astype(F32)).astype(BF16)

    after = rim + rows
    for place, start in ((0, after * odd), (1, after * (1 - odd))):
        high, low = matrix(start, rim)
        rim_ref[place * rim : (place + 1) * rim, :] = high
        rim_ref[(place + 2) * rim : (place + 3) * rim, :] = low
    for start in range(0, rows, rim):
        here = slice(start, start + rim)
        own_ref[0, here, :], own_ref[1, here, :] = matrix(start + rim, rim)
    table = table_ref[...]
    stress = jnp.dot(table, own_ref[0], preferred_element_type=F32)
    stress_ref[...] = stress + jnp.dot(table, own_ref[1], preferred_element_type=F32)


def power_kernel(stress_ref, far_ref, near_ref, rim_ref, power_ref):
    rows = [far_ref[...], near_ref[...]]
    stress = stress_ref[...] + lax.dot_general(
        jnp.concatenate(rows + rows, axis=0),
        rim_ref[...],
        (((0,), (0,)), ((), ())),
        preferred_element_type=F32,
    )
    squares = stress * stress
    lines = power_ref.shape[0]
    columns = squares.shape[0] // lines
    for line in range(lines):
        power_ref[line : line + 1, :] = (
            jnp.sum(squares[line * columns : (line + 1) * columns], axis=0, keepdims=True)
            / columns
        )


def call(kernel, name, out, *operands, flops, scratch=()):
    shapes = [jax.ShapeDtypeStruct(shape, dtype) for shape, dtype in out]
    moved = sum(x.size * x.dtype.itemsize for x in operands)
    moved += sum(math.prod(shape) * jnp.dtype(dtype).itemsize for shape, dtype in out)
    result = pl.pallas_call(
        kernel,
        out_shape=shapes,
        in_specs=[whole()] * len(operands),
        out_specs=[whole()] * len(out),
        scratch_shapes=scratch,
        compiler_params=pltpu.CompilerParams(vmem_limit_bytes=VMEM_BYTES),
        cost_estimate=pl.CostEstimate(flops=flops, bytes_accessed=moved, transcendentals=0),
        name=name,
    )(*operands)
    return result if len(out) > 1 else result[0]


def pseudo_by_sum(input_rows, input_factor, mode_freq, mode_damping, line_freq):
    lines = line_freq.shape[0]
    columns = input_factor.shape[1] // lines
    half = columns // 2
    forced = lax.psum(
        lax.dot_general(
            input_rows, input_factor, (((0,), (0,)), ((), ())), preferred_element_type=F32
        ),
        AXES,
    )
    pieces = []
    for line in range(lines):
        gain_real, gain_imag = modal_gain(mode_freq, mode_damping, line_freq[line])
        gain_real, gain_imag = gain_real[:, None], gain_imag[:, None]
        real = forced[:, line * columns : line * columns + half]
        imag = forced[:, line * columns + half : (line + 1) * columns]
        pieces.append(gain_real * real - gain_imag * imag)
        pieces.append(gain_real * imag + gain_imag * real)
    return jnp.concatenate(pieces, axis=1).astype(BF16)


def own_pseudo(input_rows, input_factor, mode_freq, mode_damping, line_freq, copies):
    devices = math.prod(FAST_SHAPE)
    rows, modes = input_rows.shape
    width = input_factor.shape[1]
    lines = line_freq.shape[0]
    parts = modes // (devices // 2 * width)
    ones = call(ones_kernel, "ones", [((8, width), F32)], flops=LONG)
    sent = call(
        pack_kernel,
        "pack",
        [((devices, (parts + 1) * rows, width), BF16)],
        ones,
        input_rows,
        input_factor,
        flops=LONG,
    )
    got = lax.all_to_all(sent, AXES, 0, 0)
    return call(
        functools.partial(pseudo_kernel, rows=rows),
        "pseudo",
        [((copies, parts * width, width), BF16)],
        line_freq.reshape(1, lines),
        mode_freq.reshape(-1, width),
        mode_damping.reshape(-1, width),
        got,
        flops=LONG,
    )


def local(
    shape,
    mode_rows,
    input_rows,
    input_factor,
    mode_freq,
    mode_damping,
    line_freq,
    boundary_rows,
    connectivity,
    stress_coef,
):
    devices = math.prod(shape)
    rows, modes = mode_rows.shape
    width = input_factor.shape[1]
    lines = line_freq.shape[0]
    exports = boundary_rows.shape[0]
    rim = exports // 2
    elems = connectivity.shape[1]
    inputs = (input_rows, input_factor, mode_freq, mode_damping, line_freq)
    if shape == FAST_SHAPE and modes == devices * LANES and input_rows.shape[0] % 16 == 0:
        groups = [[h * 16 + j * 2 + c for j in range(8)] for h in range(2) for c in range(2)]
        got = lax.all_to_all(own_pseudo(*inputs, copies=8), AXES, 0, 0, axis_index_groups=groups)
        mine = got.reshape(modes // 2, width)
        theirs = lax.ppermute(mine, AXES, [(i, i ^ 1) for i in range(devices)])
    else:
        pseudo = pseudo_by_sum(*inputs).reshape(2, modes // 2, width)
        core = lax.axis_index(AXES) % 2
        mine = lax.dynamic_index_in_dim(pseudo, core, 0, keepdims=False)
        theirs = lax.dynamic_index_in_dim(pseudo, 1 - core, 0, keepdims=False)
    total, pick, part, picked = call(
        first_kernel,
        "first",
        [
            ((rows, width), F32),
            ((exports, rows), BF16),
            ((exports, width), F32),
            ((exports, modes // 2), BF16),
        ],
        boundary_rows.reshape(1, exports),
        mode_rows,
        mine,
        flops=rows * modes * (width + exports),
    )
    far, near, full = call(
        export_kernel,
        "export",
        [((rim, width), BF16)] * 2 + [((rows, width), F32)],
        pick,
        part,
        picked,
        mode_rows,
        total,
        theirs,
        flops=rows * modes * width,
    )
    inner = [(i, i ^ 1) for i in range(devices)]
    outer = [(i, i + 1) for i in range(1, devices - 1, 2)]
    outer += [(j, i) for i, j in outer]
    near = lax.ppermute(near, AXES, inner)
    far = lax.ppermute(far, AXES, outer)
    stress, matrix = call(
        own_kernel,
        "own",
        [((width, elems), F32), ((2 * exports, elems), BF16)],
        connectivity,
        stress_coef,
        mode_rows,
        theirs,
        total,
        full,
        flops=rows * modes * width + 4 * rows * elems * width,
        scratch=[pltpu.VMEM((2, rows, elems), BF16), pltpu.VMEM((width, rows), BF16)],
    )
    return call(
        power_kernel,
        "power",
        [((lines, elems), F32)],
        stress,
        far,
        near,
        matrix,
        flops=4 * exports * elems * width,
    )


def solution(mesh):
    shape = tuple(mesh.shape[axis] for axis in AXES)
    placed = (
        P(AXES, None),
        P(AXES, None),
        P(AXES, None),
        P(),
        P(),
        P(),
        P(AXES),
        P(None, AXES),
        P(None, AXES),
    )
    return jax.shard_map(
        functools.partial(local, shape),
        mesh=mesh,
        in_specs=placed,
        out_specs=P(None, AXES),
        check_vma=False,
    )
```

```python
import functools
import math

import jax
import jax.numpy as jnp
from jax import lax
from jax.experimental import pallas as pl
from jax.experimental.pallas import tpu as pltpu
from jax.sharding import PartitionSpec as P

AXES = ("region", "sub")
LANES = 128
F32 = jnp.float32
BF16 = jnp.bfloat16
VMEM_BYTES = 24 * 1024 * 1024
LONG = 8 * 1024**3
FAST_SHAPE = (8, 4)


def whole(*_):
    return pl.BlockSpec(memory_space=pltpu.VMEM)


def modal_gain(freq, damping, omega):
    detune = freq * freq - omega * omega
    damped = 2.0 * damping * freq * omega
    magnitude = detune * detune + damped * damped
    return detune / magnitude, -damped / magnitude


def slab_of(device):
    return device % 2 * 8 + device // 2 % 8


def ones_kernel(ones_ref):
    ones_ref[...] = jnp.ones_like(ones_ref)


def pack_kernel(ones_ref, rows_ref, factor_ref, sent_ref):
    devices, _, width = sent_ref.shape
    rows = rows_ref.shape[0]
    parts = sent_ref.shape[1] // rows - 1
    factor = factor_ref[...] * ones_ref[0:1, :].astype(BF16)
    for device in range(devices):
        for part in range(parts):
            here = (slab_of(device) * parts + part) * width
            sent_ref[device, part * rows : (part + 1) * rows, :] = rows_ref[:, here : here + width]
        sent_ref[device, parts * rows :, :] = factor


def pseudo_kernel(line_ref, freq_ref, damping_ref, got_ref, pseudo_ref, *, rows):
    devices, tall, width = got_ref.shape
    parts = tall // rows - 1
    lines = line_ref.shape[1]
    columns = width // lines
    half = columns // 2
    slab = slab_of(lax.axis_index(AXES))
    factor = got_ref[:, parts * rows :, :].reshape(devices * rows, width)
    shapes = [
        got_ref[:, part * rows : (part + 1) * rows, :].reshape(devices * rows, width)
        for part in range(parts)
    ]
    forced = lax.dot_general(
        factor,
        jnp.concatenate(shapes, axis=1),
        (((0,), (0,)), ((), ())),
        preferred_element_type=F32,
    )
    for part in range(parts):
        here = pl.ds(slab * parts + part, 1)
        summed = forced[:, part * width : (part + 1) * width]
        pieces = []
        for line in range(lines):
            gain_real, gain_imag = modal_gain(
                freq_ref[here, :], damping_ref[here, :], line_ref[:, line : line + 1]
            )
            real = summed[line * columns : line * columns + half]
            imag = summed[line * columns + half : (line + 1) * columns]
            pieces.append(gain_real * real - gain_imag * imag)
            pieces.append(gain_real * imag + gain_imag * real)
        pseudo = jnp.concatenate(pieces, axis=0).T.astype(BF16)
        for copy in range(pseudo_ref.shape[0]):
            pseudo_ref[copy, part * width : (part + 1) * width, :] = pseudo


def for_core(depth, work):
    odd = lax.axis_index(AXES) % 2
    low, high = slice(0, depth), slice(depth, 2 * depth)
    pl.when(odd == 0)(lambda: work(low, high))
    pl.when(odd == 1)(lambda: work(high, low))


def first_kernel(boundary_ref, modes_ref, pseudo_ref, total_ref, part_ref, picked_ref, pick_ref):
    rows = modes_ref.shape[0]
    exports = boundary_ref.shape[1]
    chosen = jnp.broadcast_to(boundary_ref[...], (exports, exports)).astype(F32).T
    column = lax.broadcasted_iota(jnp.int32, (exports, exports), 1).astype(F32)
    pick_ref[...] = jnp.concatenate(
        [(column + start == chosen).astype(F32) for start in range(0, rows, exports)], axis=1
    ).astype(BF16)

    def product(mine, _):
        total_ref[...] = jnp.dot(modes_ref[:, mine], pseudo_ref[...], preferred_element_type=F32)

    def exported(_, other):
        pick = pick_ref[...]
        total = total_ref[...]
        high = total.astype(BF16)
        rest = total - high.astype(F32)
        middle = rest.astype(BF16)
        low = (rest - middle.astype(F32)).astype(BF16)
        parts = jnp.dot(
            pick, jnp.concatenate([high, middle, low], axis=1), preferred_element_type=F32
        )
        width = total.shape[1]
        part_ref[...] = parts[:, :width] + parts[:, width : 2 * width] + parts[:, 2 * width :]
        picked_ref[...] = jnp.dot(
            pick, modes_ref[:, other], preferred_element_type=F32
        ).astype(BF16)

    for_core(pseudo_ref.shape[0], product)
    for_core(pseudo_ref.shape[0], exported)


def export_kernel(part_ref, picked_ref, pseudo_ref, far_ref, near_ref):
    export = part_ref[...] + jnp.dot(
        picked_ref[...], pseudo_ref[...], preferred_element_type=F32
    )
    export = export.astype(BF16)
    odd = lax.axis_index(AXES) % 2 == 1
    rim = far_ref.shape[0]
    far_ref[...] = jnp.where(odd, export[rim:], export[:rim])
    near_ref[...] = jnp.where(odd, export[:rim], export[rim:])


def own_kernel(
    connect_ref, coef_ref, modes_ref, pseudo_ref, total_ref, stress_ref, rim_ref, own_ref, table_ref
):
    rows = modes_ref.shape[0]
    elems = connect_ref.shape[1]
    rim = rim_ref.shape[0] // 4
    odd = lax.axis_index(AXES) % 2

    def responses(_, other):
        total = total_ref[...] + jnp.dot(
            modes_ref[:, other], pseudo_ref[...], preferred_element_type=F32
        )
        table_ref[...] = total.T.astype(BF16)

    for_core(pseudo_ref.shape[0], responses)

    def matrix(start, tall):
        node = lax.broadcasted_iota(jnp.int32, (tall, elems), 0) + start
        total = jnp.zeros((tall, elems), F32)
        for corner in range(connect_ref.shape[0]):
            hit = node == connect_ref[corner : corner + 1, :]
            total = total + jnp.where(hit, coef_ref[corner : corner + 1, :], 0.0)
        high = total.astype(BF16)
        return high, (total - high.astype(F32)).astype(BF16)

    after = rim + rows
    for place, start in ((0, after * odd), (1, after * (1 - odd))):
        high, low = matrix(start, rim)
        rim_ref[place * rim : (place + 1) * rim, :] = high
        rim_ref[(place + 2) * rim : (place + 3) * rim, :] = low
    for start in range(0, rows, rim):
        here = slice(start, start + rim)
        own_ref[0, here, :], own_ref[1, here, :] = matrix(start + rim, rim)
    table = table_ref[...]
    stress = jnp.dot(table, own_ref[0], preferred_element_type=F32)
    stress_ref[...] = stress + jnp.dot(table, own_ref[1], preferred_element_type=F32)


def power_kernel(stress_ref, far_ref, near_ref, rim_ref, power_ref):
    rows = [far_ref[...], near_ref[...]]
    stress = stress_ref[...] + lax.dot_general(
        jnp.concatenate(rows + rows, axis=0),
        rim_ref[...],
        (((0,), (0,)), ((), ())),
        preferred_element_type=F32,
    )
    squares = stress * stress
    lines = power_ref.shape[0]
    columns = squares.shape[0] // lines
    for line in range(lines):
        power_ref[line : line + 1, :] = (
            jnp.sum(squares[line * columns : (line + 1) * columns], axis=0, keepdims=True)
            / columns
        )


def call(kernel, name, out, *operands, flops, scratch=()):
    shapes = [jax.ShapeDtypeStruct(shape, dtype) for shape, dtype in out]
    moved = sum(x.size * x.dtype.itemsize for x in operands)
    moved += sum(math.prod(shape) * jnp.dtype(dtype).itemsize for shape, dtype in out)
    result = pl.pallas_call(
        kernel,
        out_shape=shapes,
        in_specs=[whole()] * len(operands),
        out_specs=[whole()] * len(out),
        scratch_shapes=scratch,
        compiler_params=pltpu.CompilerParams(vmem_limit_bytes=VMEM_BYTES),
        cost_estimate=pl.CostEstimate(flops=flops, bytes_accessed=moved, transcendentals=0),
        name=name,
    )(*operands)
    return result if len(out) > 1 else result[0]


def pseudo_by_sum(input_rows, input_factor, mode_freq, mode_damping, line_freq):
    lines = line_freq.shape[0]
    columns = input_factor.shape[1] // lines
    half = columns // 2
    forced = lax.psum(
        lax.dot_general(
            input_rows, input_factor, (((0,), (0,)), ((), ())), preferred_element_type=F32
        ),
        AXES,
    )
    pieces = []
    for line in range(lines):
        gain_real, gain_imag = modal_gain(mode_freq, mode_damping, line_freq[line])
        gain_real, gain_imag = gain_real[:, None], gain_imag[:, None]
        real = forced[:, line * columns : line * columns + half]
        imag = forced[:, line * columns + half : (line + 1) * columns]
        pieces.append(gain_real * real - gain_imag * imag)
        pieces.append(gain_real * imag + gain_imag * real)
    return jnp.concatenate(pieces, axis=1).astype(BF16)


def own_pseudo(input_rows, input_factor, mode_freq, mode_damping, line_freq, copies):
    devices = math.prod(FAST_SHAPE)
    rows, modes = input_rows.shape
    width = input_factor.shape[1]
    lines = line_freq.shape[0]
    parts = modes // (devices // 2 * width)
    ones = call(ones_kernel, "ones", [((8, width), F32)], flops=LONG)
    sent = call(
        pack_kernel,
        "pack",
        [((devices, (parts + 1) * rows, width), BF16)],
        ones,
        input_rows,
        input_factor,
        flops=LONG,
    )
    got = lax.all_to_all(sent, AXES, 0, 0)
    return call(
        functools.partial(pseudo_kernel, rows=rows),
        "pseudo",
        [((copies, parts * width, width), BF16)],
        line_freq.reshape(1, lines),
        mode_freq.reshape(-1, width),
        mode_damping.reshape(-1, width),
        got,
        flops=LONG,
    )


def local(
    shape,
    mode_rows,
    input_rows,
    input_factor,
    mode_freq,
    mode_damping,
    line_freq,
    boundary_rows,
    connectivity,
    stress_coef,
):
    devices = math.prod(shape)
    rows, modes = mode_rows.shape
    width = input_factor.shape[1]
    lines = line_freq.shape[0]
    exports = boundary_rows.shape[0]
    rim = exports // 2
    elems = connectivity.shape[1]
    inputs = (input_rows, input_factor, mode_freq, mode_damping, line_freq)
    if shape == FAST_SHAPE and modes == devices * LANES and input_rows.shape[0] % 16 == 0:
        groups = [[h * 16 + j * 2 + c for j in range(8)] for h in range(2) for c in range(2)]
        got = lax.all_to_all(own_pseudo(*inputs, copies=8), AXES, 0, 0, axis_index_groups=groups)
        mine = got.reshape(modes // 2, width)
        theirs = lax.ppermute(mine, AXES, [(i, i ^ 1) for i in range(devices)])
    else:
        pseudo = pseudo_by_sum(*inputs).reshape(2, modes // 2, width)
        core = lax.axis_index(AXES) % 2
        mine = lax.dynamic_index_in_dim(pseudo, core, 0, keepdims=False)
        theirs = lax.dynamic_index_in_dim(pseudo, 1 - core, 0, keepdims=False)
    total, part, picked = call(
        first_kernel,
        "first",
        [((rows, width), F32), ((exports, width), F32), ((exports, modes // 2), BF16)],
        boundary_rows.reshape(1, exports),
        mode_rows,
        mine,
        flops=rows * modes * (width + exports),
        scratch=[pltpu.VMEM((exports, rows), BF16)],
    )
    far, near = call(
        export_kernel,
        "export",
        [((rim, width), BF16)] * 2,
        part,
        picked,
        theirs,
        flops=exports * modes * width,
    )
    inner = [(i, i ^ 1) for i in range(devices)]
    outer = [(i, i + 1) for i in range(1, devices - 1, 2)]
    outer += [(j, i) for i, j in outer]
    near = lax.ppermute(near, AXES, inner)
    far = lax.ppermute(far, AXES, outer)
    stress, matrix = call(
        own_kernel,
        "own",
        [((width, elems), F32), ((2 * exports, elems), BF16)],
        connectivity,
        stress_coef,
        mode_rows,
        theirs,
        total,
        flops=rows * modes * width + 4 * rows * elems * width,
        scratch=[pltpu.VMEM((2, rows, elems), BF16), pltpu.VMEM((width, rows), BF16)],
    )
    return call(
        power_kernel,
        "power",
        [((lines, elems), F32)],
        stress,
        far,
        near,
        matrix,
        flops=4 * exports * elems * width,
    )


def solution(mesh):
    shape = tuple(mesh.shape[axis] for axis in AXES)
    placed = (
        P(AXES, None),
        P(AXES, None),
        P(AXES, None),
        P(),
        P(),
        P(),
        P(AXES),
        P(None, AXES),
        P(None, AXES),
    )
    return jax.shard_map(
        functools.partial(local, shape),
        mesh=mesh,
        in_specs=placed,
        out_specs=P(None, AXES),
        check_vma=False,
    )
```

```python
import functools
import math

import jax
import jax.numpy as jnp
from jax import lax
from jax.experimental import pallas as pl
from jax.experimental.pallas import tpu as pltpu
from jax.sharding import PartitionSpec as P

AXES = ("region", "sub")
LANES = 128
F32 = jnp.float32
BF16 = jnp.bfloat16
VMEM_BYTES = 24 * 1024 * 1024
LONG = 8 * 1024**3
FAST_SHAPE = (8, 4)


def whole(*_):
    return pl.BlockSpec(memory_space=pltpu.VMEM)


def modal_gain(freq, damping, omega):
    detune = freq * freq - omega * omega
    damped = 2.0 * damping * freq * omega
    magnitude = detune * detune + damped * damped
    return detune / magnitude, -damped / magnitude


def slab_of(device):
    chip = device // 2 % 8
    return device % 2 * 8 + (chip ^ (chip // 2) ^ (chip // 4))


def ones_kernel(ones_ref):
    ones_ref[...] = jnp.ones_like(ones_ref)


def pack_kernel(ones_ref, rows_ref, factor_ref, sent_ref):
    devices, _, width = sent_ref.shape
    rows = rows_ref.shape[0]
    parts = sent_ref.shape[1] // rows - 1
    factor = factor_ref[...] * ones_ref[0:1, :].astype(BF16)
    for device in range(devices):
        for part in range(parts):
            here = (slab_of(device) * parts + part) * width
            sent_ref[device, part * rows : (part + 1) * rows, :] = rows_ref[:, here : here + width]
        sent_ref[device, parts * rows :, :] = factor


def pseudo_kernel(line_ref, freq_ref, damping_ref, got_ref, pseudo_ref, *, rows):
    devices, tall, width = got_ref.shape
    parts = tall // rows - 1
    lines = line_ref.shape[1]
    columns = width // lines
    half = columns // 2
    slab = slab_of(lax.axis_index(AXES))
    factor = got_ref[:, parts * rows :, :].reshape(devices * rows, width)
    shapes = [
        got_ref[:, part * rows : (part + 1) * rows, :].reshape(devices * rows, width)
        for part in range(parts)
    ]
    forced = lax.dot_general(
        factor,
        jnp.concatenate(shapes, axis=1),
        (((0,), (0,)), ((), ())),
        preferred_element_type=F32,
    )
    for part in range(parts):
        here = pl.ds(slab * parts + part, 1)
        summed = forced[:, part * width : (part + 1) * width]
        pieces = []
        for line in range(lines):
            gain_real, gain_imag = modal_gain(
                freq_ref[here, :], damping_ref[here, :], line_ref[:, line : line + 1]
            )
            real = summed[line * columns : line * columns + half]
            imag = summed[line * columns + half : (line + 1) * columns]
            pieces.append(gain_real * real - gain_imag * imag)
            pieces.append(gain_real * imag + gain_imag * real)
        pseudo = jnp.concatenate(pieces, axis=0).T.astype(BF16)
        for copy in range(pseudo_ref.shape[0]):
            pseudo_ref[copy, part * width : (part + 1) * width, :] = pseudo


def for_core(depth, work):
    odd = lax.axis_index(AXES) % 2
    low, high = slice(0, depth), slice(depth, 2 * depth)
    pl.when(odd == 0)(lambda: work(low, high))
    pl.when(odd == 1)(lambda: work(high, low))


def first_kernel(boundary_ref, modes_ref, pseudo_ref, total_ref, part_ref, picked_ref, pick_ref):
    rows = modes_ref.shape[0]
    exports = boundary_ref.shape[1]
    chosen = jnp.broadcast_to(boundary_ref[...], (exports, exports)).astype(F32).T
    column = lax.broadcasted_iota(jnp.int32, (exports, exports), 1).astype(F32)
    pick_ref[...] = jnp.concatenate(
        [(column + start == chosen).astype(F32) for start in range(0, rows, exports)], axis=1
    ).astype(BF16)

    def product(mine, _):
        total_ref[...] = jnp.dot(modes_ref[:, mine], pseudo_ref[...], preferred_element_type=F32)

    def exported(_, other):
        pick = pick_ref[...]
        total = total_ref[...]
        high = total.astype(BF16)
        rest = total - high.astype(F32)
        middle = rest.astype(BF16)
        low = (rest - middle.astype(F32)).astype(BF16)
        parts = jnp.dot(
            pick, jnp.concatenate([high, middle, low], axis=1), preferred_element_type=F32
        )
        width = total.shape[1]
        part_ref[...] = parts[:, :width] + parts[:, width : 2 * width] + parts[:, 2 * width :]
        picked_ref[...] = jnp.dot(
            pick, modes_ref[:, other], preferred_element_type=F32
        ).astype(BF16)

    for_core(pseudo_ref.shape[0], product)
    for_core(pseudo_ref.shape[0], exported)


def export_kernel(part_ref, picked_ref, pseudo_ref, far_ref, near_ref):
    export = part_ref[...] + jnp.dot(
        picked_ref[...], pseudo_ref[...], preferred_element_type=F32
    )
    export = export.astype(BF16)
    odd = lax.axis_index(AXES) % 2 == 1
    rim = far_ref.shape[0]
    far_ref[...] = jnp.where(odd, export[rim:], export[:rim])
    near_ref[...] = jnp.where(odd, export[:rim], export[rim:])


def own_kernel(
    connect_ref, coef_ref, modes_ref, pseudo_ref, total_ref, stress_ref, rim_ref, own_ref, table_ref
):
    rows = modes_ref.shape[0]
    elems = connect_ref.shape[1]
    rim = rim_ref.shape[0] // 4
    odd = lax.axis_index(AXES) % 2

    def responses(_, other):
        total = total_ref[...] + jnp.dot(
            modes_ref[:, other], pseudo_ref[...], preferred_element_type=F32
        )
        table_ref[...] = total.T.astype(BF16)

    for_core(pseudo_ref.shape[0], responses)

    def matrix(start, tall):
        node = lax.broadcasted_iota(jnp.int32, (tall, elems), 0) + start
        total = jnp.zeros((tall, elems), F32)
        for corner in range(connect_ref.shape[0]):
            hit = node == connect_ref[corner : corner + 1, :]
            total = total + jnp.where(hit, coef_ref[corner : corner + 1, :], 0.0)
        high = total.astype(BF16)
        return high, (total - high.astype(F32)).astype(BF16)

    after = rim + rows
    for place, start in ((0, after * odd), (1, after * (1 - odd))):
        high, low = matrix(start, rim)
        rim_ref[place * rim : (place + 1) * rim, :] = high
        rim_ref[(place + 2) * rim : (place + 3) * rim, :] = low
    for start in range(0, rows, rim):
        here = slice(start, start + rim)
        own_ref[0, here, :], own_ref[1, here, :] = matrix(start + rim, rim)
    table = table_ref[...]
    stress = jnp.dot(table, own_ref[0], preferred_element_type=F32)
    stress_ref[...] = stress + jnp.dot(table, own_ref[1], preferred_element_type=F32)


def power_kernel(stress_ref, far_ref, near_ref, rim_ref, power_ref):
    rows = [far_ref[...], near_ref[...]]
    stress = stress_ref[...] + lax.dot_general(
        jnp.concatenate(rows + rows, axis=0),
        rim_ref[...],
        (((0,), (0,)), ((), ())),
        preferred_element_type=F32,
    )
    squares = stress * stress
    lines = power_ref.shape[0]
    columns = squares.shape[0] // lines
    for line in range(lines):
        power_ref[line : line + 1, :] = (
            jnp.sum(squares[line * columns : (line + 1) * columns], axis=0, keepdims=True)
            / columns
        )


def call(kernel, name, out, *operands, flops, scratch=()):
    shapes = [jax.ShapeDtypeStruct(shape, dtype) for shape, dtype in out]
    moved = sum(x.size * x.dtype.itemsize for x in operands)
    moved += sum(math.prod(shape) * jnp.dtype(dtype).itemsize for shape, dtype in out)
    result = pl.pallas_call(
        kernel,
        out_shape=shapes,
        in_specs=[whole()] * len(operands),
        out_specs=[whole()] * len(out),
        scratch_shapes=scratch,
        compiler_params=pltpu.CompilerParams(vmem_limit_bytes=VMEM_BYTES),
        cost_estimate=pl.CostEstimate(flops=flops, bytes_accessed=moved, transcendentals=0),
        name=name,
    )(*operands)
    return result if len(out) > 1 else result[0]


def pseudo_by_sum(input_rows, input_factor, mode_freq, mode_damping, line_freq):
    lines = line_freq.shape[0]
    columns = input_factor.shape[1] // lines
    half = columns // 2
    forced = lax.psum(
        lax.dot_general(
            input_rows, input_factor, (((0,), (0,)), ((), ())), preferred_element_type=F32
        ),
        AXES,
    )
    pieces = []
    for line in range(lines):
        gain_real, gain_imag = modal_gain(mode_freq, mode_damping, line_freq[line])
        gain_real, gain_imag = gain_real[:, None], gain_imag[:, None]
        real = forced[:, line * columns : line * columns + half]
        imag = forced[:, line * columns + half : (line + 1) * columns]
        pieces.append(gain_real * real - gain_imag * imag)
        pieces.append(gain_real * imag + gain_imag * real)
    return jnp.concatenate(pieces, axis=1).astype(BF16)


def own_pseudo(input_rows, input_factor, mode_freq, mode_damping, line_freq, copies):
    devices = math.prod(FAST_SHAPE)
    rows, modes = input_rows.shape
    width = input_factor.shape[1]
    lines = line_freq.shape[0]
    parts = modes // (devices // 2 * width)
    ones = call(ones_kernel, "ones", [((8, width), F32)], flops=LONG)
    sent = call(
        pack_kernel,
        "pack",
        [((devices, (parts + 1) * rows, width), BF16)],
        ones,
        input_rows,
        input_factor,
        flops=LONG,
    )
    got = lax.all_to_all(sent, AXES, 0, 0)
    return call(
        functools.partial(pseudo_kernel, rows=rows),
        "pseudo",
        [((copies, parts * width, width), BF16)],
        line_freq.reshape(1, lines),
        mode_freq.reshape(-1, width),
        mode_damping.reshape(-1, width),
        got,
        flops=LONG,
    )


def local(
    shape,
    mode_rows,
    input_rows,
    input_factor,
    mode_freq,
    mode_damping,
    line_freq,
    boundary_rows,
    connectivity,
    stress_coef,
):
    devices = math.prod(shape)
    rows, modes = mode_rows.shape
    width = input_factor.shape[1]
    lines = line_freq.shape[0]
    exports = boundary_rows.shape[0]
    rim = exports // 2
    elems = connectivity.shape[1]
    inputs = (input_rows, input_factor, mode_freq, mode_damping, line_freq)
    if shape == FAST_SHAPE and modes == devices * LANES and input_rows.shape[0] % 16 == 0:
        cycle = [place ^ (place // 2) for place in range(8)]
        groups = [[h * 16 + j * 2 + c for j in cycle] for h in range(2) for c in range(2)]
        got = lax.all_to_all(own_pseudo(*inputs, copies=8), AXES, 0, 0, axis_index_groups=groups)
        mine = got.reshape(modes // 2, width)
        theirs = lax.ppermute(mine, AXES, [(i, i ^ 1) for i in range(devices)])
    else:
        pseudo = pseudo_by_sum(*inputs).reshape(2, modes // 2, width)
        core = lax.axis_index(AXES) % 2
        mine = lax.dynamic_index_in_dim(pseudo, core, 0, keepdims=False)
        theirs = lax.dynamic_index_in_dim(pseudo, 1 - core, 0, keepdims=False)
    total, part, picked = call(
        first_kernel,
        "first",
        [((rows, width), F32), ((exports, width), F32), ((exports, modes // 2), BF16)],
        boundary_rows.reshape(1, exports),
        mode_rows,
        mine,
        flops=rows * modes * (width + exports),
        scratch=[pltpu.VMEM((exports, rows), BF16)],
    )
    far, near = call(
        export_kernel,
        "export",
        [((rim, width), BF16)] * 2,
        part,
        picked,
        theirs,
        flops=exports * modes * width,
    )
    inner = [(i, i ^ 1) for i in range(devices)]
    outer = [(i, i + 1) for i in range(1, devices - 1, 2)]
    outer += [(j, i) for i, j in outer]
    near = lax.ppermute(near, AXES, inner)
    far = lax.ppermute(far, AXES, outer)
    stress, matrix = call(
        own_kernel,
        "own",
        [((width, elems), F32), ((2 * exports, elems), BF16)],
        connectivity,
        stress_coef,
        mode_rows,
        theirs,
        total,
        flops=rows * modes * width + 4 * rows * elems * width,
        scratch=[pltpu.VMEM((2, rows, elems), BF16), pltpu.VMEM((width, rows), BF16)],
    )
    return call(
        power_kernel,
        "power",
        [((lines, elems), F32)],
        stress,
        far,
        near,
        matrix,
        flops=4 * exports * elems * width,
    )


def solution(mesh):
    shape = tuple(mesh.shape[axis] for axis in AXES)
    placed = (
        P(AXES, None),
        P(AXES, None),
        P(AXES, None),
        P(),
        P(),
        P(),
        P(AXES),
        P(None, AXES),
        P(None, AXES),
    )
    return jax.shard_map(
        functools.partial(local, shape),
        mesh=mesh,
        in_specs=placed,
        out_specs=P(None, AXES),
        check_vma=False,
    )
```

```python
import functools
import math

import jax
import jax.numpy as jnp
from jax import lax
from jax.experimental import pallas as pl
from jax.experimental.pallas import tpu as pltpu
from jax.sharding import PartitionSpec as P

AXES = ("region", "sub")
LANES = 128
F32 = jnp.float32
BF16 = jnp.bfloat16
VMEM_BYTES = 24 * 1024 * 1024
LONG = 8 * 1024**3
FAST_SHAPE = (8, 4)


def whole(*_):
    return pl.BlockSpec(memory_space=pltpu.VMEM)


def modal_gain(freq, damping, omega):
    detune = freq * freq - omega * omega
    damped = 2.0 * damping * freq * omega
    magnitude = detune * detune + damped * damped
    return detune / magnitude, -damped / magnitude


def slab_of(device):
    chip = device // 2 % 8
    return device % 2 * 8 + (chip ^ (chip // 2) ^ (chip // 4))


def ones_kernel(ones_ref):
    ones_ref[...] = jnp.ones_like(ones_ref)


def pack_kernel(ones_ref, rows_ref, factor_ref, sent_ref):
    devices, _, width = sent_ref.shape
    rows = rows_ref.shape[0]
    parts = sent_ref.shape[1] // rows - 1
    factor = factor_ref[...] * ones_ref[0:1, :].astype(BF16)
    for device in range(devices):
        for part in range(parts):
            here = (slab_of(device) * parts + part) * width
            sent_ref[device, part * rows : (part + 1) * rows, :] = rows_ref[:, here : here + width]
        sent_ref[device, parts * rows :, :] = factor


def pseudo_kernel(line_ref, freq_ref, damping_ref, got_ref, pseudo_ref, *, rows):
    devices, tall, width = got_ref.shape
    parts = tall // rows - 1
    lines = line_ref.shape[1]
    columns = width // lines
    half = columns // 2
    slab = slab_of(lax.axis_index(AXES))
    factor = got_ref[:, parts * rows :, :].reshape(devices * rows, width)
    shapes = [
        got_ref[:, part * rows : (part + 1) * rows, :].reshape(devices * rows, width)
        for part in range(parts)
    ]
    forced = lax.dot_general(
        factor,
        jnp.concatenate(shapes, axis=1),
        (((0,), (0,)), ((), ())),
        preferred_element_type=F32,
    )
    for part in range(parts):
        here = pl.ds(slab * parts + part, 1)
        summed = forced[:, part * width : (part + 1) * width]
        pieces = []
        for line in range(lines):
            gain_real, gain_imag = modal_gain(
                freq_ref[here, :], damping_ref[here, :], line_ref[:, line : line + 1]
            )
            real = summed[line * columns : line * columns + half]
            imag = summed[line * columns + half : (line + 1) * columns]
            pieces.append(gain_real * real - gain_imag * imag)
            pieces.append(gain_real * imag + gain_imag * real)
        pseudo = jnp.concatenate(pieces, axis=0).T.astype(BF16)
        for copy in range(pseudo_ref.shape[0]):
            pseudo_ref[copy, part * width : (part + 1) * width, :] = pseudo


def for_core(depth, work):
    odd = lax.axis_index(AXES) % 2
    low, high = slice(0, depth), slice(depth, 2 * depth)
    pl.when(odd == 0)(lambda: work(low, high))
    pl.when(odd == 1)(lambda: work(high, low))


def first_kernel(boundary_ref, modes_ref, pseudo_ref, total_ref, part_ref, picked_ref, pick_ref):
    rows = modes_ref.shape[0]
    exports = boundary_ref.shape[1]
    chosen = jnp.broadcast_to(boundary_ref[...], (exports, exports)).astype(F32).T
    column = lax.broadcasted_iota(jnp.int32, (exports, exports), 1).astype(F32)
    pick_ref[...] = jnp.concatenate(
        [(column + start == chosen).astype(F32) for start in range(0, rows, exports)], axis=1
    ).astype(BF16)

    def product(mine, _):
        total_ref[...] = jnp.dot(modes_ref[:, mine], pseudo_ref[...], preferred_element_type=F32)

    def exported(_, other):
        pick = pick_ref[...]
        total = total_ref[...]
        high = total.astype(BF16)
        rest = total - high.astype(F32)
        middle = rest.astype(BF16)
        low = (rest - middle.astype(F32)).astype(BF16)
        parts = jnp.dot(
            pick, jnp.concatenate([high, middle, low], axis=1), preferred_element_type=F32
        )
        width = total.shape[1]
        part_ref[...] = parts[:, :width] + parts[:, width : 2 * width] + parts[:, 2 * width :]
        picked_ref[...] = jnp.dot(
            pick, modes_ref[:, other], preferred_element_type=F32
        ).astype(BF16)

    for_core(pseudo_ref.shape[0], product)
    for_core(pseudo_ref.shape[0], exported)


def export_kernel(part_ref, picked_ref, low_ref, high_ref, far_ref, near_ref):
    cut = low_ref.shape[0]
    export = part_ref[...] + jnp.dot(
        picked_ref[:, :cut], low_ref[...], preferred_element_type=F32
    )
    export = export + jnp.dot(picked_ref[:, cut:], high_ref[...], preferred_element_type=F32)
    export = export.astype(BF16)
    odd = lax.axis_index(AXES) % 2 == 1
    rim = far_ref.shape[0]
    far_ref[...] = jnp.where(odd, export[rim:], export[:rim])
    near_ref[...] = jnp.where(odd, export[:rim], export[rim:])


def own_kernel(
    connect_ref, coef_ref, modes_ref, low_ref, high_ref, total_ref,
    stress_ref, rim_ref, own_ref, table_ref,
):
    rows = modes_ref.shape[0]
    elems = connect_ref.shape[1]
    rim = rim_ref.shape[0] // 4
    odd = lax.axis_index(AXES) % 2

    def responses(_, other):
        total = total_ref[...]
        cut = low_ref.shape[0]
        for part_ref, start in ((low_ref, other.start), (high_ref, other.start + cut)):
            total = total + jnp.dot(
                modes_ref[:, start : start + cut], part_ref[...], preferred_element_type=F32
            )
        table_ref[...] = total.T.astype(BF16)

    for_core(2 * low_ref.shape[0], responses)

    def matrix(start, tall):
        node = lax.broadcasted_iota(jnp.int32, (tall, elems), 0) + start
        total = jnp.zeros((tall, elems), F32)
        for corner in range(connect_ref.shape[0]):
            hit = node == connect_ref[corner : corner + 1, :]
            total = total + jnp.where(hit, coef_ref[corner : corner + 1, :], 0.0)
        high = total.astype(BF16)
        return high, (total - high.astype(F32)).astype(BF16)

    after = rim + rows
    for place, start in ((0, after * odd), (1, after * (1 - odd))):
        high, low = matrix(start, rim)
        rim_ref[place * rim : (place + 1) * rim, :] = high
        rim_ref[(place + 2) * rim : (place + 3) * rim, :] = low
    for start in range(0, rows, rim):
        here = slice(start, start + rim)
        own_ref[0, here, :], own_ref[1, here, :] = matrix(start + rim, rim)
    table = table_ref[...]
    stress = jnp.dot(table, own_ref[0], preferred_element_type=F32)
    stress_ref[...] = stress + jnp.dot(table, own_ref[1], preferred_element_type=F32)


def power_kernel(stress_ref, far_ref, near_ref, rim_ref, power_ref):
    rows = [far_ref[...], near_ref[...]]
    stress = stress_ref[...] + lax.dot_general(
        jnp.concatenate(rows + rows, axis=0),
        rim_ref[...],
        (((0,), (0,)), ((), ())),
        preferred_element_type=F32,
    )
    squares = stress * stress
    lines = power_ref.shape[0]
    columns = squares.shape[0] // lines
    for line in range(lines):
        power_ref[line : line + 1, :] = (
            jnp.sum(squares[line * columns : (line + 1) * columns], axis=0, keepdims=True)
            / columns
        )


def call(kernel, name, out, *operands, flops, scratch=()):
    shapes = [jax.ShapeDtypeStruct(shape, dtype) for shape, dtype in out]
    moved = sum(x.size * x.dtype.itemsize for x in operands)
    moved += sum(math.prod(shape) * jnp.dtype(dtype).itemsize for shape, dtype in out)
    result = pl.pallas_call(
        kernel,
        out_shape=shapes,
        in_specs=[whole()] * len(operands),
        out_specs=[whole()] * len(out),
        scratch_shapes=scratch,
        compiler_params=pltpu.CompilerParams(vmem_limit_bytes=VMEM_BYTES),
        cost_estimate=pl.CostEstimate(flops=flops, bytes_accessed=moved, transcendentals=0),
        name=name,
    )(*operands)
    return result if len(out) > 1 else result[0]


def pseudo_by_sum(input_rows, input_factor, mode_freq, mode_damping, line_freq):
    lines = line_freq.shape[0]
    columns = input_factor.shape[1] // lines
    half = columns // 2
    forced = lax.psum(
        lax.dot_general(
            input_rows, input_factor, (((0,), (0,)), ((), ())), preferred_element_type=F32
        ),
        AXES,
    )
    pieces = []
    for line in range(lines):
        gain_real, gain_imag = modal_gain(mode_freq, mode_damping, line_freq[line])
        gain_real, gain_imag = gain_real[:, None], gain_imag[:, None]
        real = forced[:, line * columns : line * columns + half]
        imag = forced[:, line * columns + half : (line + 1) * columns]
        pieces.append(gain_real * real - gain_imag * imag)
        pieces.append(gain_real * imag + gain_imag * real)
    return jnp.concatenate(pieces, axis=1).astype(BF16)


def own_pseudo(input_rows, input_factor, mode_freq, mode_damping, line_freq, copies):
    devices = math.prod(FAST_SHAPE)
    rows, modes = input_rows.shape
    width = input_factor.shape[1]
    lines = line_freq.shape[0]
    parts = modes // (devices // 2 * width)
    ones = call(ones_kernel, "ones", [((8, width), F32)], flops=LONG)
    sent = call(
        pack_kernel,
        "pack",
        [((devices, (parts + 1) * rows, width), BF16)],
        ones,
        input_rows,
        input_factor,
        flops=LONG,
    )
    got = lax.all_to_all(sent, AXES, 0, 0)
    return call(
        functools.partial(pseudo_kernel, rows=rows),
        "pseudo",
        [((copies, parts * width, width), BF16)],
        line_freq.reshape(1, lines),
        mode_freq.reshape(-1, width),
        mode_damping.reshape(-1, width),
        got,
        flops=LONG,
    )


def local(
    shape,
    mode_rows,
    input_rows,
    input_factor,
    mode_freq,
    mode_damping,
    line_freq,
    boundary_rows,
    connectivity,
    stress_coef,
):
    devices = math.prod(shape)
    rows, modes = mode_rows.shape
    width = input_factor.shape[1]
    lines = line_freq.shape[0]
    exports = boundary_rows.shape[0]
    rim = exports // 2
    elems = connectivity.shape[1]
    inputs = (input_rows, input_factor, mode_freq, mode_damping, line_freq)
    if shape == FAST_SHAPE and modes == devices * LANES and input_rows.shape[0] % 16 == 0:
        cycle = [place ^ (place // 2) for place in range(8)]
        groups = [[h * 16 + j * 2 + c for j in cycle] for h in range(2) for c in range(2)]
        got = lax.all_to_all(own_pseudo(*inputs, copies=8), AXES, 0, 0, axis_index_groups=groups)
        mine = got.reshape(modes // 2, width)
        cut = modes // 4
        swap = [(i, i ^ 1) for i in range(devices)]
        theirs = [lax.ppermute(part, AXES, swap) for part in (mine[:cut], mine[cut:])]
    else:
        pseudo = pseudo_by_sum(*inputs).reshape(2, modes // 2, width)
        core = lax.axis_index(AXES) % 2
        mine = lax.dynamic_index_in_dim(pseudo, core, 0, keepdims=False)
        other = lax.dynamic_index_in_dim(pseudo, 1 - core, 0, keepdims=False)
        theirs = [other[: modes // 4], other[modes // 4 :]]
    total, part, picked = call(
        first_kernel,
        "first",
        [((rows, width), F32), ((exports, width), F32), ((exports, modes // 2), BF16)],
        boundary_rows.reshape(1, exports),
        mode_rows,
        mine,
        flops=rows * modes * (width + exports),
        scratch=[pltpu.VMEM((exports, rows), BF16)],
    )
    far, near = call(
        export_kernel,
        "export",
        [((rim, width), BF16)] * 2,
        part,
        picked,
        *theirs,
        flops=exports * modes * width,
    )
    inner = [(i, i ^ 1) for i in range(devices)]
    outer = [(i, i + 1) for i in range(1, devices - 1, 2)]
    outer += [(j, i) for i, j in outer]
    near = lax.ppermute(near, AXES, inner)
    far = lax.ppermute(far, AXES, outer)
    stress, matrix = call(
        own_kernel,
        "own",
        [((width, elems), F32), ((2 * exports, elems), BF16)],
        connectivity,
        stress_coef,
        mode_rows,
        *theirs,
        total,
        flops=rows * modes * width + 4 * rows * elems * width,
        scratch=[pltpu.VMEM((2, rows, elems), BF16), pltpu.VMEM((width, rows), BF16)],
    )
    return call(
        power_kernel,
        "power",
        [((lines, elems), F32)],
        stress,
        far,
        near,
        matrix,
        flops=4 * exports * elems * width,
    )


def solution(mesh):
    shape = tuple(mesh.shape[axis] for axis in AXES)
    placed = (
        P(AXES, None),
        P(AXES, None),
        P(AXES, None),
        P(),
        P(),
        P(),
        P(AXES),
        P(None, AXES),
        P(None, AXES),
    )
    return jax.shard_map(
        functools.partial(local, shape),
        mesh=mesh,
        in_specs=placed,
        out_specs=P(None, AXES),
        check_vma=False,
    )
```

```python
import functools
import math

import jax
import jax.numpy as jnp
from jax import lax
from jax.experimental import pallas as pl
from jax.experimental.pallas import tpu as pltpu
from jax.sharding import PartitionSpec as P

AXES = ("region", "sub")
LANES = 128
F32 = jnp.float32
BF16 = jnp.bfloat16
VMEM_BYTES = 24 * 1024 * 1024
LONG = 8 * 1024**3
FAST_SHAPE = (8, 4)


def whole(*_):
    return pl.BlockSpec(memory_space=pltpu.VMEM)


def modal_gain(freq, damping, omega):
    detune = freq * freq - omega * omega
    damped = 2.0 * damping * freq * omega
    magnitude = detune * detune + damped * damped
    return detune / magnitude, -damped / magnitude


def slab_of(device):
    chip = device // 2 % 8
    return device % 2 * 8 + (chip ^ (chip // 2) ^ (chip // 4))


def ones_kernel(ones_ref):
    ones_ref[...] = jnp.ones_like(ones_ref)


def pack_kernel(ones_ref, rows_ref, factor_ref, sent_ref):
    devices, _, width = sent_ref.shape
    rows = rows_ref.shape[0]
    parts = sent_ref.shape[1] // rows - 1
    factor = factor_ref[...] * ones_ref[0:1, :].astype(BF16)
    for device in range(devices):
        for part in range(parts):
            here = (slab_of(device) * parts + part) * width
            sent_ref[device, part * rows : (part + 1) * rows, :] = rows_ref[:, here : here + width]
        sent_ref[device, parts * rows :, :] = factor


def pseudo_kernel(
    boundary_ref, line_ref, freq_ref, damping_ref, got_ref, pseudo_ref, pick_ref, *, rows
):
    devices, tall, width = got_ref.shape
    parts = tall // rows - 1
    lines = line_ref.shape[1]
    columns = width // lines
    half = columns // 2
    slab = slab_of(lax.axis_index(AXES))
    factor = got_ref[:, parts * rows :, :].reshape(devices * rows, width)
    shapes = [
        got_ref[:, part * rows : (part + 1) * rows, :].reshape(devices * rows, width)
        for part in range(parts)
    ]
    forced = lax.dot_general(
        factor,
        jnp.concatenate(shapes, axis=1),
        (((0,), (0,)), ((), ())),
        preferred_element_type=F32,
    )
    for part in range(parts):
        here = pl.ds(slab * parts + part, 1)
        summed = forced[:, part * width : (part + 1) * width]
        pieces = []
        for line in range(lines):
            gain_real, gain_imag = modal_gain(
                freq_ref[here, :], damping_ref[here, :], line_ref[:, line : line + 1]
            )
            real = summed[line * columns : line * columns + half]
            imag = summed[line * columns + half : (line + 1) * columns]
            pieces.append(gain_real * real - gain_imag * imag)
            pieces.append(gain_real * imag + gain_imag * real)
        pseudo = jnp.concatenate(pieces, axis=0).T.astype(BF16)
        for copy in range(pseudo_ref.shape[0]):
            pseudo_ref[copy, part * width : (part + 1) * width, :] = pseudo
    exports, owned = pick_ref.shape
    chosen = jnp.broadcast_to(boundary_ref[...], (exports, exports)).astype(F32).T
    column = lax.broadcasted_iota(jnp.int32, (exports, exports), 1).astype(F32)
    for start in range(0, owned, exports):
        pick = (column + start == chosen).astype(F32).astype(BF16)
        pick_ref[:, start : start + exports] = pick


def for_core(depth, work):
    odd = lax.axis_index(AXES) % 2
    low, high = slice(0, depth), slice(depth, 2 * depth)
    pl.when(odd == 0)(lambda: work(low, high))
    pl.when(odd == 1)(lambda: work(high, low))


def first_kernel(pick_ref, modes_ref, pseudo_ref, total_ref, part_ref, picked_ref):
    depth = pseudo_ref.shape[0]
    odd = lax.axis_index(AXES) % 2
    mine = pl.ds(pl.multiple_of(odd * depth, depth), depth)
    total_ref[...] = jnp.dot(modes_ref[:, mine], pseudo_ref[...], preferred_element_type=F32)

    def shapes(_, other):
        picked_ref[...] = jnp.dot(
            pick_ref[...], modes_ref[:, other], preferred_element_type=F32
        ).astype(BF16)

    for_core(depth, shapes)
    total = total_ref[...]
    high = total.astype(BF16)
    rest = total - high.astype(F32)
    middle = rest.astype(BF16)
    low = (rest - middle.astype(F32)).astype(BF16)
    parts = jnp.dot(
        pick_ref[...], jnp.concatenate([high, middle, low], axis=1), preferred_element_type=F32
    )
    width = total.shape[1]
    part_ref[...] = parts[:, :width] + parts[:, width : 2 * width] + parts[:, 2 * width :]


def export_kernel(part_ref, picked_ref, low_ref, high_ref, far_ref, near_ref):
    cut = low_ref.shape[0]
    export = part_ref[...] + jnp.dot(
        picked_ref[:, :cut], low_ref[...], preferred_element_type=F32
    )
    export = export + jnp.dot(picked_ref[:, cut:], high_ref[...], preferred_element_type=F32)
    export = export.astype(BF16)
    odd = lax.axis_index(AXES) % 2 == 1
    rim = far_ref.shape[0]
    far_ref[...] = jnp.where(odd, export[rim:], export[:rim])
    near_ref[...] = jnp.where(odd, export[:rim], export[rim:])


def own_kernel(
    connect_ref, coef_ref, modes_ref, low_ref, high_ref, total_ref,
    stress_ref, rim_ref, own_ref, table_ref,
):
    rows = modes_ref.shape[0]
    elems = connect_ref.shape[1]
    rim = rim_ref.shape[0] // 4
    odd = lax.axis_index(AXES) % 2

    def responses(_, other):
        total = total_ref[...]
        cut = low_ref.shape[0]
        for part_ref, start in ((low_ref, other.start), (high_ref, other.start + cut)):
            total = total + jnp.dot(
                modes_ref[:, start : start + cut], part_ref[...], preferred_element_type=F32
            )
        table_ref[...] = total.T.astype(BF16)

    for_core(2 * low_ref.shape[0], responses)

    def matrix(start, tall):
        node = lax.broadcasted_iota(jnp.int32, (tall, elems), 0) + start
        total = jnp.zeros((tall, elems), F32)
        for corner in range(connect_ref.shape[0]):
            hit = node == connect_ref[corner : corner + 1, :]
            total = total + jnp.where(hit, coef_ref[corner : corner + 1, :], 0.0)
        high = total.astype(BF16)
        return high, (total - high.astype(F32)).astype(BF16)

    after = rim + rows
    for place, start in ((0, after * odd), (1, after * (1 - odd))):
        high, low = matrix(start, rim)
        rim_ref[place * rim : (place + 1) * rim, :] = high
        rim_ref[(place + 2) * rim : (place + 3) * rim, :] = low
    for start in range(0, rows, rim):
        here = slice(start, start + rim)
        own_ref[0, here, :], own_ref[1, here, :] = matrix(start + rim, rim)
    table = table_ref[...]
    stress = jnp.dot(table, own_ref[0], preferred_element_type=F32)
    stress_ref[...] = stress + jnp.dot(table, own_ref[1], preferred_element_type=F32)


def power_kernel(stress_ref, far_ref, near_ref, rim_ref, power_ref):
    rows = [far_ref[...], near_ref[...]]
    stress = stress_ref[...] + lax.dot_general(
        jnp.concatenate(rows + rows, axis=0),
        rim_ref[...],
        (((0,), (0,)), ((), ())),
        preferred_element_type=F32,
    )
    squares = stress * stress
    lines = power_ref.shape[0]
    columns = squares.shape[0] // lines
    for line in range(lines):
        power_ref[line : line + 1, :] = (
            jnp.sum(squares[line * columns : (line + 1) * columns], axis=0, keepdims=True)
            / columns
        )


def call(kernel, name, out, *operands, flops, scratch=()):
    shapes = [jax.ShapeDtypeStruct(shape, dtype) for shape, dtype in out]
    moved = sum(x.size * x.dtype.itemsize for x in operands)
    moved += sum(math.prod(shape) * jnp.dtype(dtype).itemsize for shape, dtype in out)
    result = pl.pallas_call(
        kernel,
        out_shape=shapes,
        in_specs=[whole()] * len(operands),
        out_specs=[whole()] * len(out),
        scratch_shapes=scratch,
        compiler_params=pltpu.CompilerParams(vmem_limit_bytes=VMEM_BYTES),
        cost_estimate=pl.CostEstimate(flops=flops, bytes_accessed=moved, transcendentals=0),
        name=name,
    )(*operands)
    return result if len(out) > 1 else result[0]


def pseudo_by_sum(input_rows, input_factor, mode_freq, mode_damping, line_freq):
    lines = line_freq.shape[0]
    columns = input_factor.shape[1] // lines
    half = columns // 2
    forced = lax.psum(
        lax.dot_general(
            input_rows, input_factor, (((0,), (0,)), ((), ())), preferred_element_type=F32
        ),
        AXES,
    )
    pieces = []
    for line in range(lines):
        gain_real, gain_imag = modal_gain(mode_freq, mode_damping, line_freq[line])
        gain_real, gain_imag = gain_real[:, None], gain_imag[:, None]
        real = forced[:, line * columns : line * columns + half]
        imag = forced[:, line * columns + half : (line + 1) * columns]
        pieces.append(gain_real * real - gain_imag * imag)
        pieces.append(gain_real * imag + gain_imag * real)
    return jnp.concatenate(pieces, axis=1).astype(BF16)


def own_pseudo(
    input_rows, input_factor, mode_freq, mode_damping, line_freq, boundary_rows, owned, copies
):
    devices = math.prod(FAST_SHAPE)
    rows, modes = input_rows.shape
    width = input_factor.shape[1]
    lines = line_freq.shape[0]
    parts = modes // (devices // 2 * width)
    ones = call(ones_kernel, "ones", [((8, width), F32)], flops=LONG)
    sent = call(
        pack_kernel,
        "pack",
        [((devices, (parts + 1) * rows, width), BF16)],
        ones,
        input_rows,
        input_factor,
        flops=LONG,
    )
    got = lax.all_to_all(sent, AXES, 0, 0)
    return call(
        functools.partial(pseudo_kernel, rows=rows),
        "pseudo",
        [((copies, parts * width, width), BF16), ((boundary_rows.shape[0], owned), BF16)],
        boundary_rows.reshape(1, -1),
        line_freq.reshape(1, lines),
        mode_freq.reshape(-1, width),
        mode_damping.reshape(-1, width),
        got,
        flops=LONG,
    )


def local(
    shape,
    mode_rows,
    input_rows,
    input_factor,
    mode_freq,
    mode_damping,
    line_freq,
    boundary_rows,
    connectivity,
    stress_coef,
):
    devices = math.prod(shape)
    rows, modes = mode_rows.shape
    width = input_factor.shape[1]
    lines = line_freq.shape[0]
    exports = boundary_rows.shape[0]
    rim = exports // 2
    elems = connectivity.shape[1]
    inputs = (input_rows, input_factor, mode_freq, mode_damping, line_freq)
    if shape == FAST_SHAPE and modes == devices * LANES and input_rows.shape[0] % 16 == 0:
        cycle = [place ^ (place // 2) for place in range(8)]
        groups = [[h * 16 + j * 2 + c for j in cycle] for h in range(2) for c in range(2)]
        block, pick = own_pseudo(*inputs, boundary_rows, rows, copies=8)
        got = lax.all_to_all(block, AXES, 0, 0, axis_index_groups=groups)
        mine = got.reshape(modes // 2, width)
        cut = modes // 4
        swap = [(i, i ^ 1) for i in range(devices)]
        theirs = [lax.ppermute(part, AXES, swap) for part in (mine[:cut], mine[cut:])]
    else:
        pseudo = pseudo_by_sum(*inputs).reshape(2, modes // 2, width)
        pick = (boundary_rows[:, None] == jnp.arange(rows)[None, :]).astype(BF16)
        core = lax.axis_index(AXES) % 2
        mine = lax.dynamic_index_in_dim(pseudo, core, 0, keepdims=False)
        other = lax.dynamic_index_in_dim(pseudo, 1 - core, 0, keepdims=False)
        theirs = [other[: modes // 4], other[modes // 4 :]]
    total, part, picked = call(
        first_kernel,
        "first",
        [((rows, width), F32), ((exports, width), F32), ((exports, modes // 2), BF16)],
        pick,
        mode_rows,
        mine,
        flops=rows * modes * (width + exports),
    )
    far, near = call(
        export_kernel,
        "export",
        [((rim, width), BF16)] * 2,
        part,
        picked,
        *theirs,
        flops=exports * modes * width,
    )
    inner = [(i, i ^ 1) for i in range(devices)]
    outer = [(i, i + 1) for i in range(1, devices - 1, 2)]
    outer += [(j, i) for i, j in outer]
    near = lax.ppermute(near, AXES, inner)
    far = lax.ppermute(far, AXES, outer)
    stress, matrix = call(
        own_kernel,
        "own",
        [((width, elems), F32), ((2 * exports, elems), BF16)],
        connectivity,
        stress_coef,
        mode_rows,
        *theirs,
        total,
        flops=rows * modes * width + 4 * rows * elems * width,
        scratch=[pltpu.VMEM((2, rows, elems), BF16), pltpu.VMEM((width, rows), BF16)],
    )
    return call(
        power_kernel,
        "power",
        [((lines, elems), F32)],
        stress,
        far,
        near,
        matrix,
        flops=4 * exports * elems * width,
    )


def solution(mesh):
    shape = tuple(mesh.shape[axis] for axis in AXES)
    placed = (
        P(AXES, None),
        P(AXES, None),
        P(AXES, None),
        P(),
        P(),
        P(),
        P(AXES),
        P(None, AXES),
        P(None, AXES),
    )
    return jax.shard_map(
        functools.partial(local, shape),
        mesh=mesh,
        in_specs=placed,
        out_specs=P(None, AXES),
        check_vma=False,
    )
```

```python
import functools
import math

import jax
import jax.numpy as jnp
from jax import lax
from jax.experimental import pallas as pl
from jax.experimental.pallas import tpu as pltpu
from jax.sharding import PartitionSpec as P

AXES = ("region", "sub")
LANES = 128
F32 = jnp.float32
BF16 = jnp.bfloat16
VMEM_BYTES = 24 * 1024 * 1024
LONG = 8 * 1024**3
FAST_SHAPE = (8, 4)


def whole(*_):
    return pl.BlockSpec(memory_space=pltpu.VMEM)


def modal_gain(freq, damping, omega):
    detune = freq * freq - omega * omega
    damped = 2.0 * damping * freq * omega
    magnitude = detune * detune + damped * damped
    return detune / magnitude, -damped / magnitude


def slab_of(device):
    chip = device // 2 % 8
    return device % 2 * 8 + (chip ^ (chip // 2) ^ (chip // 4))


def ones_kernel(ones_ref):
    ones_ref[...] = jnp.ones_like(ones_ref)


def pack_kernel(ones_ref, rows_ref, factor_ref, sent_ref):
    devices, _, width = sent_ref.shape
    rows = rows_ref.shape[0]
    parts = sent_ref.shape[1] // rows - 1
    factor = factor_ref[...] * ones_ref[0:1, :].astype(BF16)
    for device in range(devices):
        for part in range(parts):
            here = (slab_of(device) * parts + part) * width
            sent_ref[device, part * rows : (part + 1) * rows, :] = rows_ref[:, here : here + width]
        sent_ref[device, parts * rows :, :] = factor


def pseudo_kernel(line_ref, freq_ref, damping_ref, got_ref, pseudo_ref, *, rows):
    devices, tall, width = got_ref.shape
    parts = tall // rows - 1
    lines = line_ref.shape[1]
    columns = width // lines
    half = columns // 2
    slab = slab_of(lax.axis_index(AXES))
    factor = got_ref[:, parts * rows :, :].reshape(devices * rows, width)
    shapes = [
        got_ref[:, part * rows : (part + 1) * rows, :].reshape(devices * rows, width)
        for part in range(parts)
    ]
    forced = lax.dot_general(
        factor,
        jnp.concatenate(shapes, axis=1),
        (((0,), (0,)), ((), ())),
        preferred_element_type=F32,
    )
    for part in range(parts):
        here = pl.ds(slab * parts + part, 1)
        summed = forced[:, part * width : (part + 1) * width]
        pieces = []
        for line in range(lines):
            gain_real, gain_imag = modal_gain(
                freq_ref[here, :], damping_ref[here, :], line_ref[:, line : line + 1]
            )
            real = summed[line * columns : line * columns + half]
            imag = summed[line * columns + half : (line + 1) * columns]
            pieces.append(gain_real * real - gain_imag * imag)
            pieces.append(gain_real * imag + gain_imag * real)
        pseudo = jnp.concatenate(pieces, axis=0).T.astype(BF16)
        for copy in range(pseudo_ref.shape[0]):
            pseudo_ref[copy, part * width : (part + 1) * width, :] = pseudo


def for_core(depth, work):
    odd = lax.axis_index(AXES) % 2
    low, high = slice(0, depth), slice(depth, 2 * depth)
    pl.when(odd == 0)(lambda: work(low, high))
    pl.when(odd == 1)(lambda: work(high, low))


def first_kernel(boundary_ref, modes_ref, pseudo_ref, total_ref, part_ref, picked_ref, pick_ref):
    rows = modes_ref.shape[0]
    exports = boundary_ref.shape[1]
    chosen = jnp.broadcast_to(boundary_ref[...], (exports, exports)).astype(F32).T
    column = lax.broadcasted_iota(jnp.int32, (exports, exports), 1).astype(F32)
    pick_ref[...] = jnp.concatenate(
        [(column + start == chosen).astype(F32) for start in range(0, rows, exports)], axis=1
    ).astype(BF16)

    def product(mine, _):
        total_ref[...] = jnp.dot(modes_ref[:, mine], pseudo_ref[...], preferred_element_type=F32)

    def exported(_, other):
        pick = pick_ref[...]
        total = total_ref[...]
        high = total.astype(BF16)
        rest = total - high.astype(F32)
        middle = rest.astype(BF16)
        low = (rest - middle.astype(F32)).astype(BF16)
        parts = jnp.dot(
            pick, jnp.concatenate([high, middle, low], axis=1), preferred_element_type=F32
        )
        width = total.shape[1]
        part_ref[...] = parts[:, :width] + parts[:, width : 2 * width] + parts[:, 2 * width :]
        picked_ref[...] = jnp.dot(
            pick, modes_ref[:, other], preferred_element_type=F32
        ).astype(BF16)

    for_core(pseudo_ref.shape[0], product)
    for_core(pseudo_ref.shape[0], exported)


def export_kernel(part_ref, picked_ref, pseudo_ref, far_ref, near_ref):
    exports = part_ref.shape[0]
    cut = pseudo_ref.shape[0] // 2
    width = pseudo_ref.shape[1]
    both = jnp.dot(
        jnp.concatenate([picked_ref[:, :cut], picked_ref[:, cut:]], axis=0),
        jnp.concatenate([pseudo_ref[:cut], pseudo_ref[cut:]], axis=1),
        preferred_element_type=F32,
    )
    export = part_ref[...] + both[:exports, :width] + both[exports:, width:]
    export = export.astype(BF16)
    odd = lax.axis_index(AXES) % 2 == 1
    rim = far_ref.shape[0]
    far_ref[...] = jnp.where(odd, export[rim:], export[:rim])
    near_ref[...] = jnp.where(odd, export[:rim], export[rim:])


def own_kernel(
    connect_ref, coef_ref, modes_ref, pseudo_ref, total_ref, stress_ref, rim_ref, own_ref, table_ref
):
    rows = modes_ref.shape[0]
    elems = connect_ref.shape[1]
    rim = rim_ref.shape[0] // 4
    odd = lax.axis_index(AXES) % 2

    depth = pseudo_ref.shape[0]
    other = pl.ds(pl.multiple_of((1 - odd) * depth, depth), depth)
    total = total_ref[...] + jnp.dot(
        modes_ref[:, other], pseudo_ref[...], preferred_element_type=F32
    )
    table_ref[...] = total.T.astype(BF16)

    def matrix(start, tall):
        node = lax.broadcasted_iota(jnp.int32, (tall, elems), 0) + start
        total = jnp.zeros((tall, elems), F32)
        for corner in range(connect_ref.shape[0]):
            hit = node == connect_ref[corner : corner + 1, :]
            total = total + jnp.where(hit, coef_ref[corner : corner + 1, :], 0.0)
        high = total.astype(BF16)
        return high, (total - high.astype(F32)).astype(BF16)

    after = rim + rows
    for place, start in ((0, after * odd), (1, after * (1 - odd))):
        high, low = matrix(start, rim)
        rim_ref[place * rim : (place + 1) * rim, :] = high
        rim_ref[(place + 2) * rim : (place + 3) * rim, :] = low
    for start in range(0, rows, rim):
        here = slice(start, start + rim)
        own_ref[0, here, :], own_ref[1, here, :] = matrix(start + rim, rim)
    table = table_ref[...]
    stress = jnp.dot(table, own_ref[0], preferred_element_type=F32)
    stress_ref[...] = stress + jnp.dot(table, own_ref[1], preferred_element_type=F32)


def power_kernel(stress_ref, far_ref, near_ref, rim_ref, power_ref):
    rows = [far_ref[...], near_ref[...]]
    stress = stress_ref[...] + lax.dot_general(
        jnp.concatenate(rows + rows, axis=0),
        rim_ref[...],
        (((0,), (0,)), ((), ())),
        preferred_element_type=F32,
    )
    squares = stress * stress
    lines = power_ref.shape[0]
    columns = squares.shape[0] // lines
    for line in range(lines):
        power_ref[line : line + 1, :] = (
            jnp.sum(squares[line * columns : (line + 1) * columns], axis=0, keepdims=True)
            / columns
        )


def call(kernel, name, out, *operands, flops, scratch=()):
    shapes = [jax.ShapeDtypeStruct(shape, dtype) for shape, dtype in out]
    moved = sum(x.size * x.dtype.itemsize for x in operands)
    moved += sum(math.prod(shape) * jnp.dtype(dtype).itemsize for shape, dtype in out)
    result = pl.pallas_call(
        kernel,
        out_shape=shapes,
        in_specs=[whole()] * len(operands),
        out_specs=[whole()] * len(out),
        scratch_shapes=scratch,
        compiler_params=pltpu.CompilerParams(vmem_limit_bytes=VMEM_BYTES),
        cost_estimate=pl.CostEstimate(flops=flops, bytes_accessed=moved, transcendentals=0),
        name=name,
    )(*operands)
    return result if len(out) > 1 else result[0]


def pseudo_by_sum(input_rows, input_factor, mode_freq, mode_damping, line_freq):
    lines = line_freq.shape[0]
    columns = input_factor.shape[1] // lines
    half = columns // 2
    forced = lax.psum(
        lax.dot_general(
            input_rows, input_factor, (((0,), (0,)), ((), ())), preferred_element_type=F32
        ),
        AXES,
    )
    pieces = []
    for line in range(lines):
        gain_real, gain_imag = modal_gain(mode_freq, mode_damping, line_freq[line])
        gain_real, gain_imag = gain_real[:, None], gain_imag[:, None]
        real = forced[:, line * columns : line * columns + half]
        imag = forced[:, line * columns + half : (line + 1) * columns]
        pieces.append(gain_real * real - gain_imag * imag)
        pieces.append(gain_real * imag + gain_imag * real)
    return jnp.concatenate(pieces, axis=1).astype(BF16)


def own_pseudo(input_rows, input_factor, mode_freq, mode_damping, line_freq, copies):
    devices = math.prod(FAST_SHAPE)
    rows, modes = input_rows.shape
    width = input_factor.shape[1]
    lines = line_freq.shape[0]
    parts = modes // (devices // 2 * width)
    ones = call(ones_kernel, "ones", [((8, width), F32)], flops=LONG)
    sent = call(
        pack_kernel,
        "pack",
        [((devices, (parts + 1) * rows, width), BF16)],
        ones,
        input_rows,
        input_factor,
        flops=LONG,
    )
    got = lax.all_to_all(sent, AXES, 0, 0)
    return call(
        functools.partial(pseudo_kernel, rows=rows),
        "pseudo",
        [((copies, parts * width, width), BF16)],
        line_freq.reshape(1, lines),
        mode_freq.reshape(-1, width),
        mode_damping.reshape(-1, width),
        got,
        flops=LONG,
    )


def local(
    shape,
    mode_rows,
    input_rows,
    input_factor,
    mode_freq,
    mode_damping,
    line_freq,
    boundary_rows,
    connectivity,
    stress_coef,
):
    devices = math.prod(shape)
    rows, modes = mode_rows.shape
    width = input_factor.shape[1]
    lines = line_freq.shape[0]
    exports = boundary_rows.shape[0]
    rim = exports // 2
    elems = connectivity.shape[1]
    inputs = (input_rows, input_factor, mode_freq, mode_damping, line_freq)
    if shape == FAST_SHAPE and modes == devices * LANES and input_rows.shape[0] % 16 == 0:
        cycle = [place ^ (place // 2) for place in range(8)]
        groups = [[h * 16 + j * 2 + c for j in cycle] for h in range(2) for c in range(2)]
        got = lax.all_to_all(own_pseudo(*inputs, copies=8), AXES, 0, 0, axis_index_groups=groups)
        mine = got.reshape(modes // 2, width)
        theirs = lax.ppermute(mine, AXES, [(i, i ^ 1) for i in range(devices)])
    else:
        pseudo = pseudo_by_sum(*inputs).reshape(2, modes // 2, width)
        core = lax.axis_index(AXES) % 2
        mine = lax.dynamic_index_in_dim(pseudo, core, 0, keepdims=False)
        theirs = lax.dynamic_index_in_dim(pseudo, 1 - core, 0, keepdims=False)
    total, part, picked = call(
        first_kernel,
        "first",
        [((rows, width), F32), ((exports, width), F32), ((exports, modes // 2), BF16)],
        boundary_rows.reshape(1, exports),
        mode_rows,
        mine,
        flops=rows * modes * (width + exports),
        scratch=[pltpu.VMEM((exports, rows), BF16)],
    )
    far, near = call(
        export_kernel,
        "export",
        [((rim, width), BF16)] * 2,
        part,
        picked,
        theirs,
        flops=exports * modes * width,
    )
    inner = [(i, i ^ 1) for i in range(devices)]
    outer = [(i, i + 1) for i in range(1, devices - 1, 2)]
    outer += [(j, i) for i, j in outer]
    near = lax.ppermute(near, AXES, inner)
    far = lax.ppermute(far, AXES, outer)
    stress, matrix = call(
        own_kernel,
        "own",
        [((width, elems), F32), ((2 * exports, elems), BF16)],
        connectivity,
        stress_coef,
        mode_rows,
        theirs,
        total,
        flops=rows * modes * width + 4 * rows * elems * width,
        scratch=[pltpu.VMEM((2, rows, elems), BF16), pltpu.VMEM((width, rows), BF16)],
    )
    return call(
        power_kernel,
        "power",
        [((lines, elems), F32)],
        stress,
        far,
        near,
        matrix,
        flops=4 * exports * elems * width,
    )


def solution(mesh):
    shape = tuple(mesh.shape[axis] for axis in AXES)
    placed = (
        P(AXES, None),
        P(AXES, None),
        P(AXES, None),
        P(),
        P(),
        P(),
        P(AXES),
        P(None, AXES),
        P(None, AXES),
    )
    return jax.shard_map(
        functools.partial(local, shape),
        mesh=mesh,
        in_specs=placed,
        out_specs=P(None, AXES),
        check_vma=False,
    )
```

```python
import functools
import math

import jax
import jax.numpy as jnp
from jax import lax
from jax.experimental import pallas as pl
from jax.experimental.pallas import tpu as pltpu
from jax.sharding import PartitionSpec as P

AXES = ("region", "sub")
LANES = 128
F32 = jnp.float32
BF16 = jnp.bfloat16
VMEM_BYTES = 24 * 1024 * 1024
LONG = 8 * 1024**3
FAST_SHAPE = (8, 4)


def whole(*_):
    return pl.BlockSpec(memory_space=pltpu.VMEM)


def modal_gain(freq, damping, omega):
    detune = freq * freq - omega * omega
    damped = 2.0 * damping * freq * omega
    magnitude = detune * detune + damped * damped
    return detune / magnitude, -damped / magnitude


def slab_of(device):
    chip = device // 2 % 8
    return 2 * (chip ^ (chip // 2) ^ (chip // 4)) + device % 2


def ones_kernel(ones_ref):
    ones_ref[...] = jnp.ones_like(ones_ref)


def pack_kernel(ones_ref, rows_ref, factor_ref, sent_ref):
    devices, _, width = sent_ref.shape
    rows = rows_ref.shape[0]
    parts = sent_ref.shape[1] // rows - 1
    slabs = rows_ref.shape[1] // (parts * width)
    factor = factor_ref[...] * ones_ref[0:1, :].astype(BF16)
    for device in range(devices):
        for part in range(parts):
            here = (part * slabs + slab_of(device)) * width
            sent_ref[device, part * rows : (part + 1) * rows, :] = rows_ref[:, here : here + width]
        sent_ref[device, parts * rows :, :] = factor


def pseudo_kernel(line_ref, freq_ref, damping_ref, got_ref, pseudo_ref, *, rows):
    devices, tall, width = got_ref.shape
    parts = tall // rows - 1
    lines = line_ref.shape[1]
    columns = width // lines
    half = columns // 2
    slab = slab_of(lax.axis_index(AXES))
    slabs = freq_ref.shape[0] // parts
    factor = got_ref[:, parts * rows :, :].reshape(devices * rows, width)
    shapes = [
        got_ref[:, part * rows : (part + 1) * rows, :].reshape(devices * rows, width)
        for part in range(parts)
    ]
    forced = lax.dot_general(
        factor,
        jnp.concatenate(shapes, axis=1),
        (((0,), (0,)), ((), ())),
        preferred_element_type=F32,
    )
    for part in range(parts):
        here = pl.ds(part * slabs + slab, 1)
        summed = forced[:, part * width : (part + 1) * width]
        pieces = []
        for line in range(lines):
            gain_real, gain_imag = modal_gain(
                freq_ref[here, :], damping_ref[here, :], line_ref[:, line : line + 1]
            )
            real = summed[line * columns : line * columns + half]
            imag = summed[line * columns + half : (line + 1) * columns]
            pieces.append(gain_real * real - gain_imag * imag)
            pieces.append(gain_real * imag + gain_imag * real)
        pseudo = jnp.concatenate(pieces, axis=0).T.astype(BF16)
        for member in range(part, pseudo_ref.shape[0], parts):
            pseudo_ref[member] = pseudo


def for_core(depth, work):
    odd = lax.axis_index(AXES) % 2
    low, high = slice(0, depth), slice(depth, 2 * depth)
    pl.when(odd == 0)(lambda: work(low, high))
    pl.when(odd == 1)(lambda: work(high, low))


def first_kernel(boundary_ref, modes_ref, pseudo_ref, total_ref, part_ref, picked_ref, pick_ref):
    rows = modes_ref.shape[0]
    exports = boundary_ref.shape[1]
    chosen = jnp.broadcast_to(boundary_ref[...], (exports, exports)).astype(F32).T
    column = lax.broadcasted_iota(jnp.int32, (exports, exports), 1).astype(F32)
    pick_ref[...] = jnp.concatenate(
        [(column + start == chosen).astype(F32) for start in range(0, rows, exports)], axis=1
    ).astype(BF16)

    def product(mine, _):
        total_ref[...] = jnp.dot(modes_ref[:, mine], pseudo_ref[...], preferred_element_type=F32)

    def exported(_, other):
        pick = pick_ref[...]
        total = total_ref[...]
        high = total.astype(BF16)
        rest = total - high.astype(F32)
        middle = rest.astype(BF16)
        low = (rest - middle.astype(F32)).astype(BF16)
        parts = jnp.dot(
            pick, jnp.concatenate([high, middle, low], axis=1), preferred_element_type=F32
        )
        width = total.shape[1]
        part_ref[...] = parts[:, :width] + parts[:, width : 2 * width] + parts[:, 2 * width :]
        picked_ref[...] = jnp.dot(
            pick, modes_ref[:, other], preferred_element_type=F32
        ).astype(BF16)

    for_core(pseudo_ref.shape[0], product)
    for_core(pseudo_ref.shape[0], exported)


def export_kernel(part_ref, picked_ref, pseudo_ref, far_ref, near_ref):
    exports = part_ref.shape[0]
    cut = pseudo_ref.shape[0] // 2
    width = pseudo_ref.shape[1]
    both = jnp.dot(
        jnp.concatenate([picked_ref[:, :cut], picked_ref[:, cut:]], axis=0),
        jnp.concatenate([pseudo_ref[:cut], pseudo_ref[cut:]], axis=1),
        preferred_element_type=F32,
    )
    export = part_ref[...] + both[:exports, :width] + both[exports:, width:]
    export = export.astype(BF16)
    odd = lax.axis_index(AXES) % 2 == 1
    rim = far_ref.shape[0]
    far_ref[...] = jnp.where(odd, export[rim:], export[:rim])
    near_ref[...] = jnp.where(odd, export[:rim], export[rim:])


def own_kernel(
    connect_ref, coef_ref, modes_ref, pseudo_ref, total_ref, stress_ref, rim_ref, own_ref, table_ref
):
    rows = modes_ref.shape[0]
    elems = connect_ref.shape[1]
    rim = rim_ref.shape[0] // 4
    odd = lax.axis_index(AXES) % 2

    depth = pseudo_ref.shape[0]
    other = pl.ds(pl.multiple_of((1 - odd) * depth, depth), depth)
    total = total_ref[...] + jnp.dot(
        modes_ref[:, other], pseudo_ref[...], preferred_element_type=F32
    )
    table_ref[...] = total.T.astype(BF16)

    def matrix(start, tall):
        node = lax.broadcasted_iota(jnp.int32, (tall, elems), 0) + start
        total = jnp.zeros((tall, elems), F32)
        for corner in range(connect_ref.shape[0]):
            hit = node == connect_ref[corner : corner + 1, :]
            total = total + jnp.where(hit, coef_ref[corner : corner + 1, :], 0.0)
        high = total.astype(BF16)
        return high, (total - high.astype(F32)).astype(BF16)

    after = rim + rows
    for place, start in ((0, after * odd), (1, after * (1 - odd))):
        high, low = matrix(start, rim)
        rim_ref[place * rim : (place + 1) * rim, :] = high
        rim_ref[(place + 2) * rim : (place + 3) * rim, :] = low
    for start in range(0, rows, rim):
        here = slice(start, start + rim)
        own_ref[0, here, :], own_ref[1, here, :] = matrix(start + rim, rim)
    table = table_ref[...]
    stress = jnp.dot(table, own_ref[0], preferred_element_type=F32)
    stress_ref[...] = stress + jnp.dot(table, own_ref[1], preferred_element_type=F32)


def power_kernel(stress_ref, far_ref, near_ref, rim_ref, power_ref):
    rows = [far_ref[...], near_ref[...]]
    stress = stress_ref[...] + lax.dot_general(
        jnp.concatenate(rows + rows, axis=0),
        rim_ref[...],
        (((0,), (0,)), ((), ())),
        preferred_element_type=F32,
    )
    squares = stress * stress
    lines = power_ref.shape[0]
    columns = squares.shape[0] // lines
    for line in range(lines):
        power_ref[line : line + 1, :] = (
            jnp.sum(squares[line * columns : (line + 1) * columns], axis=0, keepdims=True)
            / columns
        )


def call(kernel, name, out, *operands, flops, scratch=()):
    shapes = [jax.ShapeDtypeStruct(shape, dtype) for shape, dtype in out]
    moved = sum(x.size * x.dtype.itemsize for x in operands)
    moved += sum(math.prod(shape) * jnp.dtype(dtype).itemsize for shape, dtype in out)
    result = pl.pallas_call(
        kernel,
        out_shape=shapes,
        in_specs=[whole()] * len(operands),
        out_specs=[whole()] * len(out),
        scratch_shapes=scratch,
        compiler_params=pltpu.CompilerParams(vmem_limit_bytes=VMEM_BYTES),
        cost_estimate=pl.CostEstimate(flops=flops, bytes_accessed=moved, transcendentals=0),
        name=name,
    )(*operands)
    return result if len(out) > 1 else result[0]


def pseudo_by_sum(input_rows, input_factor, mode_freq, mode_damping, line_freq):
    lines = line_freq.shape[0]
    columns = input_factor.shape[1] // lines
    half = columns // 2
    forced = lax.psum(
        lax.dot_general(
            input_rows, input_factor, (((0,), (0,)), ((), ())), preferred_element_type=F32
        ),
        AXES,
    )
    pieces = []
    for line in range(lines):
        gain_real, gain_imag = modal_gain(mode_freq, mode_damping, line_freq[line])
        gain_real, gain_imag = gain_real[:, None], gain_imag[:, None]
        real = forced[:, line * columns : line * columns + half]
        imag = forced[:, line * columns + half : (line + 1) * columns]
        pieces.append(gain_real * real - gain_imag * imag)
        pieces.append(gain_real * imag + gain_imag * real)
    return jnp.concatenate(pieces, axis=1).astype(BF16)


def own_pseudo(input_rows, input_factor, mode_freq, mode_damping, line_freq, members):
    devices = math.prod(FAST_SHAPE)
    rows, modes = input_rows.shape
    width = input_factor.shape[1]
    lines = line_freq.shape[0]
    parts = modes // (devices // 2 * width)
    ones = call(ones_kernel, "ones", [((8, width), F32)], flops=LONG)
    sent = call(
        pack_kernel,
        "pack",
        [((devices, (parts + 1) * rows, width), BF16)],
        ones,
        input_rows,
        input_factor,
        flops=LONG,
    )
    got = lax.all_to_all(sent, AXES, 0, 0)
    return call(
        functools.partial(pseudo_kernel, rows=rows),
        "pseudo",
        [((members, width, width), BF16)],
        line_freq.reshape(1, lines),
        mode_freq.reshape(-1, width),
        mode_damping.reshape(-1, width),
        got,
        flops=LONG,
    )


def local(
    shape,
    mode_rows,
    input_rows,
    input_factor,
    mode_freq,
    mode_damping,
    line_freq,
    boundary_rows,
    connectivity,
    stress_coef,
):
    devices = math.prod(shape)
    rows, modes = mode_rows.shape
    width = input_factor.shape[1]
    lines = line_freq.shape[0]
    exports = boundary_rows.shape[0]
    rim = exports // 2
    elems = connectivity.shape[1]
    inputs = (input_rows, input_factor, mode_freq, mode_damping, line_freq)
    if shape == FAST_SHAPE and modes == devices * LANES and input_rows.shape[0] % 16 == 0:
        cycle = [place ^ (place // 2) for place in range(8)]
        groups = [[h * 16 + j * 2 + c for j in cycle for c in range(2)] for h in range(2)]
        block = own_pseudo(*inputs, members=16)
        got = lax.all_to_all(block, AXES, 0, 0, axis_index_groups=groups)
        mine = got.reshape(modes // 2, width)
        theirs = lax.ppermute(mine, AXES, [(i, i ^ 1) for i in range(devices)])
    else:
        pseudo = pseudo_by_sum(*inputs).reshape(2, modes // 2, width)
        core = lax.axis_index(AXES) % 2
        mine = lax.dynamic_index_in_dim(pseudo, core, 0, keepdims=False)
        theirs = lax.dynamic_index_in_dim(pseudo, 1 - core, 0, keepdims=False)
    total, part, picked = call(
        first_kernel,
        "first",
        [((rows, width), F32), ((exports, width), F32), ((exports, modes // 2), BF16)],
        boundary_rows.reshape(1, exports),
        mode_rows,
        mine,
        flops=rows * modes * (width + exports),
        scratch=[pltpu.VMEM((exports, rows), BF16)],
    )
    far, near = call(
        export_kernel,
        "export",
        [((rim, width), BF16)] * 2,
        part,
        picked,
        theirs,
        flops=exports * modes * width,
    )
    inner = [(i, i ^ 1) for i in range(devices)]
    outer = [(i, i + 1) for i in range(1, devices - 1, 2)]
    outer += [(j, i) for i, j in outer]
    near = lax.ppermute(near, AXES, inner)
    far = lax.ppermute(far, AXES, outer)
    stress, matrix = call(
        own_kernel,
        "own",
        [((width, elems), F32), ((2 * exports, elems), BF16)],
        connectivity,
        stress_coef,
        mode_rows,
        theirs,
        total,
        flops=rows * modes * width + 4 * rows * elems * width,
        scratch=[pltpu.VMEM((2, rows, elems), BF16), pltpu.VMEM((width, rows), BF16)],
    )
    return call(
        power_kernel,
        "power",
        [((lines, elems), F32)],
        stress,
        far,
        near,
        matrix,
        flops=4 * exports * elems * width,
    )


def solution(mesh):
    shape = tuple(mesh.shape[axis] for axis in AXES)
    placed = (
        P(AXES, None),
        P(AXES, None),
        P(AXES, None),
        P(),
        P(),
        P(),
        P(AXES),
        P(None, AXES),
        P(None, AXES),
    )
    return jax.shard_map(
        functools.partial(local, shape),
        mesh=mesh,
        in_specs=placed,
        out_specs=P(None, AXES),
        check_vma=False,
    )
```

```python
import functools
import math

import jax
import jax.numpy as jnp
from jax import lax
from jax.experimental import pallas as pl
from jax.experimental.pallas import tpu as pltpu
from jax.sharding import PartitionSpec as P

AXES = ("region", "sub")
LANES = 128
F32 = jnp.float32
BF16 = jnp.bfloat16
VMEM_BYTES = 24 * 1024 * 1024
LONG = 8 * 1024**3
FAST_SHAPE = (8, 4)


def whole(*_):
    return pl.BlockSpec(memory_space=pltpu.VMEM)


def modal_gain(freq, damping, omega):
    detune = freq * freq - omega * omega
    damped = 2.0 * damping * freq * omega
    magnitude = detune * detune + damped * damped
    return detune / magnitude, -damped / magnitude


def slab_of(device):
    chip = device // 2 % 8
    return device % 2 * 8 + (chip ^ (chip // 2) ^ (chip // 4))


def ones_kernel(ones_ref):
    ones_ref[...] = jnp.ones_like(ones_ref)


def pack_kernel(ones_ref, rows_ref, factor_ref, sent_ref):
    devices, _, width = sent_ref.shape
    rows = rows_ref.shape[0]
    parts = sent_ref.shape[1] // rows - 1
    factor = factor_ref[...] * ones_ref[0:1, :].astype(BF16)
    for device in range(devices):
        for part in range(parts):
            here = (slab_of(device) * parts + part) * width
            sent_ref[device, part * rows : (part + 1) * rows, :] = rows_ref[:, here : here + width]
        sent_ref[device, parts * rows :, :] = factor


def pseudo_kernel(line_ref, freq_ref, damping_ref, got_ref, pseudo_ref, *, rows):
    devices, tall, width = got_ref.shape
    parts = tall // rows - 1
    lines = line_ref.shape[1]
    columns = width // lines
    half = columns // 2
    slab = slab_of(lax.axis_index(AXES))
    factor = got_ref[:, parts * rows :, :].reshape(devices * rows, width)
    shapes = [
        got_ref[:, part * rows : (part + 1) * rows, :].reshape(devices * rows, width)
        for part in range(parts)
    ]
    forced = lax.dot_general(
        factor,
        jnp.concatenate(shapes, axis=1),
        (((0,), (0,)), ((), ())),
        preferred_element_type=F32,
    )
    for part in range(parts):
        here = pl.ds(slab * parts + part, 1)
        summed = forced[:, part * width : (part + 1) * width]
        pieces = []
        for line in range(lines):
            gain_real, gain_imag = modal_gain(
                freq_ref[here, :], damping_ref[here, :], line_ref[:, line : line + 1]
            )
            real = summed[line * columns : line * columns + half]
            imag = summed[line * columns + half : (line + 1) * columns]
            pieces.append(gain_real * real - gain_imag * imag)
            pieces.append(gain_real * imag + gain_imag * real)
        pseudo = jnp.concatenate(pieces, axis=0).T.astype(BF16)
        for copy in range(pseudo_ref.shape[0]):
            pseudo_ref[copy, part * width : (part + 1) * width, :] = pseudo


def for_core(depth, work):
    odd = lax.axis_index(AXES) % 2
    low, high = slice(0, depth), slice(depth, 2 * depth)
    pl.when(odd == 0)(lambda: work(low, high))
    pl.when(odd == 1)(lambda: work(high, low))


def first_kernel(boundary_ref, modes_ref, pseudo_ref, total_ref, part_ref, picked_ref, pick_ref):
    rows = modes_ref.shape[0]
    exports = boundary_ref.shape[1]
    chosen = jnp.broadcast_to(boundary_ref[...], (exports, exports)).astype(F32).T
    column = lax.broadcasted_iota(jnp.int32, (exports, exports), 1).astype(F32)
    pick_ref[...] = jnp.concatenate(
        [(column + start == chosen).astype(F32) for start in range(0, rows, exports)], axis=1
    ).astype(BF16)

    def work(mine, other):
        pick = pick_ref[...]
        picked_ref[...] = jnp.dot(
            pick, modes_ref[:, other], preferred_element_type=F32
        ).astype(BF16)
        total = jnp.dot(modes_ref[:, mine], pseudo_ref[...], preferred_element_type=F32)
        total_ref[...] = total
        high = total.astype(BF16)
        rest = total - high.astype(F32)
        middle = rest.astype(BF16)
        low = (rest - middle.astype(F32)).astype(BF16)
        parts = jnp.dot(
            pick, jnp.concatenate([high, middle, low], axis=1), preferred_element_type=F32
        )
        width = total.shape[1]
        part_ref[...] = parts[:, :width] + parts[:, width : 2 * width] + parts[:, 2 * width :]

    for_core(pseudo_ref.shape[0], work)


def export_kernel(part_ref, picked_ref, low_ref, high_ref, far_ref, near_ref):
    cut = low_ref.shape[0]
    export = part_ref[...] + jnp.dot(
        picked_ref[:, :cut], low_ref[...], preferred_element_type=F32
    )
    export = export + jnp.dot(picked_ref[:, cut:], high_ref[...], preferred_element_type=F32)
    export = export.astype(BF16)
    odd = lax.axis_index(AXES) % 2 == 1
    rim = far_ref.shape[0]
    far_ref[...] = jnp.where(odd, export[rim:], export[:rim])
    near_ref[...] = jnp.where(odd, export[:rim], export[rim:])


def own_kernel(
    connect_ref, coef_ref, modes_ref, low_ref, high_ref, total_ref,
    stress_ref, rim_ref, own_ref, table_ref,
):
    rows = modes_ref.shape[0]
    elems = connect_ref.shape[1]
    rim = rim_ref.shape[0] // 4
    odd = lax.axis_index(AXES) % 2

    cut = low_ref.shape[0]
    total = total_ref[...]
    for part, part_ref in enumerate((low_ref, high_ref)):
        here = pl.ds(pl.multiple_of((2 * (1 - odd) + part) * cut, cut), cut)
        total = total + jnp.dot(modes_ref[:, here], part_ref[...], preferred_element_type=F32)
    table_ref[...] = total.T.astype(BF16)

    def matrix(start, tall):
        node = lax.broadcasted_iota(jnp.int32, (tall, elems), 0) + start
        total = jnp.zeros((tall, elems), F32)
        for corner in range(connect_ref.shape[0]):
            hit = node == connect_ref[corner : corner + 1, :]
            total = total + jnp.where(hit, coef_ref[corner : corner + 1, :], 0.0)
        high = total.astype(BF16)
        return high, (total - high.astype(F32)).astype(BF16)

    after = rim + rows
    for place, start in ((0, after * odd), (1, after * (1 - odd))):
        high, low = matrix(start, rim)
        rim_ref[place * rim : (place + 1) * rim, :] = high
        rim_ref[(place + 2) * rim : (place + 3) * rim, :] = low
    for start in range(0, rows, rim):
        here = slice(start, start + rim)
        own_ref[0, here, :], own_ref[1, here, :] = matrix(start + rim, rim)
    table = table_ref[...]
    stress = jnp.dot(table, own_ref[0], preferred_element_type=F32)
    stress_ref[...] = stress + jnp.dot(table, own_ref[1], preferred_element_type=F32)


def power_kernel(stress_ref, far_ref, near_ref, rim_ref, power_ref):
    rows = [far_ref[...], near_ref[...]]
    stress = stress_ref[...] + lax.dot_general(
        jnp.concatenate(rows + rows, axis=0),
        rim_ref[...],
        (((0,), (0,)), ((), ())),
        preferred_element_type=F32,
    )
    squares = stress * stress
    lines = power_ref.shape[0]
    columns = squares.shape[0] // lines
    for line in range(lines):
        power_ref[line : line + 1, :] = (
            jnp.sum(squares[line * columns : (line + 1) * columns], axis=0, keepdims=True)
            / columns
        )


def call(kernel, name, out, *operands, flops, scratch=()):
    shapes = [jax.ShapeDtypeStruct(shape, dtype) for shape, dtype in out]
    moved = sum(x.size * x.dtype.itemsize for x in operands)
    moved += sum(math.prod(shape) * jnp.dtype(dtype).itemsize for shape, dtype in out)
    result = pl.pallas_call(
        kernel,
        out_shape=shapes,
        in_specs=[whole()] * len(operands),
        out_specs=[whole()] * len(out),
        scratch_shapes=scratch,
        compiler_params=pltpu.CompilerParams(vmem_limit_bytes=VMEM_BYTES),
        cost_estimate=pl.CostEstimate(flops=flops, bytes_accessed=moved, transcendentals=0),
        name=name,
    )(*operands)
    return result if len(out) > 1 else result[0]


def pseudo_by_sum(input_rows, input_factor, mode_freq, mode_damping, line_freq):
    lines = line_freq.shape[0]
    columns = input_factor.shape[1] // lines
    half = columns // 2
    forced = lax.psum(
        lax.dot_general(
            input_rows, input_factor, (((0,), (0,)), ((), ())), preferred_element_type=F32
        ),
        AXES,
    )
    pieces = []
    for line in range(lines):
        gain_real, gain_imag = modal_gain(mode_freq, mode_damping, line_freq[line])
        gain_real, gain_imag = gain_real[:, None], gain_imag[:, None]
        real = forced[:, line * columns : line * columns + half]
        imag = forced[:, line * columns + half : (line + 1) * columns]
        pieces.append(gain_real * real - gain_imag * imag)
        pieces.append(gain_real * imag + gain_imag * real)
    return jnp.concatenate(pieces, axis=1).astype(BF16)


def own_pseudo(input_rows, input_factor, mode_freq, mode_damping, line_freq, copies):
    devices = math.prod(FAST_SHAPE)
    rows, modes = input_rows.shape
    width = input_factor.shape[1]
    lines = line_freq.shape[0]
    parts = modes // (devices // 2 * width)
    ones = call(ones_kernel, "ones", [((8, width), F32)], flops=LONG)
    sent = call(
        pack_kernel,
        "pack",
        [((devices, (parts + 1) * rows, width), BF16)],
        ones,
        input_rows,
        input_factor,
        flops=LONG,
    )
    got = lax.all_to_all(sent, AXES, 0, 0)
    return call(
        functools.partial(pseudo_kernel, rows=rows),
        "pseudo",
        [((copies, parts * width, width), BF16)],
        line_freq.reshape(1, lines),
        mode_freq.reshape(-1, width),
        mode_damping.reshape(-1, width),
        got,
        flops=LONG,
    )


def local(
    shape,
    mode_rows,
    input_rows,
    input_factor,
    mode_freq,
    mode_damping,
    line_freq,
    boundary_rows,
    connectivity,
    stress_coef,
):
    devices = math.prod(shape)
    rows, modes = mode_rows.shape
    width = input_factor.shape[1]
    lines = line_freq.shape[0]
    exports = boundary_rows.shape[0]
    rim = exports // 2
    elems = connectivity.shape[1]
    inputs = (input_rows, input_factor, mode_freq, mode_damping, line_freq)
    if shape == FAST_SHAPE and modes == devices * LANES and input_rows.shape[0] % 16 == 0:
        cycle = [place ^ (place // 2) for place in range(8)]
        groups = [[h * 16 + j * 2 + c for j in cycle] for h in range(2) for c in range(2)]
        got = lax.all_to_all(own_pseudo(*inputs, copies=8), AXES, 0, 0, axis_index_groups=groups)
        mine = got.reshape(modes // 2, width)
        cut = modes // 4
        swap = [(i, i ^ 1) for i in range(devices)]
        theirs = [lax.ppermute(part, AXES, swap) for part in (mine[:cut], mine[cut:])]
    else:
        pseudo = pseudo_by_sum(*inputs).reshape(2, modes // 2, width)
        core = lax.axis_index(AXES) % 2
        mine = lax.dynamic_index_in_dim(pseudo, core, 0, keepdims=False)
        other = lax.dynamic_index_in_dim(pseudo, 1 - core, 0, keepdims=False)
        theirs = [other[: modes // 4], other[modes // 4 :]]
    total, part, picked = call(
        first_kernel,
        "first",
        [((rows, width), F32), ((exports, width), F32), ((exports, modes // 2), BF16)],
        boundary_rows.reshape(1, exports),
        mode_rows,
        mine,
        flops=rows * modes * (width + exports),
        scratch=[pltpu.VMEM((exports, rows), BF16)],
    )
    far, near = call(
        export_kernel,
        "export",
        [((rim, width), BF16)] * 2,
        part,
        picked,
        *theirs,
        flops=exports * modes * width,
    )
    inner = [(i, i ^ 1) for i in range(devices)]
    outer = [(i, i + 1) for i in range(1, devices - 1, 2)]
    outer += [(j, i) for i, j in outer]
    near = lax.ppermute(near, AXES, inner)
    far = lax.ppermute(far, AXES, outer)
    stress, matrix = call(
        own_kernel,
        "own",
        [((width, elems), F32), ((2 * exports, elems), BF16)],
        connectivity,
        stress_coef,
        mode_rows,
        *theirs,
        total,
        flops=rows * modes * width + 4 * rows * elems * width,
        scratch=[pltpu.VMEM((2, rows, elems), BF16), pltpu.VMEM((width, rows), BF16)],
    )
    return call(
        power_kernel,
        "power",
        [((lines, elems), F32)],
        stress,
        far,
        near,
        matrix,
        flops=4 * exports * elems * width,
    )


def solution(mesh):
    shape = tuple(mesh.shape[axis] for axis in AXES)
    placed = (
        P(AXES, None),
        P(AXES, None),
        P(AXES, None),
        P(),
        P(),
        P(),
        P(AXES),
        P(None, AXES),
        P(None, AXES),
    )
    return jax.shard_map(
        functools.partial(local, shape),
        mesh=mesh,
        in_specs=placed,
        out_specs=P(None, AXES),
        check_vma=False,
    )
```

```python
import functools
import math

import jax
import jax.numpy as jnp
from jax import lax
from jax.experimental import pallas as pl
from jax.experimental.pallas import tpu as pltpu
from jax.sharding import PartitionSpec as P

AXES = ("region", "sub")
LANES = 128
F32 = jnp.float32
BF16 = jnp.bfloat16
VMEM_BYTES = 24 * 1024 * 1024
LONG = 8 * 1024**3
FAST_SHAPE = (8, 4)


def whole(*_):
    return pl.BlockSpec(memory_space=pltpu.VMEM)


def modal_gain(freq, damping, omega):
    detune = freq * freq - omega * omega
    damped = 2.0 * damping * freq * omega
    magnitude = detune * detune + damped * damped
    return detune / magnitude, -damped / magnitude


def slab_of(device):
    chip = device // 2 % 8
    return device % 2 * 8 + (chip ^ (chip // 2) ^ (chip // 4))


def ones_kernel(ones_ref):
    ones_ref[...] = jnp.ones_like(ones_ref)


def pack_kernel(ones_ref, rows_ref, factor_ref, sent_ref):
    devices, _, width = sent_ref.shape
    rows = rows_ref.shape[0]
    parts = sent_ref.shape[1] // rows - 1
    factor = factor_ref[...] * ones_ref[0:1, :].astype(BF16)
    for device in range(devices):
        for part in range(parts):
            here = (slab_of(device) * parts + part) * width
            sent_ref[device, part * rows : (part + 1) * rows, :] = rows_ref[:, here : here + width]
        sent_ref[device, parts * rows :, :] = factor


def pseudo_kernel(line_ref, freq_ref, damping_ref, got_ref, pseudo_ref, *, rows):
    devices, tall, width = got_ref.shape
    parts = tall // rows - 1
    lines = line_ref.shape[1]
    columns = width // lines
    half = columns // 2
    slab = slab_of(lax.axis_index(AXES))
    factor = got_ref[:, parts * rows :, :].reshape(devices * rows, width)
    shapes = [
        got_ref[:, part * rows : (part + 1) * rows, :].reshape(devices * rows, width)
        for part in range(parts)
    ]
    forced = lax.dot_general(
        factor,
        jnp.concatenate(shapes, axis=1),
        (((0,), (0,)), ((), ())),
        preferred_element_type=F32,
    )
    for part in range(parts):
        here = pl.ds(slab * parts + part, 1)
        summed = forced[:, part * width : (part + 1) * width]
        pieces = []
        for line in range(lines):
            gain_real, gain_imag = modal_gain(
                freq_ref[here, :], damping_ref[here, :], line_ref[:, line : line + 1]
            )
            real = summed[line * columns : line * columns + half]
            imag = summed[line * columns + half : (line + 1) * columns]
            pieces.append(gain_real * real - gain_imag * imag)
            pieces.append(gain_real * imag + gain_imag * real)
        pseudo = jnp.concatenate(pieces, axis=0).astype(BF16).T
        for copy in range(pseudo_ref.shape[0]):
            pseudo_ref[copy, part * width : (part + 1) * width, :] = pseudo


def for_core(depth, work):
    odd = lax.axis_index(AXES) % 2
    low, high = slice(0, depth), slice(depth, 2 * depth)
    pl.when(odd == 0)(lambda: work(low, high))
    pl.when(odd == 1)(lambda: work(high, low))


def first_kernel(boundary_ref, modes_ref, pseudo_ref, total_ref, part_ref, picked_ref, pick_ref):
    rows = modes_ref.shape[0]
    exports = boundary_ref.shape[1]
    chosen = jnp.broadcast_to(boundary_ref[...], (exports, exports)).astype(F32).T
    column = lax.broadcasted_iota(jnp.int32, (exports, exports), 1).astype(F32)
    pick_ref[...] = jnp.concatenate(
        [(column + start == chosen).astype(F32) for start in range(0, rows, exports)], axis=1
    ).astype(BF16)

    def product(mine, _):
        total_ref[...] = jnp.dot(modes_ref[:, mine], pseudo_ref[...], preferred_element_type=F32)

    def exported(_, other):
        pick = pick_ref[...]
        total = total_ref[...]
        high = total.astype(BF16)
        rest = total - high.astype(F32)
        middle = rest.astype(BF16)
        low = (rest - middle.astype(F32)).astype(BF16)
        parts = jnp.dot(
            pick, jnp.concatenate([high, middle, low], axis=1), preferred_element_type=F32
        )
        width = total.shape[1]
        part_ref[...] = parts[:, :width] + parts[:, width : 2 * width] + parts[:, 2 * width :]
        picked_ref[...] = jnp.dot(
            pick, modes_ref[:, other], preferred_element_type=F32
        ).astype(BF16)

    for_core(pseudo_ref.shape[0], product)
    for_core(pseudo_ref.shape[0], exported)


def export_kernel(part_ref, picked_ref, pseudo_ref, far_ref, near_ref):
    exports = part_ref.shape[0]
    cut = pseudo_ref.shape[0] // 2
    width = pseudo_ref.shape[1]
    both = jnp.dot(
        jnp.concatenate([picked_ref[:, :cut], picked_ref[:, cut:]], axis=0),
        jnp.concatenate([pseudo_ref[:cut], pseudo_ref[cut:]], axis=1),
        preferred_element_type=F32,
    )
    export = part_ref[...] + both[:exports, :width] + both[exports:, width:]
    export = export.astype(BF16)
    odd = lax.axis_index(AXES) % 2 == 1
    rim = far_ref.shape[0]
    far_ref[...] = jnp.where(odd, export[rim:], export[:rim])
    near_ref[...] = jnp.where(odd, export[:rim], export[rim:])


def own_kernel(
    connect_ref, coef_ref, modes_ref, pseudo_ref, total_ref, stress_ref, rim_ref, own_ref, table_ref
):
    rows = modes_ref.shape[0]
    elems = connect_ref.shape[1]
    rim = rim_ref.shape[0] // 4
    odd = lax.axis_index(AXES) % 2

    depth = pseudo_ref.shape[0]
    other = pl.ds(pl.multiple_of((1 - odd) * depth, depth), depth)
    total = total_ref[...] + jnp.dot(
        modes_ref[:, other], pseudo_ref[...], preferred_element_type=F32
    )
    table_ref[...] = total.astype(BF16).T

    def matrix(start, tall):
        node = lax.broadcasted_iota(jnp.int32, (tall, elems), 0) + start
        total = jnp.zeros((tall, elems), F32)
        for corner in range(connect_ref.shape[0]):
            hit = node == connect_ref[corner : corner + 1, :]
            total = total + jnp.where(hit, coef_ref[corner : corner + 1, :], 0.0)
        high = total.astype(BF16)
        return high, (total - high.astype(F32)).astype(BF16)

    after = rim + rows
    for place, start in ((0, after * odd), (1, after * (1 - odd))):
        high, low = matrix(start, rim)
        rim_ref[place * rim : (place + 1) * rim, :] = high
        rim_ref[(place + 2) * rim : (place + 3) * rim, :] = low
    for start in range(0, rows, rim):
        here = slice(start, start + rim)
        own_ref[0, here, :], own_ref[1, here, :] = matrix(start + rim, rim)
    table = table_ref[...]
    stress = jnp.dot(table, own_ref[0], preferred_element_type=F32)
    stress_ref[...] = stress + jnp.dot(table, own_ref[1], preferred_element_type=F32)


def power_kernel(stress_ref, far_ref, near_ref, rim_ref, power_ref):
    rows = jnp.concatenate([far_ref[...], near_ref[...]], axis=0).T
    stress = stress_ref[...] + jnp.dot(
        jnp.concatenate([rows, rows], axis=1), rim_ref[...], preferred_element_type=F32
    )
    squares = stress * stress
    lines = power_ref.shape[0]
    columns = squares.shape[0] // lines
    for line in range(lines):
        power_ref[line : line + 1, :] = (
            jnp.sum(squares[line * columns : (line + 1) * columns], axis=0, keepdims=True)
            / columns
        )


def call(kernel, name, out, *operands, flops, scratch=()):
    shapes = [jax.ShapeDtypeStruct(shape, dtype) for shape, dtype in out]
    moved = sum(x.size * x.dtype.itemsize for x in operands)
    moved += sum(math.prod(shape) * jnp.dtype(dtype).itemsize for shape, dtype in out)
    result = pl.pallas_call(
        kernel,
        out_shape=shapes,
        in_specs=[whole()] * len(operands),
        out_specs=[whole()] * len(out),
        scratch_shapes=scratch,
        compiler_params=pltpu.CompilerParams(vmem_limit_bytes=VMEM_BYTES),
        cost_estimate=pl.CostEstimate(flops=flops, bytes_accessed=moved, transcendentals=0),
        name=name,
    )(*operands)
    return result if len(out) > 1 else result[0]


def pseudo_by_sum(input_rows, input_factor, mode_freq, mode_damping, line_freq):
    lines = line_freq.shape[0]
    columns = input_factor.shape[1] // lines
    half = columns // 2
    forced = lax.psum(
        lax.dot_general(
            input_rows, input_factor, (((0,), (0,)), ((), ())), preferred_element_type=F32
        ),
        AXES,
    )
    pieces = []
    for line in range(lines):
        gain_real, gain_imag = modal_gain(mode_freq, mode_damping, line_freq[line])
        gain_real, gain_imag = gain_real[:, None], gain_imag[:, None]
        real = forced[:, line * columns : line * columns + half]
        imag = forced[:, line * columns + half : (line + 1) * columns]
        pieces.append(gain_real * real - gain_imag * imag)
        pieces.append(gain_real * imag + gain_imag * real)
    return jnp.concatenate(pieces, axis=1).astype(BF16)


def own_pseudo(input_rows, input_factor, mode_freq, mode_damping, line_freq, copies):
    devices = math.prod(FAST_SHAPE)
    rows, modes = input_rows.shape
    width = input_factor.shape[1]
    lines = line_freq.shape[0]
    parts = modes // (devices // 2 * width)
    ones = call(ones_kernel, "ones", [((8, width), F32)], flops=LONG)
    sent = call(
        pack_kernel,
        "pack",
        [((devices, (parts + 1) * rows, width), BF16)],
        ones,
        input_rows,
        input_factor,
        flops=LONG,
    )
    got = lax.all_to_all(sent, AXES, 0, 0)
    return call(
        functools.partial(pseudo_kernel, rows=rows),
        "pseudo",
        [((copies, parts * width, width), BF16)],
        line_freq.reshape(1, lines),
        mode_freq.reshape(-1, width),
        mode_damping.reshape(-1, width),
        got,
        flops=LONG,
    )


def local(
    shape,
    mode_rows,
    input_rows,
    input_factor,
    mode_freq,
    mode_damping,
    line_freq,
    boundary_rows,
    connectivity,
    stress_coef,
):
    devices = math.prod(shape)
    rows, modes = mode_rows.shape
    width = input_factor.shape[1]
    lines = line_freq.shape[0]
    exports = boundary_rows.shape[0]
    rim = exports // 2
    elems = connectivity.shape[1]
    inputs = (input_rows, input_factor, mode_freq, mode_damping, line_freq)
    if shape == FAST_SHAPE and modes == devices * LANES and input_rows.shape[0] % 16 == 0:
        cycle = [place ^ (place // 2) for place in range(8)]
        groups = [[h * 16 + j * 2 + c for j in cycle] for h in range(2) for c in range(2)]
        got = lax.all_to_all(own_pseudo(*inputs, copies=8), AXES, 0, 0, axis_index_groups=groups)
        mine = got.reshape(modes // 2, width)
        theirs = lax.ppermute(mine, AXES, [(i, i ^ 1) for i in range(devices)])
    else:
        pseudo = pseudo_by_sum(*inputs).reshape(2, modes // 2, width)
        core = lax.axis_index(AXES) % 2
        mine = lax.dynamic_index_in_dim(pseudo, core, 0, keepdims=False)
        theirs = lax.dynamic_index_in_dim(pseudo, 1 - core, 0, keepdims=False)
    total, part, picked = call(
        first_kernel,
        "first",
        [((rows, width), F32), ((exports, width), F32), ((exports, modes // 2), BF16)],
        boundary_rows.reshape(1, exports),
        mode_rows,
        mine,
        flops=rows * modes * (width + exports),
        scratch=[pltpu.VMEM((exports, rows), BF16)],
    )
    far, near = call(
        export_kernel,
        "export",
        [((rim, width), BF16)] * 2,
        part,
        picked,
        theirs,
        flops=exports * modes * width,
    )
    inner = [(i, i ^ 1) for i in range(devices)]
    outer = [(i, i + 1) for i in range(1, devices - 1, 2)]
    outer += [(j, i) for i, j in outer]
    near = lax.ppermute(near, AXES, inner)
    far = lax.ppermute(far, AXES, outer)
    stress, matrix = call(
        own_kernel,
        "own",
        [((width, elems), F32), ((2 * exports, elems), BF16)],
        connectivity,
        stress_coef,
        mode_rows,
        theirs,
        total,
        flops=rows * modes * width + 4 * rows * elems * width,
        scratch=[pltpu.VMEM((2, rows, elems), BF16), pltpu.VMEM((width, rows), BF16)],
    )
    return call(
        power_kernel,
        "power",
        [((lines, elems), F32)],
        stress,
        far,
        near,
        matrix,
        flops=4 * exports * elems * width,
    )


def solution(mesh):
    shape = tuple(mesh.shape[axis] for axis in AXES)
    placed = (
        P(AXES, None),
        P(AXES, None),
        P(AXES, None),
        P(),
        P(),
        P(),
        P(AXES),
        P(None, AXES),
        P(None, AXES),
    )
    return jax.shard_map(
        functools.partial(local, shape),
        mesh=mesh,
        in_specs=placed,
        out_specs=P(None, AXES),
        check_vma=False,
    )
```

```python
import functools
import math

import jax
import jax.numpy as jnp
from jax import lax
from jax.experimental import pallas as pl
from jax.experimental.pallas import tpu as pltpu
from jax.sharding import PartitionSpec as P

AXES = ("region", "sub")
LANES = 128
F32 = jnp.float32
BF16 = jnp.bfloat16
VMEM_BYTES = 24 * 1024 * 1024
LONG = 8 * 1024**3
FAST_SHAPE = (8, 4)


def whole(*_):
    return pl.BlockSpec(memory_space=pltpu.VMEM)


def modal_gain(freq, damping, omega):
    detune = freq * freq - omega * omega
    damped = 2.0 * damping * freq * omega
    magnitude = detune * detune + damped * damped
    return detune / magnitude, -damped / magnitude


def slab_of(device):
    chip = device // 2 % 8
    step = chip % 2 + chip // 4 * 2 + chip // 2 % 2 * 4
    return device % 2 * 8 + (step ^ (step // 2) ^ (step // 4))


def ones_kernel(ones_ref):
    ones_ref[...] = jnp.ones_like(ones_ref)


def pack_kernel(ones_ref, rows_ref, factor_ref, sent_ref):
    devices, _, width = sent_ref.shape
    rows = rows_ref.shape[0]
    parts = sent_ref.shape[1] // rows - 1
    factor = factor_ref[...] * ones_ref[0:1, :].astype(BF16)
    for device in range(devices):
        for part in range(parts):
            here = (slab_of(device) * parts + part) * width
            sent_ref[device, part * rows : (part + 1) * rows, :] = rows_ref[:, here : here + width]
        sent_ref[device, parts * rows :, :] = factor


def pseudo_kernel(line_ref, freq_ref, damping_ref, got_ref, pseudo_ref, *, rows):
    devices, tall, width = got_ref.shape
    parts = tall // rows - 1
    lines = line_ref.shape[1]
    columns = width // lines
    half = columns // 2
    slab = slab_of(lax.axis_index(AXES))
    factor = got_ref[:, parts * rows :, :].reshape(devices * rows, width)
    shapes = [
        got_ref[:, part * rows : (part + 1) * rows, :].reshape(devices * rows, width)
        for part in range(parts)
    ]
    forced = lax.dot_general(
        factor,
        jnp.concatenate(shapes, axis=1),
        (((0,), (0,)), ((), ())),
        preferred_element_type=F32,
    )
    for part in range(parts):
        here = pl.ds(slab * parts + part, 1)
        summed = forced[:, part * width : (part + 1) * width]
        pieces = []
        for line in range(lines):
            gain_real, gain_imag = modal_gain(
                freq_ref[here, :], damping_ref[here, :], line_ref[:, line : line + 1]
            )
            real = summed[line * columns : line * columns + half]
            imag = summed[line * columns + half : (line + 1) * columns]
            pieces.append(gain_real * real - gain_imag * imag)
            pieces.append(gain_real * imag + gain_imag * real)
        pseudo = jnp.concatenate(pieces, axis=0).T.astype(BF16)
        for copy in range(pseudo_ref.shape[0]):
            pseudo_ref[copy, part * width : (part + 1) * width, :] = pseudo


def for_core(depth, work):
    odd = lax.axis_index(AXES) % 2
    low, high = slice(0, depth), slice(depth, 2 * depth)
    pl.when(odd == 0)(lambda: work(low, high))
    pl.when(odd == 1)(lambda: work(high, low))


def first_kernel(boundary_ref, modes_ref, pseudo_ref, total_ref, part_ref, picked_ref, pick_ref):
    rows = modes_ref.shape[0]
    exports = boundary_ref.shape[1]
    chosen = jnp.broadcast_to(boundary_ref[...], (exports, exports)).astype(F32).T
    column = lax.broadcasted_iota(jnp.int32, (exports, exports), 1).astype(F32)
    pick_ref[...] = jnp.concatenate(
        [(column + start == chosen).astype(F32) for start in range(0, rows, exports)], axis=1
    ).astype(BF16)

    def product(mine, _):
        total_ref[...] = jnp.dot(modes_ref[:, mine], pseudo_ref[...], preferred_element_type=F32)

    def exported(_, other):
        pick = pick_ref[...]
        total = total_ref[...]
        high = total.astype(BF16)
        rest = total - high.astype(F32)
        middle = rest.astype(BF16)
        low = (rest - middle.astype(F32)).astype(BF16)
        parts = jnp.dot(
            pick, jnp.concatenate([high, middle, low], axis=1), preferred_element_type=F32
        )
        width = total.shape[1]
        part_ref[...] = parts[:, :width] + parts[:, width : 2 * width] + parts[:, 2 * width :]
        picked_ref[...] = jnp.dot(
            pick, modes_ref[:, other], preferred_element_type=F32
        ).astype(BF16)

    for_core(pseudo_ref.shape[0], product)
    for_core(pseudo_ref.shape[0], exported)


def export_kernel(part_ref, picked_ref, pseudo_ref, far_ref, near_ref):
    exports = part_ref.shape[0]
    cut = pseudo_ref.shape[0] // 2
    width = pseudo_ref.shape[1]
    both = jnp.dot(
        jnp.concatenate([picked_ref[:, :cut], picked_ref[:, cut:]], axis=0),
        jnp.concatenate([pseudo_ref[:cut], pseudo_ref[cut:]], axis=1),
        preferred_element_type=F32,
    )
    export = part_ref[...] + both[:exports, :width] + both[exports:, width:]
    export = export.astype(BF16)
    odd = lax.axis_index(AXES) % 2 == 1
    rim = far_ref.shape[0]
    far_ref[...] = jnp.where(odd, export[rim:], export[:rim])
    near_ref[...] = jnp.where(odd, export[:rim], export[rim:])


def own_kernel(
    connect_ref, coef_ref, modes_ref, pseudo_ref, total_ref, stress_ref, rim_ref, own_ref, table_ref
):
    rows = modes_ref.shape[0]
    elems = connect_ref.shape[1]
    rim = rim_ref.shape[0] // 4
    odd = lax.axis_index(AXES) % 2

    depth = pseudo_ref.shape[0]
    other = pl.ds(pl.multiple_of((1 - odd) * depth, depth), depth)
    total = total_ref[...] + jnp.dot(
        modes_ref[:, other], pseudo_ref[...], preferred_element_type=F32
    )
    table_ref[...] = total.T.astype(BF16)

    def matrix(start, tall):
        node = lax.broadcasted_iota(jnp.int32, (tall, elems), 0) + start
        total = jnp.zeros((tall, elems), F32)
        for corner in range(connect_ref.shape[0]):
            hit = node == connect_ref[corner : corner + 1, :]
            total = total + jnp.where(hit, coef_ref[corner : corner + 1, :], 0.0)
        high = total.astype(BF16)
        return high, (total - high.astype(F32)).astype(BF16)

    after = rim + rows
    for place, start in ((0, after * odd), (1, after * (1 - odd))):
        high, low = matrix(start, rim)
        rim_ref[place * rim : (place + 1) * rim, :] = high
        rim_ref[(place + 2) * rim : (place + 3) * rim, :] = low
    for start in range(0, rows, rim):
        here = slice(start, start + rim)
        own_ref[0, here, :], own_ref[1, here, :] = matrix(start + rim, rim)
    table = table_ref[...]
    stress = jnp.dot(table, own_ref[0], preferred_element_type=F32)
    stress_ref[...] = stress + jnp.dot(table, own_ref[1], preferred_element_type=F32)


def power_kernel(stress_ref, far_ref, near_ref, rim_ref, power_ref):
    rows = [far_ref[...], near_ref[...]]
    stress = stress_ref[...] + lax.dot_general(
        jnp.concatenate(rows + rows, axis=0),
        rim_ref[...],
        (((0,), (0,)), ((), ())),
        preferred_element_type=F32,
    )
    squares = stress * stress
    lines = power_ref.shape[0]
    columns = squares.shape[0] // lines
    for line in range(lines):
        power_ref[line : line + 1, :] = (
            jnp.sum(squares[line * columns : (line + 1) * columns], axis=0, keepdims=True)
            / columns
        )


def call(kernel, name, out, *operands, flops, scratch=()):
    shapes = [jax.ShapeDtypeStruct(shape, dtype) for shape, dtype in out]
    moved = sum(x.size * x.dtype.itemsize for x in operands)
    moved += sum(math.prod(shape) * jnp.dtype(dtype).itemsize for shape, dtype in out)
    result = pl.pallas_call(
        kernel,
        out_shape=shapes,
        in_specs=[whole()] * len(operands),
        out_specs=[whole()] * len(out),
        scratch_shapes=scratch,
        compiler_params=pltpu.CompilerParams(vmem_limit_bytes=VMEM_BYTES),
        cost_estimate=pl.CostEstimate(flops=flops, bytes_accessed=moved, transcendentals=0),
        name=name,
    )(*operands)
    return result if len(out) > 1 else result[0]


def pseudo_by_sum(input_rows, input_factor, mode_freq, mode_damping, line_freq):
    lines = line_freq.shape[0]
    columns = input_factor.shape[1] // lines
    half = columns // 2
    forced = lax.psum(
        lax.dot_general(
            input_rows, input_factor, (((0,), (0,)), ((), ())), preferred_element_type=F32
        ),
        AXES,
    )
    pieces = []
    for line in range(lines):
        gain_real, gain_imag = modal_gain(mode_freq, mode_damping, line_freq[line])
        gain_real, gain_imag = gain_real[:, None], gain_imag[:, None]
        real = forced[:, line * columns : line * columns + half]
        imag = forced[:, line * columns + half : (line + 1) * columns]
        pieces.append(gain_real * real - gain_imag * imag)
        pieces.append(gain_real * imag + gain_imag * real)
    return jnp.concatenate(pieces, axis=1).astype(BF16)


def own_pseudo(input_rows, input_factor, mode_freq, mode_damping, line_freq, copies):
    devices = math.prod(FAST_SHAPE)
    rows, modes = input_rows.shape
    width = input_factor.shape[1]
    lines = line_freq.shape[0]
    parts = modes // (devices // 2 * width)
    ones = call(ones_kernel, "ones", [((8, width), F32)], flops=LONG)
    sent = call(
        pack_kernel,
        "pack",
        [((devices, (parts + 1) * rows, width), BF16)],
        ones,
        input_rows,
        input_factor,
        flops=LONG,
    )
    got = lax.all_to_all(sent, AXES, 0, 0)
    return call(
        functools.partial(pseudo_kernel, rows=rows),
        "pseudo",
        [((copies, parts * width, width), BF16)],
        line_freq.reshape(1, lines),
        mode_freq.reshape(-1, width),
        mode_damping.reshape(-1, width),
        got,
        flops=LONG,
    )


def local(
    shape,
    mode_rows,
    input_rows,
    input_factor,
    mode_freq,
    mode_damping,
    line_freq,
    boundary_rows,
    connectivity,
    stress_coef,
):
    devices = math.prod(shape)
    rows, modes = mode_rows.shape
    width = input_factor.shape[1]
    lines = line_freq.shape[0]
    exports = boundary_rows.shape[0]
    rim = exports // 2
    elems = connectivity.shape[1]
    inputs = (input_rows, input_factor, mode_freq, mode_damping, line_freq)
    if shape == FAST_SHAPE and modes == devices * LANES and input_rows.shape[0] % 16 == 0:
        cycle = [0, 1, 5, 4, 6, 7, 3, 2]
        groups = [[h * 16 + j * 2 + c for j in cycle] for h in range(2) for c in range(2)]
        got = lax.all_to_all(own_pseudo(*inputs, copies=8), AXES, 0, 0, axis_index_groups=groups)
        mine = got.reshape(modes // 2, width)
        theirs = lax.ppermute(mine, AXES, [(i, i ^ 1) for i in range(devices)])
    else:
        pseudo = pseudo_by_sum(*inputs).reshape(2, modes // 2, width)
        core = lax.axis_index(AXES) % 2
        mine = lax.dynamic_index_in_dim(pseudo, core, 0, keepdims=False)
        theirs = lax.dynamic_index_in_dim(pseudo, 1 - core, 0, keepdims=False)
    total, part, picked = call(
        first_kernel,
        "first",
        [((rows, width), F32), ((exports, width), F32), ((exports, modes // 2), BF16)],
        boundary_rows.reshape(1, exports),
        mode_rows,
        mine,
        flops=rows * modes * (width + exports),
        scratch=[pltpu.VMEM((exports, rows), BF16)],
    )
    far, near = call(
        export_kernel,
        "export",
        [((rim, width), BF16)] * 2,
        part,
        picked,
        theirs,
        flops=exports * modes * width,
    )
    inner = [(i, i ^ 1) for i in range(devices)]
    outer = [(i, i + 1) for i in range(1, devices - 1, 2)]
    outer += [(j, i) for i, j in outer]
    near = lax.ppermute(near, AXES, inner)
    far = lax.ppermute(far, AXES, outer)
    stress, matrix = call(
        own_kernel,
        "own",
        [((width, elems), F32), ((2 * exports, elems), BF16)],
        connectivity,
        stress_coef,
        mode_rows,
        theirs,
        total,
        flops=rows * modes * width + 4 * rows * elems * width,
        scratch=[pltpu.VMEM((2, rows, elems), BF16), pltpu.VMEM((width, rows), BF16)],
    )
    return call(
        power_kernel,
        "power",
        [((lines, elems), F32)],
        stress,
        far,
        near,
        matrix,
        flops=4 * exports * elems * width,
    )


def solution(mesh):
    shape = tuple(mesh.shape[axis] for axis in AXES)
    placed = (
        P(AXES, None),
        P(AXES, None),
        P(AXES, None),
        P(),
        P(),
        P(),
        P(AXES),
        P(None, AXES),
        P(None, AXES),
    )
    return jax.shard_map(
        functools.partial(local, shape),
        mesh=mesh,
        in_specs=placed,
        out_specs=P(None, AXES),
        check_vma=False,
    )
```

```python
import functools
import math

import jax
import jax.numpy as jnp
from jax import lax
from jax.experimental import pallas as pl
from jax.experimental.pallas import tpu as pltpu
from jax.sharding import PartitionSpec as P

AXES = ("region", "sub")
LANES = 128
F32 = jnp.float32
BF16 = jnp.bfloat16
VMEM_BYTES = 24 * 1024 * 1024
LONG = 8 * 1024**3
FAST_SHAPE = (8, 4)


def whole(*_):
    return pl.BlockSpec(memory_space=pltpu.VMEM)


def modal_gain(freq, damping, omega):
    detune = freq * freq - omega * omega
    damped = 2.0 * damping * freq * omega
    magnitude = detune * detune + damped * damped
    return detune / magnitude, -damped / magnitude


def slab_of(device):
    chip = device // 2 % 8
    return device % 2 * 8 + (chip ^ (chip // 2) ^ (chip // 4))


def ones_kernel(ones_ref):
    ones_ref[...] = jnp.ones_like(ones_ref)


def pack_kernel(ones_ref, rows_ref, factor_ref, sent_ref):
    devices, _, width = sent_ref.shape
    rows = rows_ref.shape[0]
    parts = sent_ref.shape[1] // rows - 1
    factor = factor_ref[...] * ones_ref[0:1, :].astype(BF16)
    for device in range(devices):
        for part in range(parts):
            here = (slab_of(device) * parts + part) * width
            sent_ref[device, part * rows : (part + 1) * rows, :] = rows_ref[:, here : here + width]
        sent_ref[device, parts * rows :, :] = factor


def pseudo_kernel(line_ref, freq_ref, damping_ref, got_ref, pseudo_ref, *, rows):
    devices, tall, width = got_ref.shape
    parts = tall // rows - 1
    lines = line_ref.shape[1]
    columns = width // lines
    half = columns // 2
    slab = slab_of(lax.axis_index(AXES))
    factor = got_ref[:, parts * rows :, :].reshape(devices * rows, width)
    shapes = [
        got_ref[:, part * rows : (part + 1) * rows, :].reshape(devices * rows, width)
        for part in range(parts)
    ]
    forced = lax.dot_general(
        factor,
        jnp.concatenate(shapes, axis=1),
        (((0,), (0,)), ((), ())),
        preferred_element_type=F32,
    )
    for part in range(parts):
        here = pl.ds(slab * parts + part, 1)
        summed = forced[:, part * width : (part + 1) * width]
        pieces = []
        for line in range(lines):
            gain_real, gain_imag = modal_gain(
                freq_ref[here, :], damping_ref[here, :], line_ref[:, line : line + 1]
            )
            real = summed[line * columns : line * columns + half]
            imag = summed[line * columns + half : (line + 1) * columns]
            pieces.append(gain_real * real - gain_imag * imag)
            pieces.append(gain_real * imag + gain_imag * real)
        pseudo = jnp.concatenate(pieces, axis=0).T.astype(BF16)
        for copy in range(pseudo_ref.shape[0]):
            pseudo_ref[copy, part * width : (part + 1) * width, :] = pseudo


def for_core(depth, work):
    odd = lax.axis_index(AXES) % 2
    low, high = slice(0, depth), slice(depth, 2 * depth)
    pl.when(odd == 0)(lambda: work(low, high))
    pl.when(odd == 1)(lambda: work(high, low))


def first_kernel(boundary_ref, modes_ref, pseudo_ref, total_ref, part_ref, picked_ref, pick_ref):
    rows = modes_ref.shape[0]
    exports = boundary_ref.shape[1]
    odd = lax.axis_index(AXES) % 2
    rim = exports // 2
    listed = boundary_ref[...]
    turned = jnp.concatenate([listed[:, rim:], listed[:, :rim]], axis=1)
    listed = jnp.where(odd == 1, turned, listed)
    chosen = jnp.broadcast_to(listed, (exports, exports)).astype(F32).T
    column = lax.broadcasted_iota(jnp.int32, (exports, exports), 1).astype(F32)
    pick_ref[...] = jnp.concatenate(
        [(column + start == chosen).astype(F32) for start in range(0, rows, exports)], axis=1
    ).astype(BF16)

    def product(mine, _):
        total_ref[...] = jnp.dot(modes_ref[:, mine], pseudo_ref[...], preferred_element_type=F32)

    def exported(_, other):
        pick = pick_ref[...]
        total = total_ref[...]
        high = total.astype(BF16)
        rest = total - high.astype(F32)
        middle = rest.astype(BF16)
        low = (rest - middle.astype(F32)).astype(BF16)
        parts = jnp.dot(
            pick, jnp.concatenate([high, middle, low], axis=1), preferred_element_type=F32
        )
        width = total.shape[1]
        part_ref[...] = parts[:, :width] + parts[:, width : 2 * width] + parts[:, 2 * width :]
        picked_ref[...] = jnp.dot(
            pick, modes_ref[:, other], preferred_element_type=F32
        ).astype(BF16)

    for_core(pseudo_ref.shape[0], product)
    for_core(pseudo_ref.shape[0], exported)


def export_kernel(part_ref, picked_ref, pseudo_ref, export_ref, *, start):
    here = slice(start, start + export_ref.shape[0])
    export_ref[...] = (
        part_ref[here, :]
        + jnp.dot(picked_ref[here, :], pseudo_ref[...], preferred_element_type=F32)
    ).astype(BF16)


def own_kernel(
    connect_ref, coef_ref, modes_ref, pseudo_ref, total_ref, stress_ref, rim_ref, own_ref, table_ref
):
    rows = modes_ref.shape[0]
    elems = connect_ref.shape[1]
    rim = rim_ref.shape[0] // 4
    odd = lax.axis_index(AXES) % 2

    depth = pseudo_ref.shape[0]
    other = pl.ds(pl.multiple_of((1 - odd) * depth, depth), depth)
    total = total_ref[...] + jnp.dot(
        modes_ref[:, other], pseudo_ref[...], preferred_element_type=F32
    )
    table_ref[...] = total.T.astype(BF16)

    def matrix(start, tall):
        node = lax.broadcasted_iota(jnp.int32, (tall, elems), 0) + start
        total = jnp.zeros((tall, elems), F32)
        for corner in range(connect_ref.shape[0]):
            hit = node == connect_ref[corner : corner + 1, :]
            total = total + jnp.where(hit, coef_ref[corner : corner + 1, :], 0.0)
        high = total.astype(BF16)
        return high, (total - high.astype(F32)).astype(BF16)

    after = rim + rows
    for place, start in ((0, after * odd), (1, after * (1 - odd))):
        high, low = matrix(start, rim)
        rim_ref[place * rim : (place + 1) * rim, :] = high
        rim_ref[(place + 2) * rim : (place + 3) * rim, :] = low
    for start in range(0, rows, rim):
        here = slice(start, start + rim)
        own_ref[0, here, :], own_ref[1, here, :] = matrix(start + rim, rim)
    table = table_ref[...]
    stress = jnp.dot(table, own_ref[0], preferred_element_type=F32)
    stress_ref[...] = stress + jnp.dot(table, own_ref[1], preferred_element_type=F32)


def power_kernel(stress_ref, far_ref, near_ref, rim_ref, power_ref):
    rows = [far_ref[...], near_ref[...]]
    stress = stress_ref[...] + lax.dot_general(
        jnp.concatenate(rows + rows, axis=0),
        rim_ref[...],
        (((0,), (0,)), ((), ())),
        preferred_element_type=F32,
    )
    squares = stress * stress
    lines = power_ref.shape[0]
    columns = squares.shape[0] // lines
    for line in range(lines):
        power_ref[line : line + 1, :] = (
            jnp.sum(squares[line * columns : (line + 1) * columns], axis=0, keepdims=True)
            / columns
        )


def call(kernel, name, out, *operands, flops, scratch=()):
    shapes = [jax.ShapeDtypeStruct(shape, dtype) for shape, dtype in out]
    moved = sum(x.size * x.dtype.itemsize for x in operands)
    moved += sum(math.prod(shape) * jnp.dtype(dtype).itemsize for shape, dtype in out)
    result = pl.pallas_call(
        kernel,
        out_shape=shapes,
        in_specs=[whole()] * len(operands),
        out_specs=[whole()] * len(out),
        scratch_shapes=scratch,
        compiler_params=pltpu.CompilerParams(vmem_limit_bytes=VMEM_BYTES),
        cost_estimate=pl.CostEstimate(flops=flops, bytes_accessed=moved, transcendentals=0),
        name=name,
    )(*operands)
    return result if len(out) > 1 else result[0]


def pseudo_by_sum(input_rows, input_factor, mode_freq, mode_damping, line_freq):
    lines = line_freq.shape[0]
    columns = input_factor.shape[1] // lines
    half = columns // 2
    forced = lax.psum(
        lax.dot_general(
            input_rows, input_factor, (((0,), (0,)), ((), ())), preferred_element_type=F32
        ),
        AXES,
    )
    pieces = []
    for line in range(lines):
        gain_real, gain_imag = modal_gain(mode_freq, mode_damping, line_freq[line])
        gain_real, gain_imag = gain_real[:, None], gain_imag[:, None]
        real = forced[:, line * columns : line * columns + half]
        imag = forced[:, line * columns + half : (line + 1) * columns]
        pieces.append(gain_real * real - gain_imag * imag)
        pieces.append(gain_real * imag + gain_imag * real)
    return jnp.concatenate(pieces, axis=1).astype(BF16)


def own_pseudo(input_rows, input_factor, mode_freq, mode_damping, line_freq, copies):
    devices = math.prod(FAST_SHAPE)
    rows, modes = input_rows.shape
    width = input_factor.shape[1]
    lines = line_freq.shape[0]
    parts = modes // (devices // 2 * width)
    ones = call(ones_kernel, "ones", [((8, width), F32)], flops=LONG)
    sent = call(
        pack_kernel,
        "pack",
        [((devices, (parts + 1) * rows, width), BF16)],
        ones,
        input_rows,
        input_factor,
        flops=LONG,
    )
    got = lax.all_to_all(sent, AXES, 0, 0)
    return call(
        functools.partial(pseudo_kernel, rows=rows),
        "pseudo",
        [((copies, parts * width, width), BF16)],
        line_freq.reshape(1, lines),
        mode_freq.reshape(-1, width),
        mode_damping.reshape(-1, width),
        got,
        flops=LONG,
    )


def local(
    shape,
    mode_rows,
    input_rows,
    input_factor,
    mode_freq,
    mode_damping,
    line_freq,
    boundary_rows,
    connectivity,
    stress_coef,
):
    devices = math.prod(shape)
    rows, modes = mode_rows.shape
    width = input_factor.shape[1]
    lines = line_freq.shape[0]
    exports = boundary_rows.shape[0]
    rim = exports // 2
    elems = connectivity.shape[1]
    inputs = (input_rows, input_factor, mode_freq, mode_damping, line_freq)
    if shape == FAST_SHAPE and modes == devices * LANES and input_rows.shape[0] % 16 == 0:
        cycle = [place ^ (place // 2) for place in range(8)]
        groups = [[h * 16 + j * 2 + c for j in cycle] for h in range(2) for c in range(2)]
        got = lax.all_to_all(own_pseudo(*inputs, copies=8), AXES, 0, 0, axis_index_groups=groups)
        mine = got.reshape(modes // 2, width)
        theirs = lax.ppermute(mine, AXES, [(i, i ^ 1) for i in range(devices)])
    else:
        pseudo = pseudo_by_sum(*inputs).reshape(2, modes // 2, width)
        core = lax.axis_index(AXES) % 2
        mine = lax.dynamic_index_in_dim(pseudo, core, 0, keepdims=False)
        theirs = lax.dynamic_index_in_dim(pseudo, 1 - core, 0, keepdims=False)
    total, part, picked = call(
        first_kernel,
        "first",
        [((rows, width), F32), ((exports, width), F32), ((exports, modes // 2), BF16)],
        boundary_rows.reshape(1, exports),
        mode_rows,
        mine,
        flops=rows * modes * (width + exports),
        scratch=[pltpu.VMEM((exports, rows), BF16)],
    )
    far, near = (
        call(
            functools.partial(export_kernel, start=start),
            name,
            [((rim, width), BF16)],
            part,
            picked,
            theirs,
            flops=rim * modes * width,
        )
        for name, start in (("far", 0), ("near", rim))
    )
    inner = [(i, i ^ 1) for i in range(devices)]
    outer = [(i, i + 1) for i in range(1, devices - 1, 2)]
    outer += [(j, i) for i, j in outer]
    near = lax.ppermute(near, AXES, inner)
    far = lax.ppermute(far, AXES, outer)
    stress, matrix = call(
        own_kernel,
        "own",
        [((width, elems), F32), ((2 * exports, elems), BF16)],
        connectivity,
        stress_coef,
        mode_rows,
        theirs,
        total,
        flops=rows * modes * width + 4 * rows * elems * width,
        scratch=[pltpu.VMEM((2, rows, elems), BF16), pltpu.VMEM((width, rows), BF16)],
    )
    return call(
        power_kernel,
        "power",
        [((lines, elems), F32)],
        stress,
        far,
        near,
        matrix,
        flops=4 * exports * elems * width,
    )


def solution(mesh):
    shape = tuple(mesh.shape[axis] for axis in AXES)
    placed = (
        P(AXES, None),
        P(AXES, None),
        P(AXES, None),
        P(),
        P(),
        P(),
        P(AXES),
        P(None, AXES),
        P(None, AXES),
    )
    return jax.shard_map(
        functools.partial(local, shape),
        mesh=mesh,
        in_specs=placed,
        out_specs=P(None, AXES),
        check_vma=False,
    )
```

```python
import functools
import math

import jax
import jax.numpy as jnp
from jax import lax
from jax.experimental import pallas as pl
from jax.experimental.pallas import tpu as pltpu
from jax.sharding import PartitionSpec as P

AXES = ("region", "sub")
LANES = 128
F32 = jnp.float32
BF16 = jnp.bfloat16
VMEM_BYTES = 24 * 1024 * 1024
LONG = 8 * 1024**3
FAST_SHAPE = (8, 4)


def whole(*_):
    return pl.BlockSpec(memory_space=pltpu.VMEM)


def modal_gain(freq, damping, omega):
    detune = freq * freq - omega * omega
    damped = 2.0 * damping * freq * omega
    magnitude = detune * detune + damped * damped
    return detune / magnitude, -damped / magnitude


def slab_of(device):
    chip = device // 2 % 8
    return device % 2 * 8 + (chip ^ (chip // 2) ^ (chip // 4))


def ones_kernel(ones_ref):
    ones_ref[...] = jnp.ones_like(ones_ref)


def pack_kernel(ones_ref, rows_ref, factor_ref, sent_ref):
    devices, _, width = sent_ref.shape
    rows = rows_ref.shape[0]
    parts = sent_ref.shape[1] // rows - 1
    factor = factor_ref[...] * ones_ref[0:1, :].astype(BF16)
    for device in range(devices):
        for part in range(parts):
            here = (slab_of(device) * parts + part) * width
            sent_ref[device, part * rows : (part + 1) * rows, :] = rows_ref[:, here : here + width]
        sent_ref[device, parts * rows :, :] = factor


def pseudo_kernel(line_ref, freq_ref, damping_ref, got_ref, pseudo_ref, *, rows):
    devices, tall, width = got_ref.shape
    parts = tall // rows - 1
    lines = line_ref.shape[1]
    columns = width // lines
    half = columns // 2
    slab = slab_of(lax.axis_index(AXES))
    factor = got_ref[:, parts * rows :, :].reshape(devices * rows, width)
    shapes = [
        got_ref[:, part * rows : (part + 1) * rows, :].reshape(devices * rows, width)
        for part in range(parts)
    ]
    forced = lax.dot_general(
        factor,
        jnp.concatenate(shapes, axis=1),
        (((0,), (0,)), ((), ())),
        preferred_element_type=F32,
    )
    for part in range(parts):
        here = pl.ds(slab * parts + part, 1)
        summed = forced[:, part * width : (part + 1) * width]
        pieces = []
        for line in range(lines):
            gain_real, gain_imag = modal_gain(
                freq_ref[here, :], damping_ref[here, :], line_ref[:, line : line + 1]
            )
            real = summed[line * columns : line * columns + half]
            imag = summed[line * columns + half : (line + 1) * columns]
            pieces.append(gain_real * real - gain_imag * imag)
            pieces.append(gain_real * imag + gain_imag * real)
        pseudo = jnp.concatenate(pieces, axis=0).T.astype(BF16)
        for copy in range(pseudo_ref.shape[0]):
            pseudo_ref[copy, part * width : (part + 1) * width, :] = pseudo


def for_core(depth, work):
    odd = lax.axis_index(AXES) % 2
    low, high = slice(0, depth), slice(depth, 2 * depth)
    pl.when(odd == 0)(lambda: work(low, high))
    pl.when(odd == 1)(lambda: work(high, low))


def stress_matrix(connect_ref, coef_ref, start, tall):
    elems = connect_ref.shape[1]
    node = lax.broadcasted_iota(jnp.int32, (tall, elems), 0) + start
    total = jnp.zeros((tall, elems), F32)
    for corner in range(connect_ref.shape[0]):
        hit = node == connect_ref[corner : corner + 1, :]
        total = total + jnp.where(hit, coef_ref[corner : corner + 1, :], 0.0)
    high = total.astype(BF16)
    return high, (total - high.astype(F32)).astype(BF16)


def first_kernel(
    boundary_ref, connect_ref, coef_ref, modes_ref, pseudo_ref,
    total_ref, part_ref, picked_ref, early_ref, pick_ref,
):
    rows = modes_ref.shape[0]
    exports = boundary_ref.shape[1]
    odd = lax.axis_index(AXES) % 2
    rim = exports // 2
    listed = boundary_ref[...]
    turned = jnp.concatenate([listed[:, rim:], listed[:, :rim]], axis=1)
    listed = jnp.where(odd == 1, turned, listed)
    chosen = jnp.broadcast_to(listed, (exports, exports)).astype(F32).T
    column = lax.broadcasted_iota(jnp.int32, (exports, exports), 1).astype(F32)
    pick_ref[...] = jnp.concatenate(
        [(column + start == chosen).astype(F32) for start in range(0, rows, exports)], axis=1
    ).astype(BF16)

    def product(mine, _):
        total_ref[...] = jnp.dot(modes_ref[:, mine], pseudo_ref[...], preferred_element_type=F32)

    def exported(_, other):
        pick = pick_ref[...]
        total = total_ref[...]
        high = total.astype(BF16)
        rest = total - high.astype(F32)
        middle = rest.astype(BF16)
        low = (rest - middle.astype(F32)).astype(BF16)
        parts = jnp.dot(
            pick, jnp.concatenate([high, middle, low], axis=1), preferred_element_type=F32
        )
        width = total.shape[1]
        part_ref[...] = parts[:, :width] + parts[:, width : 2 * width] + parts[:, 2 * width :]
        picked_ref[...] = jnp.dot(
            pick, modes_ref[:, other], preferred_element_type=F32
        ).astype(BF16)

    for_core(pseudo_ref.shape[0], product)
    for_core(pseudo_ref.shape[0], exported)

    @pl.when(odd == 0)
    def _():
        for start in range(0, early_ref.shape[1], rim):
            here = slice(start, start + rim)
            early_ref[0, here, :], early_ref[1, here, :] = stress_matrix(
                connect_ref, coef_ref, start + rim, rim
            )


def export_kernel(part_ref, picked_ref, pseudo_ref, export_ref, *, start):
    here = slice(start, start + export_ref.shape[0])
    export_ref[...] = (
        part_ref[here, :]
        + jnp.dot(picked_ref[here, :], pseudo_ref[...], preferred_element_type=F32)
    ).astype(BF16)


def own_kernel(
    connect_ref, coef_ref, modes_ref, pseudo_ref, total_ref, early_ref,
    stress_ref, rim_ref, own_ref, table_ref,
):
    rows = modes_ref.shape[0]
    rim = rim_ref.shape[0] // 4
    early = early_ref.shape[1]
    odd = lax.axis_index(AXES) % 2
    depth = pseudo_ref.shape[0]
    other = pl.ds(pl.multiple_of((1 - odd) * depth, depth), depth)
    total = total_ref[...] + jnp.dot(
        modes_ref[:, other], pseudo_ref[...], preferred_element_type=F32
    )
    table_ref[...] = total.T.astype(BF16)

    def build(first, last):
        for start in range(first, last, rim):
            here = slice(start, start + rim)
            own_ref[0, here, :], own_ref[1, here, :] = stress_matrix(
                connect_ref, coef_ref, start + rim, rim
            )

    after = rim + rows
    for place, start in ((0, after * odd), (1, after * (1 - odd))):
        high, low = stress_matrix(connect_ref, coef_ref, start, rim)
        rim_ref[place * rim : (place + 1) * rim, :] = high
        rim_ref[(place + 2) * rim : (place + 3) * rim, :] = low
    build(early, rows)
    table = table_ref[:, early:]
    stress = jnp.dot(table, own_ref[0, early:, :], preferred_element_type=F32)
    stress_ref[...] = stress + jnp.dot(
        table, own_ref[1, early:, :], preferred_element_type=F32
    )

    def rest(matrix_ref):
        table = table_ref[:, :early]
        stress = jnp.dot(table, matrix_ref[0, :early, :], preferred_element_type=F32)
        stress_ref[...] += stress + jnp.dot(
            table, matrix_ref[1, :early, :], preferred_element_type=F32
        )

    @pl.when(odd == 0)
    def _():
        rest(early_ref)

    @pl.when(odd == 1)
    def _():
        build(0, early)
        rest(own_ref)


def power_kernel(stress_ref, far_ref, near_ref, rim_ref, power_ref):
    rows = [far_ref[...], near_ref[...]]
    stress = stress_ref[...] + lax.dot_general(
        jnp.concatenate(rows + rows, axis=0),
        rim_ref[...],
        (((0,), (0,)), ((), ())),
        preferred_element_type=F32,
    )
    squares = stress * stress
    lines = power_ref.shape[0]
    columns = squares.shape[0] // lines
    for line in range(lines):
        power_ref[line : line + 1, :] = (
            jnp.sum(squares[line * columns : (line + 1) * columns], axis=0, keepdims=True)
            / columns
        )


def call(kernel, name, out, *operands, flops, scratch=()):
    shapes = [jax.ShapeDtypeStruct(shape, dtype) for shape, dtype in out]
    moved = sum(x.size * x.dtype.itemsize for x in operands)
    moved += sum(math.prod(shape) * jnp.dtype(dtype).itemsize for shape, dtype in out)
    result = pl.pallas_call(
        kernel,
        out_shape=shapes,
        in_specs=[whole()] * len(operands),
        out_specs=[whole()] * len(out),
        scratch_shapes=scratch,
        compiler_params=pltpu.CompilerParams(vmem_limit_bytes=VMEM_BYTES),
        cost_estimate=pl.CostEstimate(flops=flops, bytes_accessed=moved, transcendentals=0),
        name=name,
    )(*operands)
    return result if len(out) > 1 else result[0]


def pseudo_by_sum(input_rows, input_factor, mode_freq, mode_damping, line_freq):
    lines = line_freq.shape[0]
    columns = input_factor.shape[1] // lines
    half = columns // 2
    forced = lax.psum(
        lax.dot_general(
            input_rows, input_factor, (((0,), (0,)), ((), ())), preferred_element_type=F32
        ),
        AXES,
    )
    pieces = []
    for line in range(lines):
        gain_real, gain_imag = modal_gain(mode_freq, mode_damping, line_freq[line])
        gain_real, gain_imag = gain_real[:, None], gain_imag[:, None]
        real = forced[:, line * columns : line * columns + half]
        imag = forced[:, line * columns + half : (line + 1) * columns]
        pieces.append(gain_real * real - gain_imag * imag)
        pieces.append(gain_real * imag + gain_imag * real)
    return jnp.concatenate(pieces, axis=1).astype(BF16)


def own_pseudo(input_rows, input_factor, mode_freq, mode_damping, line_freq, copies):
    devices = math.prod(FAST_SHAPE)
    rows, modes = input_rows.shape
    width = input_factor.shape[1]
    lines = line_freq.shape[0]
    parts = modes // (devices // 2 * width)
    ones = call(ones_kernel, "ones", [((8, width), F32)], flops=LONG)
    sent = call(
        pack_kernel,
        "pack",
        [((devices, (parts + 1) * rows, width), BF16)],
        ones,
        input_rows,
        input_factor,
        flops=LONG,
    )
    got = lax.all_to_all(sent, AXES, 0, 0)
    return call(
        functools.partial(pseudo_kernel, rows=rows),
        "pseudo",
        [((copies, parts * width, width), BF16)],
        line_freq.reshape(1, lines),
        mode_freq.reshape(-1, width),
        mode_damping.reshape(-1, width),
        got,
        flops=LONG,
    )


def local(
    shape,
    mode_rows,
    input_rows,
    input_factor,
    mode_freq,
    mode_damping,
    line_freq,
    boundary_rows,
    connectivity,
    stress_coef,
):
    devices = math.prod(shape)
    rows, modes = mode_rows.shape
    width = input_factor.shape[1]
    lines = line_freq.shape[0]
    exports = boundary_rows.shape[0]
    rim = exports // 2
    elems = connectivity.shape[1]
    inputs = (input_rows, input_factor, mode_freq, mode_damping, line_freq)
    if shape == FAST_SHAPE and modes == devices * LANES and input_rows.shape[0] % 16 == 0:
        cycle = [place ^ (place // 2) for place in range(8)]
        groups = [[h * 16 + j * 2 + c for j in cycle] for h in range(2) for c in range(2)]
        got = lax.all_to_all(own_pseudo(*inputs, copies=8), AXES, 0, 0, axis_index_groups=groups)
        mine = got.reshape(modes // 2, width)
        theirs = lax.ppermute(mine, AXES, [(i, i ^ 1) for i in range(devices)])
    else:
        pseudo = pseudo_by_sum(*inputs).reshape(2, modes // 2, width)
        core = lax.axis_index(AXES) % 2
        mine = lax.dynamic_index_in_dim(pseudo, core, 0, keepdims=False)
        theirs = lax.dynamic_index_in_dim(pseudo, 1 - core, 0, keepdims=False)
    total, part, picked, early = call(
        first_kernel,
        "first",
        [
            ((rows, width), F32),
            ((exports, width), F32),
            ((exports, modes // 2), BF16),
            ((2, rows * 3 // 4, elems), BF16),
        ],
        boundary_rows.reshape(1, exports),
        connectivity,
        stress_coef,
        mode_rows,
        mine,
        flops=rows * modes * (width + exports),
        scratch=[pltpu.VMEM((exports, rows), BF16)],
    )
    far, near = (
        call(
            functools.partial(export_kernel, start=start),
            name,
            [((rim, width), BF16)],
            part,
            picked,
            theirs,
            flops=rim * modes * width,
        )
        for name, start in (("far", 0), ("near", rim))
    )
    inner = [(i, i ^ 1) for i in range(devices)]
    outer = [(i, i + 1) for i in range(1, devices - 1, 2)]
    outer += [(j, i) for i, j in outer]
    near = lax.ppermute(near, AXES, inner)
    far = lax.ppermute(far, AXES, outer)
    stress, matrix = call(
        own_kernel,
        "own",
        [((width, elems), F32), ((2 * exports, elems), BF16)],
        connectivity,
        stress_coef,
        mode_rows,
        theirs,
        total,
        early,
        flops=rows * modes * width + 4 * rows * elems * width,
        scratch=[pltpu.VMEM((2, rows, elems), BF16), pltpu.VMEM((width, rows), BF16)],
    )
    return call(
        power_kernel,
        "power",
        [((lines, elems), F32)],
        stress,
        far,
        near,
        matrix,
        flops=4 * exports * elems * width,
    )


def solution(mesh):
    shape = tuple(mesh.shape[axis] for axis in AXES)
    placed = (
        P(AXES, None),
        P(AXES, None),
        P(AXES, None),
        P(),
        P(),
        P(),
        P(AXES),
        P(None, AXES),
        P(None, AXES),
    )
    return jax.shard_map(
        functools.partial(local, shape),
        mesh=mesh,
        in_specs=placed,
        out_specs=P(None, AXES),
        check_vma=False,
    )
```

```python
import functools
import math

import jax
import jax.numpy as jnp
from jax import lax
from jax.experimental import pallas as pl
from jax.experimental.pallas import tpu as pltpu
from jax.sharding import PartitionSpec as P

AXES = ("region", "sub")
LANES = 128
F32 = jnp.float32
BF16 = jnp.bfloat16
VMEM_BYTES = 24 * 1024 * 1024
LONG = 8 * 1024**3
FAST_SHAPE = (8, 4)


def whole(*_):
    return pl.BlockSpec(memory_space=pltpu.VMEM)


def modal_gain(freq, damping, omega):
    detune = freq * freq - omega * omega
    damped = 2.0 * damping * freq * omega
    magnitude = detune * detune + damped * damped
    return detune / magnitude, -damped / magnitude


def slab_of(device):
    chip = device // 2 % 8
    return device % 2 * 8 + (chip ^ (chip // 2) ^ (chip // 4))


def ones_kernel(ones_ref):
    ones_ref[...] = jnp.ones_like(ones_ref)


def pack_kernel(ones_ref, rows_ref, factor_ref, sent_ref):
    devices, _, width = sent_ref.shape
    rows = rows_ref.shape[0]
    parts = sent_ref.shape[1] // rows - 1
    factor = factor_ref[...] * ones_ref[0:1, :].astype(BF16)
    for device in range(devices):
        for part in range(parts):
            here = (slab_of(device) * parts + part) * width
            sent_ref[device, part * rows : (part + 1) * rows, :] = rows_ref[:, here : here + width]
        sent_ref[device, parts * rows :, :] = factor


def pseudo_kernel(
    boundary_ref, line_ref, freq_ref, damping_ref, got_ref, pseudo_ref, pick_ref, *, rows
):
    devices, tall, width = got_ref.shape
    parts = tall // rows - 1
    lines = line_ref.shape[1]
    columns = width // lines
    half = columns // 2
    slab = slab_of(lax.axis_index(AXES))
    factor = got_ref[:, parts * rows :, :].reshape(devices * rows, width)
    shapes = [
        got_ref[:, part * rows : (part + 1) * rows, :].reshape(devices * rows, width)
        for part in range(parts)
    ]
    forced = lax.dot_general(
        factor,
        jnp.concatenate(shapes, axis=1),
        (((0,), (0,)), ((), ())),
        preferred_element_type=F32,
    )
    for part in range(parts):
        here = pl.ds(slab * parts + part, 1)
        summed = forced[:, part * width : (part + 1) * width]
        pieces = []
        for line in range(lines):
            gain_real, gain_imag = modal_gain(
                freq_ref[here, :], damping_ref[here, :], line_ref[:, line : line + 1]
            )
            real = summed[line * columns : line * columns + half]
            imag = summed[line * columns + half : (line + 1) * columns]
            pieces.append(gain_real * real - gain_imag * imag)
            pieces.append(gain_real * imag + gain_imag * real)
        pseudo = jnp.concatenate(pieces, axis=0).T.astype(BF16)
        for copy in range(pseudo_ref.shape[0]):
            pseudo_ref[copy, part * width : (part + 1) * width, :] = pseudo
    exports, owned = pick_ref.shape
    rim = exports // 2
    listed = boundary_ref[...]
    turned = jnp.concatenate([listed[:, rim:], listed[:, :rim]], axis=1)
    listed = jnp.where(lax.axis_index(AXES) % 2 == 1, turned, listed)
    chosen = jnp.broadcast_to(listed, (exports, exports)).astype(F32).T
    column = lax.broadcasted_iota(jnp.int32, (exports, exports), 1).astype(F32)
    for start in range(0, owned, exports):
        pick = (column + start == chosen).astype(F32).astype(BF16)
        pick_ref[:, start : start + exports] = pick


def for_core(depth, work):
    odd = lax.axis_index(AXES) % 2
    low, high = slice(0, depth), slice(depth, 2 * depth)
    pl.when(odd == 0)(lambda: work(low, high))
    pl.when(odd == 1)(lambda: work(high, low))


def first_kernel(pick_ref, modes_ref, pseudo_ref, total_ref, part_ref, picked_ref):
    depth = pseudo_ref.shape[0]
    odd = lax.axis_index(AXES) % 2
    mine = pl.ds(pl.multiple_of(odd * depth, depth), depth)
    total_ref[...] = jnp.dot(modes_ref[:, mine], pseudo_ref[...], preferred_element_type=F32)

    def exported(_, other):
        pick = pick_ref[...]
        total = total_ref[...]
        high = total.astype(BF16)
        rest = total - high.astype(F32)
        middle = rest.astype(BF16)
        low = (rest - middle.astype(F32)).astype(BF16)
        parts = jnp.dot(
            pick, jnp.concatenate([high, middle, low], axis=1), preferred_element_type=F32
        )
        width = total.shape[1]
        part_ref[...] = parts[:, :width] + parts[:, width : 2 * width] + parts[:, 2 * width :]
        picked_ref[...] = jnp.dot(
            pick, modes_ref[:, other], preferred_element_type=F32
        ).astype(BF16)

    for_core(depth, exported)


def export_kernel(part_ref, picked_ref, low_ref, high_ref, export_ref, *, start):
    here = slice(start, start + export_ref.shape[0])
    cut = low_ref.shape[0]
    export = part_ref[here, :] + jnp.dot(
        picked_ref[here, :cut], low_ref[...], preferred_element_type=F32
    )
    export_ref[...] = (
        export + jnp.dot(picked_ref[here, cut:], high_ref[...], preferred_element_type=F32)
    ).astype(BF16)


def own_kernel(
    connect_ref, coef_ref, modes_ref, low_ref, high_ref, total_ref,
    stress_ref, rim_ref, own_ref, table_ref,
):
    rows = modes_ref.shape[0]
    elems = connect_ref.shape[1]
    rim = rim_ref.shape[0] // 4
    odd = lax.axis_index(AXES) % 2

    cut = low_ref.shape[0]
    total = total_ref[...]
    for part, part_ref in enumerate((low_ref, high_ref)):
        here = pl.ds(pl.multiple_of((2 * (1 - odd) + part) * cut, cut), cut)
        total = total + jnp.dot(modes_ref[:, here], part_ref[...], preferred_element_type=F32)
    table_ref[...] = total.T.astype(BF16)

    def matrix(start, tall):
        node = lax.broadcasted_iota(jnp.int32, (tall, elems), 0) + start
        total = jnp.zeros((tall, elems), F32)
        for corner in range(connect_ref.shape[0]):
            hit = node == connect_ref[corner : corner + 1, :]
            total = total + jnp.where(hit, coef_ref[corner : corner + 1, :], 0.0)
        high = total.astype(BF16)
        return high, (total - high.astype(F32)).astype(BF16)

    after = rim + rows
    for place, start in ((0, after * odd), (1, after * (1 - odd))):
        high, low = matrix(start, rim)
        rim_ref[place * rim : (place + 1) * rim, :] = high
        rim_ref[(place + 2) * rim : (place + 3) * rim, :] = low
    for start in range(0, rows, rim):
        here = slice(start, start + rim)
        own_ref[0, here, :], own_ref[1, here, :] = matrix(start + rim, rim)
    table = table_ref[...]
    stress = jnp.dot(table, own_ref[0], preferred_element_type=F32)
    stress_ref[...] = stress + jnp.dot(table, own_ref[1], preferred_element_type=F32)


def power_kernel(stress_ref, far_ref, near_ref, rim_ref, power_ref):
    rows = [far_ref[...], near_ref[...]]
    stress = stress_ref[...] + lax.dot_general(
        jnp.concatenate(rows + rows, axis=0),
        rim_ref[...],
        (((0,), (0,)), ((), ())),
        preferred_element_type=F32,
    )
    squares = stress * stress
    lines = power_ref.shape[0]
    columns = squares.shape[0] // lines
    for line in range(lines):
        power_ref[line : line + 1, :] = (
            jnp.sum(squares[line * columns : (line + 1) * columns], axis=0, keepdims=True)
            / columns
        )


def call(kernel, name, out, *operands, flops, scratch=()):
    shapes = [jax.ShapeDtypeStruct(shape, dtype) for shape, dtype in out]
    moved = sum(x.size * x.dtype.itemsize for x in operands)
    moved += sum(math.prod(shape) * jnp.dtype(dtype).itemsize for shape, dtype in out)
    result = pl.pallas_call(
        kernel,
        out_shape=shapes,
        in_specs=[whole()] * len(operands),
        out_specs=[whole()] * len(out),
        scratch_shapes=scratch,
        compiler_params=pltpu.CompilerParams(vmem_limit_bytes=VMEM_BYTES),
        cost_estimate=pl.CostEstimate(flops=flops, bytes_accessed=moved, transcendentals=0),
        name=name,
    )(*operands)
    return result if len(out) > 1 else result[0]


def pseudo_by_sum(input_rows, input_factor, mode_freq, mode_damping, line_freq):
    lines = line_freq.shape[0]
    columns = input_factor.shape[1] // lines
    half = columns // 2
    forced = lax.psum(
        lax.dot_general(
            input_rows, input_factor, (((0,), (0,)), ((), ())), preferred_element_type=F32
        ),
        AXES,
    )
    pieces = []
    for line in range(lines):
        gain_real, gain_imag = modal_gain(mode_freq, mode_damping, line_freq[line])
        gain_real, gain_imag = gain_real[:, None], gain_imag[:, None]
        real = forced[:, line * columns : line * columns + half]
        imag = forced[:, line * columns + half : (line + 1) * columns]
        pieces.append(gain_real * real - gain_imag * imag)
        pieces.append(gain_real * imag + gain_imag * real)
    return jnp.concatenate(pieces, axis=1).astype(BF16)


def own_pseudo(
    input_rows, input_factor, mode_freq, mode_damping, line_freq, boundary_rows, owned, copies
):
    devices = math.prod(FAST_SHAPE)
    rows, modes = input_rows.shape
    width = input_factor.shape[1]
    lines = line_freq.shape[0]
    parts = modes // (devices // 2 * width)
    ones = call(ones_kernel, "ones", [((8, width), F32)], flops=LONG)
    sent = call(
        pack_kernel,
        "pack",
        [((devices, (parts + 1) * rows, width), BF16)],
        ones,
        input_rows,
        input_factor,
        flops=LONG,
    )
    got = lax.all_to_all(sent, AXES, 0, 0)
    return call(
        functools.partial(pseudo_kernel, rows=rows),
        "pseudo",
        [((copies, parts * width, width), BF16), ((boundary_rows.shape[0], owned), BF16)],
        boundary_rows.reshape(1, -1),
        line_freq.reshape(1, lines),
        mode_freq.reshape(-1, width),
        mode_damping.reshape(-1, width),
        got,
        flops=LONG,
    )


def local(
    shape,
    mode_rows,
    input_rows,
    input_factor,
    mode_freq,
    mode_damping,
    line_freq,
    boundary_rows,
    connectivity,
    stress_coef,
):
    devices = math.prod(shape)
    rows, modes = mode_rows.shape
    width = input_factor.shape[1]
    lines = line_freq.shape[0]
    exports = boundary_rows.shape[0]
    rim = exports // 2
    elems = connectivity.shape[1]
    inputs = (input_rows, input_factor, mode_freq, mode_damping, line_freq)
    if shape == FAST_SHAPE and modes == devices * LANES and input_rows.shape[0] % 16 == 0:
        cycle = [place ^ (place // 2) for place in range(8)]
        groups = [[h * 16 + j * 2 + c for j in cycle] for h in range(2) for c in range(2)]
        block, pick = own_pseudo(*inputs, boundary_rows, rows, copies=8)
        got = lax.all_to_all(block, AXES, 0, 0, axis_index_groups=groups)
        mine = got.reshape(modes // 2, width)
        cut = modes // 4
        swap = [(i, i ^ 1) for i in range(devices)]
        theirs = [lax.ppermute(part, AXES, swap) for part in (mine[:cut], mine[cut:])]
    else:
        pseudo = pseudo_by_sum(*inputs).reshape(2, modes // 2, width)
        core = lax.axis_index(AXES) % 2
        listed = jnp.where(core == 1, jnp.roll(boundary_rows, rim), boundary_rows)
        pick = (listed[:, None] == jnp.arange(rows)[None, :]).astype(BF16)
        mine = lax.dynamic_index_in_dim(pseudo, core, 0, keepdims=False)
        other = lax.dynamic_index_in_dim(pseudo, 1 - core, 0, keepdims=False)
        theirs = [other[: modes // 4], other[modes // 4 :]]
    total, part, picked = call(
        first_kernel,
        "first",
        [((rows, width), F32), ((exports, width), F32), ((exports, modes // 2), BF16)],
        pick,
        mode_rows,
        mine,
        flops=rows * modes * (width + exports),
    )
    far, near = (
        call(
            functools.partial(export_kernel, start=start),
            name,
            [((rim, width), BF16)],
            part,
            picked,
            *theirs,
            flops=rim * modes * width,
        )
        for name, start in (("far", 0), ("near", rim))
    )
    inner = [(i, i ^ 1) for i in range(devices)]
    outer = [(i, i + 1) for i in range(1, devices - 1, 2)]
    outer += [(j, i) for i, j in outer]
    near = lax.ppermute(near, AXES, inner)
    far = lax.ppermute(far, AXES, outer)
    stress, matrix = call(
        own_kernel,
        "own",
        [((width, elems), F32), ((2 * exports, elems), BF16)],
        connectivity,
        stress_coef,
        mode_rows,
        *theirs,
        total,
        flops=rows * modes * width + 4 * rows * elems * width,
        scratch=[pltpu.VMEM((2, rows, elems), BF16), pltpu.VMEM((width, rows), BF16)],
    )
    return call(
        power_kernel,
        "power",
        [((lines, elems), F32)],
        stress,
        far,
        near,
        matrix,
        flops=4 * exports * elems * width,
    )


def solution(mesh):
    shape = tuple(mesh.shape[axis] for axis in AXES)
    placed = (
        P(AXES, None),
        P(AXES, None),
        P(AXES, None),
        P(),
        P(),
        P(),
        P(AXES),
        P(None, AXES),
        P(None, AXES),
    )
    return jax.shard_map(
        functools.partial(local, shape),
        mesh=mesh,
        in_specs=placed,
        out_specs=P(None, AXES),
        check_vma=False,
    )
```

```python
import functools
import math

import jax
import jax.numpy as jnp
from jax import lax
from jax.experimental import pallas as pl
from jax.experimental.pallas import tpu as pltpu
from jax.sharding import PartitionSpec as P

AXES = ("region", "sub")
LANES = 128
F32 = jnp.float32
BF16 = jnp.bfloat16
VMEM_BYTES = 24 * 1024 * 1024
LONG = 8 * 1024**3
FAST_SHAPE = (8, 4)


def whole(*_):
    return pl.BlockSpec(memory_space=pltpu.VMEM)


def modal_gain(freq, damping, omega):
    detune = freq * freq - omega * omega
    damped = 2.0 * damping * freq * omega
    magnitude = detune * detune + damped * damped
    return detune / magnitude, -damped / magnitude


def slab_of(device):
    chip = device // 2 % 8
    return device % 2 * 8 + (chip ^ (chip // 2) ^ (chip // 4))


def ones_kernel(ones_ref):
    ones_ref[...] = jnp.ones_like(ones_ref)


def pack_kernel(ones_ref, rows_ref, factor_ref, sent_ref):
    devices, _, width = sent_ref.shape
    rows = rows_ref.shape[0]
    parts = sent_ref.shape[1] // rows - 1
    factor = factor_ref[...] * ones_ref[0:1, :].astype(BF16)
    for device in range(devices):
        for part in range(parts):
            here = (slab_of(device) * parts + part) * width
            sent_ref[device, part * rows : (part + 1) * rows, :] = rows_ref[:, here : here + width]
        sent_ref[device, parts * rows :, :] = factor


def pseudo_kernel(
    boundary_ref, line_ref, freq_ref, damping_ref, got_ref, pseudo_ref, pick_ref, *, rows
):
    devices, tall, width = got_ref.shape
    parts = tall // rows - 1
    lines = line_ref.shape[1]
    columns = width // lines
    half = columns // 2
    slab = slab_of(lax.axis_index(AXES))
    factor = got_ref[:, parts * rows :, :].reshape(devices * rows, width)
    shapes = [
        got_ref[:, part * rows : (part + 1) * rows, :].reshape(devices * rows, width)
        for part in range(parts)
    ]
    forced = lax.dot_general(
        factor,
        jnp.concatenate(shapes, axis=1),
        (((0,), (0,)), ((), ())),
        preferred_element_type=F32,
    )
    for part in range(parts):
        here = pl.ds(slab * parts + part, 1)
        summed = forced[:, part * width : (part + 1) * width]
        pieces = []
        for line in range(lines):
            gain_real, gain_imag = modal_gain(
                freq_ref[here, :], damping_ref[here, :], line_ref[:, line : line + 1]
            )
            real = summed[line * columns : line * columns + half]
            imag = summed[line * columns + half : (line + 1) * columns]
            pieces.append(gain_real * real - gain_imag * imag)
            pieces.append(gain_real * imag + gain_imag * real)
        pseudo = jnp.concatenate(pieces, axis=0).T.astype(BF16)
        for copy in range(pseudo_ref.shape[0]):
            pseudo_ref[copy, part * width : (part + 1) * width, :] = pseudo
    exports, owned = pick_ref.shape
    rim = exports // 2
    listed = boundary_ref[...]
    turned = jnp.concatenate([listed[:, rim:], listed[:, :rim]], axis=1)
    listed = jnp.where(lax.axis_index(AXES) % 2 == 1, turned, listed)
    chosen = jnp.broadcast_to(listed, (exports, exports)).astype(F32).T
    column = lax.broadcasted_iota(jnp.int32, (exports, exports), 1).astype(F32)
    for start in range(0, owned, exports):
        pick = (column + start == chosen).astype(F32).astype(BF16)
        pick_ref[:, start : start + exports] = pick


def for_core(depth, work):
    odd = lax.axis_index(AXES) % 2
    low, high = slice(0, depth), slice(depth, 2 * depth)
    pl.when(odd == 0)(lambda: work(low, high))
    pl.when(odd == 1)(lambda: work(high, low))


def first_kernel(pick_ref, modes_ref, pseudo_ref, total_ref, part_ref, picked_ref):
    depth = pseudo_ref.shape[0]
    odd = lax.axis_index(AXES) % 2
    mine = pl.ds(pl.multiple_of(odd * depth, depth), depth)
    total_ref[...] = jnp.dot(modes_ref[:, mine], pseudo_ref[...], preferred_element_type=F32)

    def exported(_, other):
        pick = pick_ref[...]
        total = total_ref[...]
        high = total.astype(BF16)
        rest = total - high.astype(F32)
        middle = rest.astype(BF16)
        low = (rest - middle.astype(F32)).astype(BF16)
        parts = jnp.dot(
            pick, jnp.concatenate([high, middle, low], axis=1), preferred_element_type=F32
        )
        width = total.shape[1]
        part_ref[...] = parts[:, :width] + parts[:, width : 2 * width] + parts[:, 2 * width :]
        picked_ref[...] = jnp.dot(
            pick, modes_ref[:, other], preferred_element_type=F32
        ).astype(BF16)

    for_core(depth, exported)


def export_kernel(part_ref, picked_ref, pseudo_ref, export_ref, *, start):
    here = slice(start, start + export_ref.shape[0])
    export_ref[...] = (
        part_ref[here, :]
        + jnp.dot(picked_ref[here, :], pseudo_ref[...], preferred_element_type=F32)
    ).astype(BF16)


def own_kernel(
    connect_ref, coef_ref, modes_ref, pseudo_ref, total_ref, stress_ref, rim_ref, own_ref, table_ref
):
    rows = modes_ref.shape[0]
    elems = connect_ref.shape[1]
    rim = rim_ref.shape[0] // 4
    odd = lax.axis_index(AXES) % 2

    depth = pseudo_ref.shape[0]
    other = pl.ds(pl.multiple_of((1 - odd) * depth, depth), depth)
    total = total_ref[...] + jnp.dot(
        modes_ref[:, other], pseudo_ref[...], preferred_element_type=F32
    )
    table_ref[...] = total.T.astype(BF16)

    def matrix(start, tall):
        node = lax.broadcasted_iota(jnp.int32, (tall, elems), 0) + start
        total = jnp.zeros((tall, elems), F32)
        for corner in range(connect_ref.shape[0]):
            hit = node == connect_ref[corner : corner + 1, :]
            total = total + jnp.where(hit, coef_ref[corner : corner + 1, :], 0.0)
        high = total.astype(BF16)
        return high, (total - high.astype(F32)).astype(BF16)

    after = rim + rows
    for place, start in ((0, after * odd), (1, after * (1 - odd))):
        high, low = matrix(start, rim)
        rim_ref[place * rim : (place + 1) * rim, :] = high
        rim_ref[(place + 2) * rim : (place + 3) * rim, :] = low
    for start in range(0, rows, rim):
        here = slice(start, start + rim)
        own_ref[0, here, :], own_ref[1, here, :] = matrix(start + rim, rim)
    table = table_ref[...]
    stress = jnp.dot(table, own_ref[0], preferred_element_type=F32)
    stress_ref[...] = stress + jnp.dot(table, own_ref[1], preferred_element_type=F32)


def power_kernel(stress_ref, far_ref, near_ref, rim_ref, power_ref):
    rows = [far_ref[...], near_ref[...]]
    stress = stress_ref[...] + lax.dot_general(
        jnp.concatenate(rows + rows, axis=0),
        rim_ref[...],
        (((0,), (0,)), ((), ())),
        preferred_element_type=F32,
    )
    squares = stress * stress
    lines = power_ref.shape[0]
    columns = squares.shape[0] // lines
    for line in range(lines):
        power_ref[line : line + 1, :] = (
            jnp.sum(squares[line * columns : (line + 1) * columns], axis=0, keepdims=True)
            / columns
        )


def call(kernel, name, out, *operands, flops, scratch=()):
    shapes = [jax.ShapeDtypeStruct(shape, dtype) for shape, dtype in out]
    moved = sum(x.size * x.dtype.itemsize for x in operands)
    moved += sum(math.prod(shape) * jnp.dtype(dtype).itemsize for shape, dtype in out)
    result = pl.pallas_call(
        kernel,
        out_shape=shapes,
        in_specs=[whole()] * len(operands),
        out_specs=[whole()] * len(out),
        scratch_shapes=scratch,
        compiler_params=pltpu.CompilerParams(vmem_limit_bytes=VMEM_BYTES),
        cost_estimate=pl.CostEstimate(flops=flops, bytes_accessed=moved, transcendentals=0),
        name=name,
    )(*operands)
    return result if len(out) > 1 else result[0]


def pseudo_by_sum(input_rows, input_factor, mode_freq, mode_damping, line_freq):
    lines = line_freq.shape[0]
    columns = input_factor.shape[1] // lines
    half = columns // 2
    forced = lax.psum(
        lax.dot_general(
            input_rows, input_factor, (((0,), (0,)), ((), ())), preferred_element_type=F32
        ),
        AXES,
    )
    pieces = []
    for line in range(lines):
        gain_real, gain_imag = modal_gain(mode_freq, mode_damping, line_freq[line])
        gain_real, gain_imag = gain_real[:, None], gain_imag[:, None]
        real = forced[:, line * columns : line * columns + half]
        imag = forced[:, line * columns + half : (line + 1) * columns]
        pieces.append(gain_real * real - gain_imag * imag)
        pieces.append(gain_real * imag + gain_imag * real)
    return jnp.concatenate(pieces, axis=1).astype(BF16)


def own_pseudo(
    input_rows, input_factor, mode_freq, mode_damping, line_freq, boundary_rows, owned, copies
):
    devices = math.prod(FAST_SHAPE)
    rows, modes = input_rows.shape
    width = input_factor.shape[1]
    lines = line_freq.shape[0]
    parts = modes // (devices // 2 * width)
    ones = call(ones_kernel, "ones", [((8, width), F32)], flops=LONG)
    sent = call(
        pack_kernel,
        "pack",
        [((devices, (parts + 1) * rows, width), BF16)],
        ones,
        input_rows,
        input_factor,
        flops=LONG,
    )
    got = lax.all_to_all(sent, AXES, 0, 0)
    return call(
        functools.partial(pseudo_kernel, rows=rows),
        "pseudo",
        [((copies, parts * width, width), BF16), ((boundary_rows.shape[0], owned), BF16)],
        boundary_rows.reshape(1, -1),
        line_freq.reshape(1, lines),
        mode_freq.reshape(-1, width),
        mode_damping.reshape(-1, width),
        got,
        flops=LONG,
    )


def local(
    shape,
    mode_rows,
    input_rows,
    input_factor,
    mode_freq,
    mode_damping,
    line_freq,
    boundary_rows,
    connectivity,
    stress_coef,
):
    devices = math.prod(shape)
    rows, modes = mode_rows.shape
    width = input_factor.shape[1]
    lines = line_freq.shape[0]
    exports = boundary_rows.shape[0]
    rim = exports // 2
    elems = connectivity.shape[1]
    inputs = (input_rows, input_factor, mode_freq, mode_damping, line_freq)
    if shape == FAST_SHAPE and modes == devices * LANES and input_rows.shape[0] % 16 == 0:
        cycle = [place ^ (place // 2) for place in range(8)]
        groups = [[h * 16 + j * 2 + c for j in cycle] for h in range(2) for c in range(2)]
        block, pick = own_pseudo(*inputs, boundary_rows, rows, copies=8)
        got = lax.all_to_all(block, AXES, 0, 0, axis_index_groups=groups)
        mine = got.reshape(modes // 2, width)
        theirs = lax.ppermute(mine, AXES, [(i, i ^ 1) for i in range(devices)])
    else:
        pseudo = pseudo_by_sum(*inputs).reshape(2, modes // 2, width)
        core = lax.axis_index(AXES) % 2
        listed = jnp.where(core == 1, jnp.roll(boundary_rows, rim), boundary_rows)
        pick = (listed[:, None] == jnp.arange(rows)[None, :]).astype(BF16)
        mine = lax.dynamic_index_in_dim(pseudo, core, 0, keepdims=False)
        theirs = lax.dynamic_index_in_dim(pseudo, 1 - core, 0, keepdims=False)
    total, part, picked = call(
        first_kernel,
        "first",
        [((rows, width), F32), ((exports, width), F32), ((exports, modes // 2), BF16)],
        pick,
        mode_rows,
        mine,
        flops=rows * modes * (width + exports),
    )
    far, near = (
        call(
            functools.partial(export_kernel, start=start),
            name,
            [((rim, width), BF16)],
            part,
            picked,
            theirs,
            flops=rim * modes * width,
        )
        for name, start in (("far", 0), ("near", rim))
    )
    inner = [(i, i ^ 1) for i in range(devices)]
    outer = [(i, i + 1) for i in range(1, devices - 1, 2)]
    outer += [(j, i) for i, j in outer]
    near = lax.ppermute(near, AXES, inner)
    far = lax.ppermute(far, AXES, outer)
    stress, matrix = call(
        own_kernel,
        "own",
        [((width, elems), F32), ((2 * exports, elems), BF16)],
        connectivity,
        stress_coef,
        mode_rows,
        theirs,
        total,
        flops=rows * modes * width + 4 * rows * elems * width,
        scratch=[pltpu.VMEM((2, rows, elems), BF16), pltpu.VMEM((width, rows), BF16)],
    )
    return call(
        power_kernel,
        "power",
        [((lines, elems), F32)],
        stress,
        far,
        near,
        matrix,
        flops=4 * exports * elems * width,
    )


def solution(mesh):
    shape = tuple(mesh.shape[axis] for axis in AXES)
    placed = (
        P(AXES, None),
        P(AXES, None),
        P(AXES, None),
        P(),
        P(),
        P(),
        P(AXES),
        P(None, AXES),
        P(None, AXES),
    )
    return jax.shard_map(
        functools.partial(local, shape),
        mesh=mesh,
        in_specs=placed,
        out_specs=P(None, AXES),
        check_vma=False,
    )
```

```python
import functools
import math

import jax
import jax.numpy as jnp
from jax import lax
from jax.experimental import pallas as pl
from jax.experimental.pallas import tpu as pltpu
from jax.sharding import PartitionSpec as P

AXES = ("region", "sub")
LANES = 128
F32 = jnp.float32
BF16 = jnp.bfloat16
VMEM_BYTES = 24 * 1024 * 1024
LONG = 8 * 1024**3
FAST_SHAPE = (8, 4)


def whole(*_):
    return pl.BlockSpec(memory_space=pltpu.VMEM)


def modal_gain(freq, damping, omega):
    detune = freq * freq - omega * omega
    damped = 2.0 * damping * freq * omega
    magnitude = detune * detune + damped * damped
    return detune / magnitude, -damped / magnitude


def slab_of(device):
    chip = device // 2 % 8
    return device % 2 * 8 + (chip ^ (chip // 2) ^ (chip // 4))


def ones_kernel(ones_ref):
    ones_ref[...] = jnp.ones_like(ones_ref)


def pack_kernel(ones_ref, rows_ref, factor_ref, sent_ref):
    devices, _, width = sent_ref.shape
    rows = rows_ref.shape[0]
    parts = sent_ref.shape[1] // rows - 1
    factor = factor_ref[...] * ones_ref[0:1, :].astype(BF16)
    for device in range(devices):
        for part in range(parts):
            here = (slab_of(device) * parts + part) * width
            sent_ref[device, part * rows : (part + 1) * rows, :] = rows_ref[:, here : here + width]
        sent_ref[device, parts * rows :, :] = factor


def pseudo_kernel(
    boundary_ref, line_ref, freq_ref, damping_ref, got_ref, pseudo_ref, pick_ref, *, rows
):
    devices, tall, width = got_ref.shape
    parts = tall // rows - 1
    lines = line_ref.shape[1]
    columns = width // lines
    half = columns // 2
    slab = slab_of(lax.axis_index(AXES))
    factor = got_ref[:, parts * rows :, :].reshape(devices * rows, width)
    shapes = [
        got_ref[:, part * rows : (part + 1) * rows, :].reshape(devices * rows, width)
        for part in range(parts)
    ]
    forced = lax.dot_general(
        factor,
        jnp.concatenate(shapes, axis=1),
        (((0,), (0,)), ((), ())),
        preferred_element_type=F32,
    )
    for part in range(parts):
        here = pl.ds(slab * parts + part, 1)
        summed = forced[:, part * width : (part + 1) * width]
        pieces = []
        for line in range(lines):
            gain_real, gain_imag = modal_gain(
                freq_ref[here, :], damping_ref[here, :], line_ref[:, line : line + 1]
            )
            real = summed[line * columns : line * columns + half]
            imag = summed[line * columns + half : (line + 1) * columns]
            pieces.append(gain_real * real - gain_imag * imag)
            pieces.append(gain_real * imag + gain_imag * real)
        pseudo = jnp.concatenate(pieces, axis=0).T.astype(BF16)
        for copy in range(pseudo_ref.shape[0]):
            pseudo_ref[copy, part * width : (part + 1) * width, :] = pseudo
    exports, owned = pick_ref.shape
    rim = exports // 2
    listed = boundary_ref[...]
    turned = jnp.concatenate([listed[:, rim:], listed[:, :rim]], axis=1)
    listed = jnp.where(lax.axis_index(AXES) % 2 == 1, turned, listed)
    chosen = jnp.broadcast_to(listed, (exports, exports)).astype(F32).T
    column = lax.broadcasted_iota(jnp.int32, (exports, exports), 1).astype(F32)
    for start in range(0, owned, exports):
        pick = (column + start == chosen).astype(F32).astype(BF16)
        pick_ref[:, start : start + exports] = pick


def for_core(depth, work):
    odd = lax.axis_index(AXES) % 2
    low, high = slice(0, depth), slice(depth, 2 * depth)
    pl.when(odd == 0)(lambda: work(low, high))
    pl.when(odd == 1)(lambda: work(high, low))


def first_kernel(pick_ref, modes_ref, pseudo_ref, total_ref, part_ref, picked_ref):
    depth = pseudo_ref.shape[0]
    odd = lax.axis_index(AXES) % 2
    mine = pl.ds(pl.multiple_of(odd * depth, depth), depth)
    total_ref[...] = jnp.dot(modes_ref[:, mine], pseudo_ref[...], preferred_element_type=F32)

    def exported(_, other):
        pick = pick_ref[...]
        total = total_ref[...]
        high = total.astype(BF16)
        rest = total - high.astype(F32)
        middle = rest.astype(BF16)
        low = (rest - middle.astype(F32)).astype(BF16)
        parts = jnp.dot(
            pick, jnp.concatenate([high, middle, low], axis=1), preferred_element_type=F32
        )
        width = total.shape[1]
        part_ref[...] = parts[:, :width] + parts[:, width : 2 * width] + parts[:, 2 * width :]
        picked_ref[...] = jnp.dot(
            pick, modes_ref[:, other], preferred_element_type=F32
        ).astype(BF16)

    for_core(depth, exported)


def export_kernel(part_ref, picked_ref, pseudo_ref, *refs, start):
    export_ref = refs[-1]
    here = slice(start, start + export_ref.shape[0])
    export_ref[...] = (
        part_ref[here, :]
        + jnp.dot(picked_ref[here, :], pseudo_ref[...], preferred_element_type=F32)
    ).astype(BF16)


def own_kernel(
    connect_ref, coef_ref, modes_ref, pseudo_ref, total_ref, stress_ref, rim_ref, own_ref, table_ref
):
    rows = modes_ref.shape[0]
    elems = connect_ref.shape[1]
    rim = rim_ref.shape[0] // 4
    odd = lax.axis_index(AXES) % 2

    depth = pseudo_ref.shape[0]
    other = pl.ds(pl.multiple_of((1 - odd) * depth, depth), depth)
    total = total_ref[...] + jnp.dot(
        modes_ref[:, other], pseudo_ref[...], preferred_element_type=F32
    )
    table_ref[...] = total.T.astype(BF16)

    def matrix(start, tall):
        node = lax.broadcasted_iota(jnp.int32, (tall, elems), 0) + start
        total = jnp.zeros((tall, elems), F32)
        for corner in range(connect_ref.shape[0]):
            hit = node == connect_ref[corner : corner + 1, :]
            total = total + jnp.where(hit, coef_ref[corner : corner + 1, :], 0.0)
        high = total.astype(BF16)
        return high, (total - high.astype(F32)).astype(BF16)

    after = rim + rows
    for place, start in ((0, after * odd), (1, after * (1 - odd))):
        high, low = matrix(start, rim)
        rim_ref[place * rim : (place + 1) * rim, :] = high
        rim_ref[(place + 2) * rim : (place + 3) * rim, :] = low
    for start in range(0, rows, rim):
        here = slice(start, start + rim)
        own_ref[0, here, :], own_ref[1, here, :] = matrix(start + rim, rim)
    table = table_ref[...]
    stress = jnp.dot(table, own_ref[0], preferred_element_type=F32)
    stress_ref[...] = stress + jnp.dot(table, own_ref[1], preferred_element_type=F32)


def power_kernel(stress_ref, far_ref, near_ref, rim_ref, power_ref):
    rows = [far_ref[...], near_ref[...]]
    stress = stress_ref[...] + lax.dot_general(
        jnp.concatenate(rows + rows, axis=0),
        rim_ref[...],
        (((0,), (0,)), ((), ())),
        preferred_element_type=F32,
    )
    squares = stress * stress
    lines = power_ref.shape[0]
    columns = squares.shape[0] // lines
    for line in range(lines):
        power_ref[line : line + 1, :] = (
            jnp.sum(squares[line * columns : (line + 1) * columns], axis=0, keepdims=True)
            / columns
        )


def call(kernel, name, out, *operands, flops, scratch=()):
    shapes = [jax.ShapeDtypeStruct(shape, dtype) for shape, dtype in out]
    moved = sum(x.size * x.dtype.itemsize for x in operands)
    moved += sum(math.prod(shape) * jnp.dtype(dtype).itemsize for shape, dtype in out)
    result = pl.pallas_call(
        kernel,
        out_shape=shapes,
        in_specs=[whole()] * len(operands),
        out_specs=[whole()] * len(out),
        scratch_shapes=scratch,
        compiler_params=pltpu.CompilerParams(vmem_limit_bytes=VMEM_BYTES),
        cost_estimate=pl.CostEstimate(flops=flops, bytes_accessed=moved, transcendentals=0),
        name=name,
    )(*operands)
    return result if len(out) > 1 else result[0]


def pseudo_by_sum(input_rows, input_factor, mode_freq, mode_damping, line_freq):
    lines = line_freq.shape[0]
    columns = input_factor.shape[1] // lines
    half = columns // 2
    forced = lax.psum(
        lax.dot_general(
            input_rows, input_factor, (((0,), (0,)), ((), ())), preferred_element_type=F32
        ),
        AXES,
    )
    pieces = []
    for line in range(lines):
        gain_real, gain_imag = modal_gain(mode_freq, mode_damping, line_freq[line])
        gain_real, gain_imag = gain_real[:, None], gain_imag[:, None]
        real = forced[:, line * columns : line * columns + half]
        imag = forced[:, line * columns + half : (line + 1) * columns]
        pieces.append(gain_real * real - gain_imag * imag)
        pieces.append(gain_real * imag + gain_imag * real)
    return jnp.concatenate(pieces, axis=1).astype(BF16)


def own_pseudo(
    input_rows, input_factor, mode_freq, mode_damping, line_freq, boundary_rows, owned, copies
):
    devices = math.prod(FAST_SHAPE)
    rows, modes = input_rows.shape
    width = input_factor.shape[1]
    lines = line_freq.shape[0]
    parts = modes // (devices // 2 * width)
    ones = call(ones_kernel, "ones", [((8, width), F32)], flops=LONG)
    sent = call(
        pack_kernel,
        "pack",
        [((devices, (parts + 1) * rows, width), BF16)],
        ones,
        input_rows,
        input_factor,
        flops=LONG,
    )
    got = lax.all_to_all(sent, AXES, 0, 0)
    return call(
        functools.partial(pseudo_kernel, rows=rows),
        "pseudo",
        [((copies, parts * width, width), BF16), ((boundary_rows.shape[0], owned), BF16)],
        boundary_rows.reshape(1, -1),
        line_freq.reshape(1, lines),
        mode_freq.reshape(-1, width),
        mode_damping.reshape(-1, width),
        got,
        flops=LONG,
    )


def local(
    shape,
    mode_rows,
    input_rows,
    input_factor,
    mode_freq,
    mode_damping,
    line_freq,
    boundary_rows,
    connectivity,
    stress_coef,
):
    devices = math.prod(shape)
    rows, modes = mode_rows.shape
    width = input_factor.shape[1]
    lines = line_freq.shape[0]
    exports = boundary_rows.shape[0]
    rim = exports // 2
    elems = connectivity.shape[1]
    inputs = (input_rows, input_factor, mode_freq, mode_damping, line_freq)
    if shape == FAST_SHAPE and modes == devices * LANES and input_rows.shape[0] % 16 == 0:
        cycle = [place ^ (place // 2) for place in range(8)]
        groups = [[h * 16 + j * 2 + c for j in cycle] for h in range(2) for c in range(2)]
        block, pick = own_pseudo(*inputs, boundary_rows, rows, copies=8)
        got = lax.all_to_all(block, AXES, 0, 0, axis_index_groups=groups)
        mine = got.reshape(modes // 2, width)
        theirs = lax.ppermute(mine, AXES, [(i, i ^ 1) for i in range(devices)])
    else:
        pseudo = pseudo_by_sum(*inputs).reshape(2, modes // 2, width)
        core = lax.axis_index(AXES) % 2
        listed = jnp.where(core == 1, jnp.roll(boundary_rows, rim), boundary_rows)
        pick = (listed[:, None] == jnp.arange(rows)[None, :]).astype(BF16)
        mine = lax.dynamic_index_in_dim(pseudo, core, 0, keepdims=False)
        theirs = lax.dynamic_index_in_dim(pseudo, 1 - core, 0, keepdims=False)
    total, part, picked = call(
        first_kernel,
        "first",
        [((rows, width), F32), ((exports, width), F32), ((exports, modes // 2), BF16)],
        pick,
        mode_rows,
        mine,
        flops=rows * modes * (width + exports),
    )
    def export(name, start, *after):
        return call(
            functools.partial(export_kernel, start=start),
            name,
            [((rim, width), BF16)],
            part,
            picked,
            theirs,
            *after,
            flops=rim * modes * width,
        )

    far = export("far", 0)
    near = export("near", rim, far)
    inner = [(i, i ^ 1) for i in range(devices)]
    outer = [(i, i + 1) for i in range(1, devices - 1, 2)]
    outer += [(j, i) for i, j in outer]
    near = lax.ppermute(near, AXES, inner)
    far = lax.ppermute(far, AXES, outer)
    stress, matrix = call(
        own_kernel,
        "own",
        [((width, elems), F32), ((2 * exports, elems), BF16)],
        connectivity,
        stress_coef,
        mode_rows,
        theirs,
        total,
        flops=rows * modes * width + 4 * rows * elems * width,
        scratch=[pltpu.VMEM((2, rows, elems), BF16), pltpu.VMEM((width, rows), BF16)],
    )
    return call(
        power_kernel,
        "power",
        [((lines, elems), F32)],
        stress,
        far,
        near,
        matrix,
        flops=4 * exports * elems * width,
    )


def solution(mesh):
    shape = tuple(mesh.shape[axis] for axis in AXES)
    placed = (
        P(AXES, None),
        P(AXES, None),
        P(AXES, None),
        P(),
        P(),
        P(),
        P(AXES),
        P(None, AXES),
        P(None, AXES),
    )
    return jax.shard_map(
        functools.partial(local, shape),
        mesh=mesh,
        in_specs=placed,
        out_specs=P(None, AXES),
        check_vma=False,
    )
```

```python
import functools
import math

import jax
import jax.numpy as jnp
from jax import lax
from jax.experimental import pallas as pl
from jax.experimental.pallas import tpu as pltpu
from jax.sharding import PartitionSpec as P

AXES = ("region", "sub")
LANES = 128
F32 = jnp.float32
BF16 = jnp.bfloat16
VMEM_BYTES = 24 * 1024 * 1024
LONG = 8 * 1024**3
FAST_SHAPE = (8, 4)


def whole(*_):
    return pl.BlockSpec(memory_space=pltpu.VMEM)


def modal_gain(freq, damping, omega):
    detune = freq * freq - omega * omega
    damped = 2.0 * damping * freq * omega
    magnitude = detune * detune + damped * damped
    return detune / magnitude, -damped / magnitude


def slab_of(device):
    chip = device // 2 % 8
    return device % 2 * 8 + (chip ^ (chip // 2) ^ (chip // 4))


def exchange_order(devices):
    chips = [place ^ (place // 2) for place in range(devices // 2)]
    return [2 * chip + core for chip in chips for core in range(2)]


def ones_kernel(ones_ref):
    ones_ref[...] = jnp.ones_like(ones_ref)


def pack_kernel(ones_ref, rows_ref, factor_ref, sent_ref):
    devices, _, width = sent_ref.shape
    rows = rows_ref.shape[0]
    parts = sent_ref.shape[1] // rows - 1
    factor = factor_ref[...] * ones_ref[0:1, :].astype(BF16)
    for place, device in enumerate(exchange_order(devices)):
        for part in range(parts):
            here = (slab_of(device) * parts + part) * width
            sent_ref[place, part * rows : (part + 1) * rows, :] = rows_ref[:, here : here + width]
        sent_ref[place, parts * rows :, :] = factor


def pseudo_kernel(line_ref, freq_ref, damping_ref, got_ref, pseudo_ref, *, rows):
    devices, tall, width = got_ref.shape
    parts = tall // rows - 1
    lines = line_ref.shape[1]
    columns = width // lines
    half = columns // 2
    slab = slab_of(lax.axis_index(AXES))
    factor = got_ref[:, parts * rows :, :].reshape(devices * rows, width)
    shapes = [
        got_ref[:, part * rows : (part + 1) * rows, :].reshape(devices * rows, width)
        for part in range(parts)
    ]
    forced = lax.dot_general(
        factor,
        jnp.concatenate(shapes, axis=1),
        (((0,), (0,)), ((), ())),
        preferred_element_type=F32,
    )
    for part in range(parts):
        here = pl.ds(slab * parts + part, 1)
        summed = forced[:, part * width : (part + 1) * width]
        pieces = []
        for line in range(lines):
            gain_real, gain_imag = modal_gain(
                freq_ref[here, :], damping_ref[here, :], line_ref[:, line : line + 1]
            )
            real = summed[line * columns : line * columns + half]
            imag = summed[line * columns + half : (line + 1) * columns]
            pieces.append(gain_real * real - gain_imag * imag)
            pieces.append(gain_real * imag + gain_imag * real)
        pseudo = jnp.concatenate(pieces, axis=0).T.astype(BF16)
        for copy in range(pseudo_ref.shape[0]):
            pseudo_ref[copy, part * width : (part + 1) * width, :] = pseudo


def for_core(depth, work):
    odd = lax.axis_index(AXES) % 2
    low, high = slice(0, depth), slice(depth, 2 * depth)
    pl.when(odd == 0)(lambda: work(low, high))
    pl.when(odd == 1)(lambda: work(high, low))


def first_kernel(boundary_ref, modes_ref, pseudo_ref, total_ref, part_ref, picked_ref, pick_ref):
    rows = modes_ref.shape[0]
    exports = boundary_ref.shape[1]
    chosen = jnp.broadcast_to(boundary_ref[...], (exports, exports)).astype(F32).T
    column = lax.broadcasted_iota(jnp.int32, (exports, exports), 1).astype(F32)
    pick_ref[...] = jnp.concatenate(
        [(column + start == chosen).astype(F32) for start in range(0, rows, exports)], axis=1
    ).astype(BF16)

    def product(mine, _):
        total_ref[...] = jnp.dot(modes_ref[:, mine], pseudo_ref[...], preferred_element_type=F32)

    def exported(_, other):
        pick = pick_ref[...]
        total = total_ref[...]
        high = total.astype(BF16)
        rest = total - high.astype(F32)
        middle = rest.astype(BF16)
        low = (rest - middle.astype(F32)).astype(BF16)
        parts = jnp.dot(
            pick, jnp.concatenate([high, middle, low], axis=1), preferred_element_type=F32
        )
        width = total.shape[1]
        part_ref[...] = parts[:, :width] + parts[:, width : 2 * width] + parts[:, 2 * width :]
        picked_ref[...] = jnp.dot(
            pick, modes_ref[:, other], preferred_element_type=F32
        ).astype(BF16)

    for_core(pseudo_ref.shape[0], product)
    for_core(pseudo_ref.shape[0], exported)


def export_kernel(part_ref, picked_ref, pseudo_ref, far_ref, near_ref):
    exports = part_ref.shape[0]
    cut = pseudo_ref.shape[0] // 2
    width = pseudo_ref.shape[1]
    both = jnp.dot(
        jnp.concatenate([picked_ref[:, :cut], picked_ref[:, cut:]], axis=0),
        jnp.concatenate([pseudo_ref[:cut], pseudo_ref[cut:]], axis=1),
        preferred_element_type=F32,
    )
    export = part_ref[...] + both[:exports, :width] + both[exports:, width:]
    export = export.astype(BF16)
    odd = lax.axis_index(AXES) % 2 == 1
    rim = far_ref.shape[0]
    far_ref[...] = jnp.where(odd, export[rim:], export[:rim])
    near_ref[...] = jnp.where(odd, export[:rim], export[rim:])


def own_kernel(
    connect_ref, coef_ref, modes_ref, pseudo_ref, total_ref, stress_ref, rim_ref, own_ref, table_ref
):
    rows = modes_ref.shape[0]
    elems = connect_ref.shape[1]
    rim = rim_ref.shape[0] // 4
    odd = lax.axis_index(AXES) % 2

    depth = pseudo_ref.shape[0]
    other = pl.ds(pl.multiple_of((1 - odd) * depth, depth), depth)
    total = total_ref[...] + jnp.dot(
        modes_ref[:, other], pseudo_ref[...], preferred_element_type=F32
    )
    table_ref[...] = total.T.astype(BF16)

    def matrix(start, tall):
        node = lax.broadcasted_iota(jnp.int32, (tall, elems), 0) + start
        total = jnp.zeros((tall, elems), F32)
        for corner in range(connect_ref.shape[0]):
            hit = node == connect_ref[corner : corner + 1, :]
            total = total + jnp.where(hit, coef_ref[corner : corner + 1, :], 0.0)
        high = total.astype(BF16)
        return high, (total - high.astype(F32)).astype(BF16)

    after = rim + rows
    for place, start in ((0, after * odd), (1, after * (1 - odd))):
        high, low = matrix(start, rim)
        rim_ref[place * rim : (place + 1) * rim, :] = high
        rim_ref[(place + 2) * rim : (place + 3) * rim, :] = low
    for start in range(0, rows, rim):
        here = slice(start, start + rim)
        own_ref[0, here, :], own_ref[1, here, :] = matrix(start + rim, rim)
    table = table_ref[...]
    stress = jnp.dot(table, own_ref[0], preferred_element_type=F32)
    stress_ref[...] = stress + jnp.dot(table, own_ref[1], preferred_element_type=F32)


def power_kernel(stress_ref, far_ref, near_ref, rim_ref, power_ref):
    rows = [far_ref[...], near_ref[...]]
    stress = stress_ref[...] + lax.dot_general(
        jnp.concatenate(rows + rows, axis=0),
        rim_ref[...],
        (((0,), (0,)), ((), ())),
        preferred_element_type=F32,
    )
    squares = stress * stress
    lines = power_ref.shape[0]
    columns = squares.shape[0] // lines
    for line in range(lines):
        power_ref[line : line + 1, :] = (
            jnp.sum(squares[line * columns : (line + 1) * columns], axis=0, keepdims=True)
            / columns
        )


def call(kernel, name, out, *operands, flops, scratch=()):
    shapes = [jax.ShapeDtypeStruct(shape, dtype) for shape, dtype in out]
    moved = sum(x.size * x.dtype.itemsize for x in operands)
    moved += sum(math.prod(shape) * jnp.dtype(dtype).itemsize for shape, dtype in out)
    result = pl.pallas_call(
        kernel,
        out_shape=shapes,
        in_specs=[whole()] * len(operands),
        out_specs=[whole()] * len(out),
        scratch_shapes=scratch,
        compiler_params=pltpu.CompilerParams(vmem_limit_bytes=VMEM_BYTES),
        cost_estimate=pl.CostEstimate(flops=flops, bytes_accessed=moved, transcendentals=0),
        name=name,
    )(*operands)
    return result if len(out) > 1 else result[0]


def pseudo_by_sum(input_rows, input_factor, mode_freq, mode_damping, line_freq):
    lines = line_freq.shape[0]
    columns = input_factor.shape[1] // lines
    half = columns // 2
    forced = lax.psum(
        lax.dot_general(
            input_rows, input_factor, (((0,), (0,)), ((), ())), preferred_element_type=F32
        ),
        AXES,
    )
    pieces = []
    for line in range(lines):
        gain_real, gain_imag = modal_gain(mode_freq, mode_damping, line_freq[line])
        gain_real, gain_imag = gain_real[:, None], gain_imag[:, None]
        real = forced[:, line * columns : line * columns + half]
        imag = forced[:, line * columns + half : (line + 1) * columns]
        pieces.append(gain_real * real - gain_imag * imag)
        pieces.append(gain_real * imag + gain_imag * real)
    return jnp.concatenate(pieces, axis=1).astype(BF16)


def own_pseudo(input_rows, input_factor, mode_freq, mode_damping, line_freq, copies):
    devices = math.prod(FAST_SHAPE)
    rows, modes = input_rows.shape
    width = input_factor.shape[1]
    lines = line_freq.shape[0]
    parts = modes // (devices // 2 * width)
    ones = call(ones_kernel, "ones", [((8, width), F32)], flops=LONG)
    sent = call(
        pack_kernel,
        "pack",
        [((devices, (parts + 1) * rows, width), BF16)],
        ones,
        input_rows,
        input_factor,
        flops=LONG,
    )
    got = lax.all_to_all(sent, AXES, 0, 0, axis_index_groups=[exchange_order(devices)])
    return call(
        functools.partial(pseudo_kernel, rows=rows),
        "pseudo",
        [((copies, parts * width, width), BF16)],
        line_freq.reshape(1, lines),
        mode_freq.reshape(-1, width),
        mode_damping.reshape(-1, width),
        got,
        flops=LONG,
    )


def local(
    shape,
    mode_rows,
    input_rows,
    input_factor,
    mode_freq,
    mode_damping,
    line_freq,
    boundary_rows,
    connectivity,
    stress_coef,
):
    devices = math.prod(shape)
    rows, modes = mode_rows.shape
    width = input_factor.shape[1]
    lines = line_freq.shape[0]
    exports = boundary_rows.shape[0]
    rim = exports // 2
    elems = connectivity.shape[1]
    inputs = (input_rows, input_factor, mode_freq, mode_damping, line_freq)
    if shape == FAST_SHAPE and modes == devices * LANES and input_rows.shape[0] % 16 == 0:
        cycle = [place ^ (place // 2) for place in range(8)]
        groups = [[h * 16 + j * 2 + c for j in cycle] for h in range(2) for c in range(2)]
        got = lax.all_to_all(own_pseudo(*inputs, copies=8), AXES, 0, 0, axis_index_groups=groups)
        mine = got.reshape(modes // 2, width)
        theirs = lax.ppermute(mine, AXES, [(i, i ^ 1) for i in range(devices)])
    else:
        pseudo = pseudo_by_sum(*inputs).reshape(2, modes // 2, width)
        core = lax.axis_index(AXES) % 2
        mine = lax.dynamic_index_in_dim(pseudo, core, 0, keepdims=False)
        theirs = lax.dynamic_index_in_dim(pseudo, 1 - core, 0, keepdims=False)
    total, part, picked = call(
        first_kernel,
        "first",
        [((rows, width), F32), ((exports, width), F32), ((exports, modes // 2), BF16)],
        boundary_rows.reshape(1, exports),
        mode_rows,
        mine,
        flops=rows * modes * (width + exports),
        scratch=[pltpu.VMEM((exports, rows), BF16)],
    )
    far, near = call(
        export_kernel,
        "export",
        [((rim, width), BF16)] * 2,
        part,
        picked,
        theirs,
        flops=exports * modes * width,
    )
    inner = [(i, i ^ 1) for i in range(devices)]
    outer = [(i, i + 1) for i in range(1, devices - 1, 2)]
    outer += [(j, i) for i, j in outer]
    near = lax.ppermute(near, AXES, inner)
    far = lax.ppermute(far, AXES, outer)
    stress, matrix = call(
        own_kernel,
        "own",
        [((width, elems), F32), ((2 * exports, elems), BF16)],
        connectivity,
        stress_coef,
        mode_rows,
        theirs,
        total,
        flops=rows * modes * width + 4 * rows * elems * width,
        scratch=[pltpu.VMEM((2, rows, elems), BF16), pltpu.VMEM((width, rows), BF16)],
    )
    return call(
        power_kernel,
        "power",
        [((lines, elems), F32)],
        stress,
        far,
        near,
        matrix,
        flops=4 * exports * elems * width,
    )


def solution(mesh):
    shape = tuple(mesh.shape[axis] for axis in AXES)
    placed = (
        P(AXES, None),
        P(AXES, None),
        P(AXES, None),
        P(),
        P(),
        P(),
        P(AXES),
        P(None, AXES),
        P(None, AXES),
    )
    return jax.shard_map(
        functools.partial(local, shape),
        mesh=mesh,
        in_specs=placed,
        out_specs=P(None, AXES),
        check_vma=False,
    )
```

```python
import functools
import math

import jax
import jax.numpy as jnp
from jax import lax
from jax.experimental import pallas as pl
from jax.experimental.pallas import tpu as pltpu
from jax.sharding import PartitionSpec as P

AXES = ("region", "sub")
LANES = 128
F32 = jnp.float32
BF16 = jnp.bfloat16
VMEM_BYTES = 24 * 1024 * 1024
LONG = 8 * 1024**3
FAST_SHAPE = (8, 4)


def whole(*_):
    return pl.BlockSpec(memory_space=pltpu.VMEM)


def modal_gain(freq, damping, omega):
    detune = freq * freq - omega * omega
    damped = 2.0 * damping * freq * omega
    magnitude = detune * detune + damped * damped
    return detune / magnitude, -damped / magnitude


def slab_of(device):
    chip = device // 2 % 8
    return device % 2 * 8 + (chip ^ (chip // 2) ^ (chip // 4))


def ones_kernel(ones_ref):
    ones_ref[...] = jnp.ones_like(ones_ref)


def pack_kernel(ones_ref, rows_ref, factor_ref, sent_ref):
    devices, _, width = sent_ref.shape
    rows = rows_ref.shape[0]
    parts = sent_ref.shape[1] // rows - 1
    factor = factor_ref[...] * ones_ref[0:1, :].astype(BF16)
    for device in range(devices):
        for part in range(parts):
            here = (slab_of(device) * parts + part) * width
            sent_ref[device, part * rows : (part + 1) * rows, :] = rows_ref[:, here : here + width]
        sent_ref[device, parts * rows :, :] = factor


def pseudo_kernel(
    boundary_ref, line_ref, freq_ref, damping_ref, got_ref, pseudo_ref, pick_ref, *, rows
):
    devices, tall, width = got_ref.shape
    parts = tall // rows - 1
    lines = line_ref.shape[1]
    columns = width // lines
    half = columns // 2
    slab = slab_of(lax.axis_index(AXES))
    factor = got_ref[:, parts * rows :, :].reshape(devices * rows, width)
    shapes = [
        got_ref[:, part * rows : (part + 1) * rows, :].reshape(devices * rows, width)
        for part in range(parts)
    ]
    forced = lax.dot_general(
        factor,
        jnp.concatenate(shapes, axis=1),
        (((0,), (0,)), ((), ())),
        preferred_element_type=F32,
    )
    for part in range(parts):
        here = pl.ds(slab * parts + part, 1)
        summed = forced[:, part * width : (part + 1) * width]
        pieces = []
        for line in range(lines):
            gain_real, gain_imag = modal_gain(
                freq_ref[here, :], damping_ref[here, :], line_ref[:, line : line + 1]
            )
            real = summed[line * columns : line * columns + half]
            imag = summed[line * columns + half : (line + 1) * columns]
            pieces.append(gain_real * real - gain_imag * imag)
            pieces.append(gain_real * imag + gain_imag * real)
        pseudo = jnp.concatenate(pieces, axis=0).T.astype(BF16)
        for copy in range(pseudo_ref.shape[0]):
            pseudo_ref[copy, part * width : (part + 1) * width, :] = pseudo
    exports, owned = pick_ref.shape
    rim = exports // 2
    listed = boundary_ref[...]
    turned = jnp.concatenate([listed[:, rim:], listed[:, :rim]], axis=1)
    listed = jnp.where(lax.axis_index(AXES) % 2 == 1, turned, listed)
    chosen = jnp.broadcast_to(listed, (exports, exports)).astype(F32).T
    column = lax.broadcasted_iota(jnp.int32, (exports, exports), 1).astype(F32)
    for start in range(0, owned, exports):
        pick = (column + start == chosen).astype(F32).astype(BF16)
        pick_ref[:, start : start + exports] = pick


def for_core(depth, work):
    odd = lax.axis_index(AXES) % 2
    low, high = slice(0, depth), slice(depth, 2 * depth)
    pl.when(odd == 0)(lambda: work(low, high))
    pl.when(odd == 1)(lambda: work(high, low))


def first_kernel(pick_ref, modes_ref, pseudo_ref, total_ref, part_ref, picked_ref):
    depth = pseudo_ref.shape[0]
    odd = lax.axis_index(AXES) % 2
    mine = pl.ds(pl.multiple_of(odd * depth, depth), depth)
    total_ref[...] = jnp.dot(modes_ref[:, mine], pseudo_ref[...], preferred_element_type=F32)

    def exported(_, other):
        pick = pick_ref[...]
        total = total_ref[...]
        high = total.astype(BF16)
        rest = total - high.astype(F32)
        middle = rest.astype(BF16)
        low = (rest - middle.astype(F32)).astype(BF16)
        parts = jnp.dot(
            pick, jnp.concatenate([high, middle, low], axis=1), preferred_element_type=F32
        )
        width = total.shape[1]
        part_ref[...] = parts[:, :width] + parts[:, width : 2 * width] + parts[:, 2 * width :]
        picked_ref[...] = jnp.dot(
            pick, modes_ref[:, other], preferred_element_type=F32
        ).astype(BF16)

    for_core(depth, exported)


def export_kernel(part_ref, picked_ref, pseudo_ref, far_ref, near_ref):
    export = part_ref[...] + jnp.dot(
        picked_ref[...], pseudo_ref[...], preferred_element_type=F32
    )
    rim = far_ref.shape[0]
    far_ref[...] = export[:rim].astype(BF16)
    near_ref[...] = export[rim:].astype(BF16)


def own_kernel(
    connect_ref, coef_ref, modes_ref, pseudo_ref, total_ref, stress_ref, rim_ref, own_ref, table_ref
):
    rows = modes_ref.shape[0]
    elems = connect_ref.shape[1]
    rim = rim_ref.shape[0] // 4
    odd = lax.axis_index(AXES) % 2

    depth = pseudo_ref.shape[0]
    other = pl.ds(pl.multiple_of((1 - odd) * depth, depth), depth)
    total = total_ref[...] + jnp.dot(
        modes_ref[:, other], pseudo_ref[...], preferred_element_type=F32
    )
    table_ref[...] = total.T.astype(BF16)

    def matrix(start, tall):
        node = lax.broadcasted_iota(jnp.int32, (tall, elems), 0) + start
        total = jnp.zeros((tall, elems), F32)
        for corner in range(connect_ref.shape[0]):
            hit = node == connect_ref[corner : corner + 1, :]
            total = total + jnp.where(hit, coef_ref[corner : corner + 1, :], 0.0)
        high = total.astype(BF16)
        return high, (total - high.astype(F32)).astype(BF16)

    after = rim + rows
    for place, start in ((0, after * odd), (1, after * (1 - odd))):
        high, low = matrix(start, rim)
        rim_ref[place * rim : (place + 1) * rim, :] = high
        rim_ref[(place + 2) * rim : (place + 3) * rim, :] = low
    for start in range(0, rows, rim):
        here = slice(start, start + rim)
        own_ref[0, here, :], own_ref[1, here, :] = matrix(start + rim, rim)
    table = table_ref[...]
    stress = jnp.dot(table, own_ref[0], preferred_element_type=F32)
    stress_ref[...] = stress + jnp.dot(table, own_ref[1], preferred_element_type=F32)


def power_kernel(stress_ref, far_ref, near_ref, rim_ref, power_ref):
    rows = [far_ref[...], near_ref[...]]
    stress = stress_ref[...] + lax.dot_general(
        jnp.concatenate(rows + rows, axis=0),
        rim_ref[...],
        (((0,), (0,)), ((), ())),
        preferred_element_type=F32,
    )
    squares = stress * stress
    lines = power_ref.shape[0]
    columns = squares.shape[0] // lines
    for line in range(lines):
        power_ref[line : line + 1, :] = (
            jnp.sum(squares[line * columns : (line + 1) * columns], axis=0, keepdims=True)
            / columns
        )


def call(kernel, name, out, *operands, flops, scratch=()):
    shapes = [jax.ShapeDtypeStruct(shape, dtype) for shape, dtype in out]
    moved = sum(x.size * x.dtype.itemsize for x in operands)
    moved += sum(math.prod(shape) * jnp.dtype(dtype).itemsize for shape, dtype in out)
    result = pl.pallas_call(
        kernel,
        out_shape=shapes,
        in_specs=[whole()] * len(operands),
        out_specs=[whole()] * len(out),
        scratch_shapes=scratch,
        compiler_params=pltpu.CompilerParams(vmem_limit_bytes=VMEM_BYTES),
        cost_estimate=pl.CostEstimate(flops=flops, bytes_accessed=moved, transcendentals=0),
        name=name,
    )(*operands)
    return result if len(out) > 1 else result[0]


def pseudo_by_sum(input_rows, input_factor, mode_freq, mode_damping, line_freq):
    lines = line_freq.shape[0]
    columns = input_factor.shape[1] // lines
    half = columns // 2
    forced = lax.psum(
        lax.dot_general(
            input_rows, input_factor, (((0,), (0,)), ((), ())), preferred_element_type=F32
        ),
        AXES,
    )
    pieces = []
    for line in range(lines):
        gain_real, gain_imag = modal_gain(mode_freq, mode_damping, line_freq[line])
        gain_real, gain_imag = gain_real[:, None], gain_imag[:, None]
        real = forced[:, line * columns : line * columns + half]
        imag = forced[:, line * columns + half : (line + 1) * columns]
        pieces.append(gain_real * real - gain_imag * imag)
        pieces.append(gain_real * imag + gain_imag * real)
    return jnp.concatenate(pieces, axis=1).astype(BF16)


def own_pseudo(
    input_rows, input_factor, mode_freq, mode_damping, line_freq, boundary_rows, owned, copies
):
    devices = math.prod(FAST_SHAPE)
    rows, modes = input_rows.shape
    width = input_factor.shape[1]
    lines = line_freq.shape[0]
    parts = modes // (devices // 2 * width)
    ones = call(ones_kernel, "ones", [((8, width), F32)], flops=LONG)
    sent = call(
        pack_kernel,
        "pack",
        [((devices, (parts + 1) * rows, width), BF16)],
        ones,
        input_rows,
        input_factor,
        flops=LONG,
    )
    got = lax.all_to_all(sent, AXES, 0, 0)
    return call(
        functools.partial(pseudo_kernel, rows=rows),
        "pseudo",
        [((copies, parts * width, width), BF16), ((boundary_rows.shape[0], owned), BF16)],
        boundary_rows.reshape(1, -1),
        line_freq.reshape(1, lines),
        mode_freq.reshape(-1, width),
        mode_damping.reshape(-1, width),
        got,
        flops=LONG,
    )


def local(
    shape,
    mode_rows,
    input_rows,
    input_factor,
    mode_freq,
    mode_damping,
    line_freq,
    boundary_rows,
    connectivity,
    stress_coef,
):
    devices = math.prod(shape)
    rows, modes = mode_rows.shape
    width = input_factor.shape[1]
    lines = line_freq.shape[0]
    exports = boundary_rows.shape[0]
    rim = exports // 2
    elems = connectivity.shape[1]
    inputs = (input_rows, input_factor, mode_freq, mode_damping, line_freq)
    if shape == FAST_SHAPE and modes == devices * LANES and input_rows.shape[0] % 16 == 0:
        cycle = [place ^ (place // 2) for place in range(8)]
        groups = [[h * 16 + j * 2 + c for j in cycle] for h in range(2) for c in range(2)]
        block, pick = own_pseudo(*inputs, boundary_rows, rows, copies=8)
        got = lax.all_to_all(block, AXES, 0, 0, axis_index_groups=groups)
        mine = got.reshape(modes // 2, width)
        theirs = lax.ppermute(mine, AXES, [(i, i ^ 1) for i in range(devices)])
    else:
        pseudo = pseudo_by_sum(*inputs).reshape(2, modes // 2, width)
        core = lax.axis_index(AXES) % 2
        listed = jnp.where(core == 1, jnp.roll(boundary_rows, rim), boundary_rows)
        pick = (listed[:, None] == jnp.arange(rows)[None, :]).astype(BF16)
        mine = lax.dynamic_index_in_dim(pseudo, core, 0, keepdims=False)
        theirs = lax.dynamic_index_in_dim(pseudo, 1 - core, 0, keepdims=False)
    total, part, picked = call(
        first_kernel,
        "first",
        [((rows, width), F32), ((exports, width), F32), ((exports, modes // 2), BF16)],
        pick,
        mode_rows,
        mine,
        flops=rows * modes * (width + exports),
    )
    far, near = call(
        export_kernel,
        "export",
        [((rim, width), BF16)] * 2,
        part,
        picked,
        theirs,
        flops=exports * modes * width,
    )
    inner = [(i, i ^ 1) for i in range(devices)]
    outer = [(i, i + 1) for i in range(1, devices - 1, 2)]
    outer += [(j, i) for i, j in outer]
    near = lax.ppermute(near, AXES, inner)
    far = lax.ppermute(far, AXES, outer)
    stress, matrix = call(
        own_kernel,
        "own",
        [((width, elems), F32), ((2 * exports, elems), BF16)],
        connectivity,
        stress_coef,
        mode_rows,
        theirs,
        total,
        flops=rows * modes * width + 4 * rows * elems * width,
        scratch=[pltpu.VMEM((2, rows, elems), BF16), pltpu.VMEM((width, rows), BF16)],
    )
    return call(
        power_kernel,
        "power",
        [((lines, elems), F32)],
        stress,
        far,
        near,
        matrix,
        flops=4 * exports * elems * width,
    )


def solution(mesh):
    shape = tuple(mesh.shape[axis] for axis in AXES)
    placed = (
        P(AXES, None),
        P(AXES, None),
        P(AXES, None),
        P(),
        P(),
        P(),
        P(AXES),
        P(None, AXES),
        P(None, AXES),
    )
    return jax.shard_map(
        functools.partial(local, shape),
        mesh=mesh,
        in_specs=placed,
        out_specs=P(None, AXES),
        check_vma=False,
    )
```

```python
import functools
import math

import jax
import jax.numpy as jnp
from jax import lax
from jax.experimental import pallas as pl
from jax.experimental.pallas import tpu as pltpu
from jax.sharding import PartitionSpec as P

AXES = ("region", "sub")
LANES = 128
F32 = jnp.float32
BF16 = jnp.bfloat16
VMEM_BYTES = 24 * 1024 * 1024
LONG = 8 * 1024**3
FAST_SHAPE = (8, 4)


def whole(*_):
    return pl.BlockSpec(memory_space=pltpu.VMEM)


def modal_gain(freq, damping, omega):
    detune = freq * freq - omega * omega
    damped = 2.0 * damping * freq * omega
    magnitude = detune * detune + damped * damped
    return detune / magnitude, -damped / magnitude


def slab_of(device):
    chip = device // 2 % 8
    return device % 2 * 8 + (chip ^ (chip // 2) ^ (chip // 4))


def ones_kernel(ones_ref):
    ones_ref[...] = jnp.ones_like(ones_ref)


def pack_kernel(ones_ref, rows_ref, factor_ref, sent_ref):
    devices, _, width = sent_ref.shape
    rows = rows_ref.shape[0]
    parts = sent_ref.shape[1] // rows - 1
    factor = factor_ref[...] * ones_ref[0:1, :].astype(BF16)
    for device in range(devices):
        for part in range(parts):
            here = (slab_of(device) * parts + part) * width
            sent_ref[device, part * rows : (part + 1) * rows, :] = rows_ref[:, here : here + width]
        sent_ref[device, parts * rows :, :] = factor


def pseudo_kernel(line_ref, freq_ref, damping_ref, got_ref, pseudo_ref, *, rows):
    devices, tall, width = got_ref.shape
    parts = tall // rows - 1
    lines = line_ref.shape[1]
    columns = width // lines
    half = columns // 2
    slab = slab_of(lax.axis_index(AXES))
    factor = got_ref[:, parts * rows :, :].reshape(devices * rows, width)
    shapes = [
        got_ref[:, part * rows : (part + 1) * rows, :].reshape(devices * rows, width)
        for part in range(parts)
    ]
    forced = lax.dot_general(
        factor,
        jnp.concatenate(shapes, axis=1),
        (((0,), (0,)), ((), ())),
        preferred_element_type=F32,
    )
    for part in range(parts):
        here = pl.ds(slab * parts + part, 1)
        summed = forced[:, part * width : (part + 1) * width]
        pieces = []
        for line in range(lines):
            gain_real, gain_imag = modal_gain(
                freq_ref[here, :], damping_ref[here, :], line_ref[:, line : line + 1]
            )
            real = summed[line * columns : line * columns + half]
            imag = summed[line * columns + half : (line + 1) * columns]
            pieces.append(gain_real * real - gain_imag * imag)
            pieces.append(gain_real * imag + gain_imag * real)
        pseudo = jnp.concatenate(pieces, axis=0).T.astype(BF16)
        for copy in range(pseudo_ref.shape[0]):
            pseudo_ref[copy, part * width : (part + 1) * width, :] = pseudo


def for_core(depth, work):
    odd = lax.axis_index(AXES) % 2
    low, high = slice(0, depth), slice(depth, 2 * depth)
    pl.when(odd == 0)(lambda: work(low, high))
    pl.when(odd == 1)(lambda: work(high, low))


def first_kernel(boundary_ref, modes_ref, pseudo_ref, total_ref, part_ref, picked_ref, pick_ref):
    rows = modes_ref.shape[0]
    exports = boundary_ref.shape[1]
    chosen = jnp.broadcast_to(boundary_ref[...], (exports, exports)).astype(F32).T
    column = lax.broadcasted_iota(jnp.int32, (exports, exports), 1).astype(F32)
    pick_ref[...] = jnp.concatenate(
        [(column + start == chosen).astype(F32) for start in range(0, rows, exports)], axis=1
    ).astype(BF16)

    def product(mine, _):
        total_ref[...] = jnp.dot(modes_ref[:, mine], pseudo_ref[...], preferred_element_type=F32)

    def exported(_, other):
        pick = pick_ref[...]
        total = total_ref[...]
        high = total.astype(BF16)
        rest = total - high.astype(F32)
        middle = rest.astype(BF16)
        low = (rest - middle.astype(F32)).astype(BF16)
        parts = jnp.dot(
            pick, jnp.concatenate([high, middle, low], axis=1), preferred_element_type=F32
        )
        width = total.shape[1]
        part_ref[...] = parts[:, :width] + parts[:, width : 2 * width] + parts[:, 2 * width :]
        picked_ref[...] = jnp.dot(
            pick, modes_ref[:, other], preferred_element_type=F32
        ).astype(BF16)

    for_core(pseudo_ref.shape[0], product)
    for_core(pseudo_ref.shape[0], exported)


def export_kernel(part_ref, picked_ref, pseudo_ref, far_ref, near_ref):
    export = part_ref[...] + jnp.dot(
        picked_ref[...], pseudo_ref[...], preferred_element_type=F32
    )
    export = export.astype(BF16)
    odd = lax.axis_index(AXES) % 2 == 1
    rim = far_ref.shape[0]
    far_ref[...] = jnp.where(odd, export[rim:], export[:rim])
    near_ref[...] = jnp.where(odd, export[:rim], export[rim:])


def own_kernel(
    connect_ref, coef_ref, modes_ref, pseudo_ref, total_ref, stress_ref, rim_ref, own_ref, table_ref
):
    rows = modes_ref.shape[0]
    elems = connect_ref.shape[1]
    rim = rim_ref.shape[0] // 4
    odd = lax.axis_index(AXES) % 2

    depth = pseudo_ref.shape[0]
    other = pl.ds(pl.multiple_of((1 - odd) * depth, depth), depth)
    total = total_ref[...] + jnp.dot(
        modes_ref[:, other], pseudo_ref[...], preferred_element_type=F32
    )
    table_ref[...] = total.T.astype(BF16)

    def matrix(start, tall):
        node = lax.broadcasted_iota(jnp.int32, (tall, elems), 0) + start
        total = jnp.zeros((tall, elems), F32)
        for corner in range(connect_ref.shape[0]):
            hit = node == connect_ref[corner : corner + 1, :]
            total = total + jnp.where(hit, coef_ref[corner : corner + 1, :], 0.0)
        high = total.astype(BF16)
        return high, (total - high.astype(F32)).astype(BF16)

    after = rim + rows
    for place, start in ((0, after * odd), (1, after * (1 - odd))):
        high, low = matrix(start, rim)
        rim_ref[place * rim : (place + 1) * rim, :] = high
        rim_ref[(place + 2) * rim : (place + 3) * rim, :] = low
    for start in range(0, rows, rim):
        here = slice(start, start + rim)
        own_ref[0, here, :], own_ref[1, here, :] = matrix(start + rim, rim)
    table = table_ref[...]
    stress = jnp.dot(table, own_ref[0], preferred_element_type=F32)
    stress_ref[...] = stress + jnp.dot(table, own_ref[1], preferred_element_type=F32)


def power_kernel(stress_ref, far_ref, near_ref, rim_ref, power_ref):
    rows = [far_ref[...], near_ref[...]]
    stress = stress_ref[...] + lax.dot_general(
        jnp.concatenate(rows + rows, axis=0),
        rim_ref[...],
        (((0,), (0,)), ((), ())),
        preferred_element_type=F32,
    )
    squares = stress * stress
    lines = power_ref.shape[0]
    columns = squares.shape[0] // lines
    for line in range(lines):
        power_ref[line : line + 1, :] = (
            jnp.sum(squares[line * columns : (line + 1) * columns], axis=0, keepdims=True)
            / columns
        )


def call(kernel, name, out, *operands, flops, scratch=()):
    shapes = [jax.ShapeDtypeStruct(shape, dtype) for shape, dtype in out]
    moved = sum(x.size * x.dtype.itemsize for x in operands)
    moved += sum(math.prod(shape) * jnp.dtype(dtype).itemsize for shape, dtype in out)
    result = pl.pallas_call(
        kernel,
        out_shape=shapes,
        in_specs=[whole()] * len(operands),
        out_specs=[whole()] * len(out),
        scratch_shapes=scratch,
        compiler_params=pltpu.CompilerParams(vmem_limit_bytes=VMEM_BYTES),
        cost_estimate=pl.CostEstimate(flops=flops, bytes_accessed=moved, transcendentals=0),
        name=name,
    )(*operands)
    return result if len(out) > 1 else result[0]


def pseudo_by_sum(input_rows, input_factor, mode_freq, mode_damping, line_freq):
    lines = line_freq.shape[0]
    columns = input_factor.shape[1] // lines
    half = columns // 2
    forced = lax.psum(
        lax.dot_general(
            input_rows, input_factor, (((0,), (0,)), ((), ())), preferred_element_type=F32
        ),
        AXES,
    )
    pieces = []
    for line in range(lines):
        gain_real, gain_imag = modal_gain(mode_freq, mode_damping, line_freq[line])
        gain_real, gain_imag = gain_real[:, None], gain_imag[:, None]
        real = forced[:, line * columns : line * columns + half]
        imag = forced[:, line * columns + half : (line + 1) * columns]
        pieces.append(gain_real * real - gain_imag * imag)
        pieces.append(gain_real * imag + gain_imag * real)
    return jnp.concatenate(pieces, axis=1).astype(BF16)


def own_pseudo(input_rows, input_factor, mode_freq, mode_damping, line_freq, copies):
    devices = math.prod(FAST_SHAPE)
    rows, modes = input_rows.shape
    width = input_factor.shape[1]
    lines = line_freq.shape[0]
    parts = modes // (devices // 2 * width)
    ones = call(ones_kernel, "ones", [((8, width), F32)], flops=LONG)
    sent = call(
        pack_kernel,
        "pack",
        [((devices, (parts + 1) * rows, width), BF16)],
        ones,
        input_rows,
        input_factor,
        flops=LONG,
    )
    got = lax.all_to_all(sent, AXES, 0, 0)
    return call(
        functools.partial(pseudo_kernel, rows=rows),
        "pseudo",
        [((copies, parts * width, width), BF16)],
        line_freq.reshape(1, lines),
        mode_freq.reshape(-1, width),
        mode_damping.reshape(-1, width),
        got,
        flops=LONG,
    )


def local(
    shape,
    mode_rows,
    input_rows,
    input_factor,
    mode_freq,
    mode_damping,
    line_freq,
    boundary_rows,
    connectivity,
    stress_coef,
):
    devices = math.prod(shape)
    rows, modes = mode_rows.shape
    width = input_factor.shape[1]
    lines = line_freq.shape[0]
    exports = boundary_rows.shape[0]
    rim = exports // 2
    elems = connectivity.shape[1]
    inputs = (input_rows, input_factor, mode_freq, mode_damping, line_freq)
    if shape == FAST_SHAPE and modes == devices * LANES and input_rows.shape[0] % 16 == 0:
        cycle = [place ^ (place // 2) for place in range(8)]
        groups = [[h * 16 + j * 2 + c for j in cycle] for h in range(2) for c in range(2)]
        got = lax.all_to_all(own_pseudo(*inputs, copies=8), AXES, 0, 0, axis_index_groups=groups)
        mine = got.reshape(modes // 2, width)
        theirs = lax.ppermute(mine, AXES, [(i, i ^ 1) for i in range(devices)])
    else:
        pseudo = pseudo_by_sum(*inputs).reshape(2, modes // 2, width)
        core = lax.axis_index(AXES) % 2
        mine = lax.dynamic_index_in_dim(pseudo, core, 0, keepdims=False)
        theirs = lax.dynamic_index_in_dim(pseudo, 1 - core, 0, keepdims=False)
    total, part, picked = call(
        first_kernel,
        "first",
        [((rows, width), F32), ((exports, width), F32), ((exports, modes // 2), BF16)],
        boundary_rows.reshape(1, exports),
        mode_rows,
        mine,
        flops=rows * modes * (width + exports),
        scratch=[pltpu.VMEM((exports, rows), BF16)],
    )
    far, near = call(
        export_kernel,
        "export",
        [((rim, width), BF16)] * 2,
        part,
        picked,
        theirs,
        flops=exports * modes * width,
    )
    inner = [(i, i ^ 1) for i in range(devices)]
    outer = [(i, i + 1) for i in range(1, devices - 1, 2)]
    outer += [(j, i) for i, j in outer]
    near = lax.ppermute(near, AXES, inner)
    far = lax.ppermute(far, AXES, outer)
    stress, matrix = call(
        own_kernel,
        "own",
        [((width, elems), F32), ((2 * exports, elems), BF16)],
        connectivity,
        stress_coef,
        mode_rows,
        theirs,
        total,
        flops=rows * modes * width + 4 * rows * elems * width,
        scratch=[pltpu.VMEM((2, rows, elems), BF16), pltpu.VMEM((width, rows), BF16)],
    )
    return call(
        power_kernel,
        "power",
        [((lines, elems), F32)],
        stress,
        far,
        near,
        matrix,
        flops=4 * exports * elems * width,
    )


def solution(mesh):
    shape = tuple(mesh.shape[axis] for axis in AXES)
    placed = (
        P(AXES, None),
        P(AXES, None),
        P(AXES, None),
        P(),
        P(),
        P(),
        P(AXES),
        P(None, AXES),
        P(None, AXES),
    )
    return jax.shard_map(
        functools.partial(local, shape),
        mesh=mesh,
        in_specs=placed,
        out_specs=P(None, AXES),
        check_vma=False,
    )
```
